32 devices in a mesh: fast: 16 (over z, y, core), slow: 2 (over x).
Axes of the slice: x: 2, y: 2, z: 4, core: 2. Of those that a mesh axis runs over, the one named last changes fastest.
Arguments:
- object_field: float32 [2, 4096, 512], P(None, 'fast', 'slow'), may hold values from -5 to 5
- probe_modes: float32 [2, 2, 128, 128], replicated, may hold values from -3 to 3
- descan: float32 [2, 3], replicated, may hold values from -0.5 to 0.5
- scan_positions: int32 [2, 32, 2], P(None, 'fast', 'slow'), may hold values from 0 to 3968, as said below
- amplitudes: float32 [32, 256, 128], P('fast', 'slow'), may hold values from 0.2 to 4
Outputs:
- object_out: float32 [2, 4096, 512], P(None, 'fast', 'slow')
- probe_out: float32 [2, 2, 128, 128], replicated
- descan_out: float32 [2, 3], replicated
The draws below stay inside these ranges and needn't reach their ends.
Inputs may be any that keep to these rules, and one draw needn't show every extreme that they name: `scan_positions`: window starts of tile (i, j) lie from i * 256 - 64 to i * 256 + 192 along the fast-scan direction and from j * 256 - 64 to j * 256 + 192 along the slow one, and every window lies inside the object.
All inputs are finite; a program needn't handle non-finite values.
Results may differ from the reference program's by a relative error of at most 0.0003.
Values sent between devices are 32-bit elements; how exact they have to be, the bound alone decides.
No kernel may reach another device: no remote copies, remote signals or barrier semaphores. Data moves between devices by JAX's collectives and lax.ppermute only.
A program may use at most 64 MiB of HBM per device.

```python
import math
import jax
import jax.numpy as jnp
from jax import lax

W = 128
M = 2
ITERS = 2
TF = 256
TS = 256
P_DEV = 2
H = 64
NF = 4096
NS = 512
NPOS = 64
N_FAST = 16
N_SLOW = 2


def draw_scan_positions(key, part):
    fast_tile = jnp.arange(P_DEV * N_FAST, dtype=jnp.int32) // P_DEV
    slow_tile = jnp.arange(N_SLOW, dtype=jnp.int32)
    shape_all = (P_DEV * N_FAST, N_SLOW)
    low_rows = jnp.broadcast_to(jnp.maximum(fast_tile * TF - H, 0)[:, None], shape_all)
    high_rows = jnp.broadcast_to(jnp.minimum(fast_tile * TF + TF + H - W, TF * N_FAST - W)[:, None], shape_all)
    low_cols = jnp.broadcast_to(jnp.maximum(slow_tile * TS - H, 0)[None, :], shape_all)
    high_cols = jnp.broadcast_to(jnp.minimum(slow_tile * TS + TS + H - W, TS * N_SLOW - W)[None, :], shape_all)
    margin = W // 4
    key_rows, key_cols = jax.random.split(jax.random.fold_in(key, 7))
    raw_rows = jax.random.randint(key_rows, shape_all, low_rows - margin, high_rows + margin + 1)
    raw_cols = jax.random.randint(key_cols, shape_all, low_cols - margin, high_cols + margin + 1)
    rows = jnp.clip(raw_rows, low_rows, high_rows)
    cols = jnp.clip(raw_cols, low_cols, high_cols)
    return jnp.stack([rows, cols]).astype(jnp.int32)


def steps_of(key, shape, shards, least, largest):
    level, own = 1.0, jax.random.fold_in(key, 6)
    for position, shards_of in shards:
        steps = jnp.exp(jax.random.uniform(jax.random.fold_in(own, position), (shards_of,), jnp.float32, least / len(shards), largest / len(shards)))
        level = level * jnp.repeat(steps, shape[position] // shards_of).reshape([-1 if axis == position else 1 for axis in range(len(shape))])
    return level


def gaussian(rng, shape, width, most, cuts=(), held_as=jnp.bfloat16):
    entries = width * jax.random.normal(rng, shape, jnp.float32)
    if cuts:
        entries = entries * steps_of(rng, shape, cuts, -0.22, 0.18)
    return jnp.clip(entries, -most, most).astype(held_as)


def setup_inputs(seed: int = 0) -> dict:
    key_of = jax.random.split(jax.random.key(seed), 6)
    return {
        "object_field": gaussian(key_of[0], (2, NF, NS), 0.7, 5.0, ((1, 16), (2, 2)), jnp.float32),
        "probe_modes": gaussian(key_of[1], (2, M, W, W), 0.5, 3.0, (), jnp.float32),
        "descan": jnp.clip(jax.random.uniform(key_of[2], (2, 3), jnp.float32, -0.5, 0.5), -0.5, 0.5),
        "scan_positions": draw_scan_positions(jax.random.fold_in(key_of[5], 71), 0),
        "amplitudes": jnp.clip(jnp.exp(math.log(4.0) - 2.9957323 * jax.random.uniform(key_of[4], (P_DEV * N_FAST, W * N_SLOW, W), jnp.float32) ** steps_of(key_of[4], (P_DEV * N_FAST, W * N_SLOW, W), ((0, 16), (1, 2)), -0.2, 0.2)), 0.2, 4.0),
    }


OBJECT_STEP = 0.1
PROBE_STEP = 8.0
DESCAN_STEP = 0.02
FLOOR_LEVEL = 0.25
PROBE_POWER = 0.5

def window_terms(objects, probes, descan_now, start_row, start_col, measured, centred):
    real_type = descan_now.dtype
    frac_row = start_row.astype(real_type) / NF
    frac_col = start_col.astype(real_type) / NS
    patches = lax.dynamic_slice(objects, (start_row, start_col), (W, W))
    shift_row = descan_now[0, 0] + descan_now[0, 1] * frac_row + descan_now[0, 2] * frac_col
    shift_col = descan_now[1, 0] + descan_now[1, 1] * frac_row + descan_now[1, 2] * frac_col
    phases = 2 * jnp.pi * (shift_row * centred[:, None] + shift_col * centred[None, :])
    ramps = lax.complex(jnp.cos(phases), jnp.sin(phases))
    illum = probes * ramps[None]
    exit_wave = illum * patches[None]
    far_field = jnp.fft.fft2(exit_wave, norm='ortho')
    intensity = lax.optimization_barrier(jnp.sum(jnp.real(far_field) ** 2 + jnp.imag(far_field) ** 2, axis=0))
    model_amp = jnp.sqrt(jnp.maximum(intensity, FLOOR_LEVEL))
    weighted = far_field * (1.0 - measured / model_amp)[None]
    backward = jnp.fft.ifft2(weighted, norm='ortho')
    object_grad = lax.optimization_barrier(jnp.sum(jnp.conj(illum) * backward, axis=0))
    probe_grad = jnp.conj(patches * ramps)[None] * backward
    twists = jnp.imag(jnp.conj(backward) * exit_wave)
    grad_row = -4 * jnp.pi * jnp.sum(twists * centred[None, :, None])
    grad_col = -4 * jnp.pi * jnp.sum(twists * centred[None, None, :])
    basis = jnp.stack([jnp.ones((), real_type), frac_row, frac_col])
    descan_grad = jnp.stack([grad_row * basis, grad_col * basis])
    return (object_grad, probe_grad, descan_grad)

def reference(object_field, probe_modes, descan, scan_positions, amplitudes):
    real_type = object_field.dtype
    objects = lax.complex(object_field[0], object_field[1])
    probes = lax.complex(probe_modes[0], probe_modes[1])
    descan_now = descan
    start_rows = scan_positions[0].reshape(-1).astype(jnp.int32)
    start_cols = scan_positions[1].reshape(-1).astype(jnp.int32)
    measured_all = amplitudes.reshape(P_DEV * N_FAST, N_SLOW, W, W).reshape(NPOS, W, W)
    centred = (jnp.arange(W).astype(real_type) - W // 2) / W
    for iteration in range(ITERS):

        def visit(carry, item):
            grad_objects, grad_probes, grad_descan = carry
            start_row, start_col, measured = item
            object_grad, probe_grad, descan_grad = window_terms(objects, probes, descan_now, start_row, start_col, measured, centred)
            current = lax.dynamic_slice(grad_objects, (start_row, start_col), (W, W))
            grad_objects = lax.dynamic_update_slice(grad_objects, current + object_grad, (start_row, start_col))
            return ((grad_objects, grad_probes + probe_grad, grad_descan + descan_grad), None)
        initial = (jnp.zeros_like(objects), jnp.zeros_like(probes), jnp.zeros((2, 3), real_type))
        (grad_objects, grad_probes, grad_descan), unused = lax.scan(visit, initial, (start_rows, start_cols, measured_all))
        objects = objects - OBJECT_STEP * grad_objects
        updated = probes - PROBE_STEP / NPOS * grad_probes
        total_power = jnp.sum(jnp.real(updated) ** 2 + jnp.imag(updated) ** 2)
        probes = updated * jnp.sqrt(PROBE_POWER * M * W * W / total_power)
        descan_now = descan_now - DESCAN_STEP / NPOS * grad_descan
    object_out = jnp.stack([jnp.real(objects), jnp.imag(objects)])
    probe_out = jnp.stack([jnp.real(probes), jnp.imag(probes)])
    return (object_out, probe_out, descan_now)
```

```python
import functools
import math

import jax
import jax.numpy as jnp
import numpy as np
from jax import lax
from jax.experimental import pallas as pl
from jax.experimental.pallas import tpu as pltpu
from jax.sharding import PartitionSpec as P

OBJECT_STEP = 0.1
PROBE_STEP = 8.0
DESCAN_STEP = 0.02
FLOOR_LEVEL = 0.25
PROBE_POWER = 0.5
LANES = 128
EXTRA = 8
AXES = ("fast", "slow")
F32 = jnp.float32
BF16 = jnp.bfloat16
VMEM = pl.BlockSpec(memory_space=pltpu.VMEM)
SMEM = pl.BlockSpec(memory_space=pltpu.SMEM)
LIMIT = 40 * 1024 * 1024


def transform_tables(width):
    counter = np.arange(width)
    angles = 2.0 * np.pi / width * (counter[:, None] * counter[None, :] % width)
    real = np.cos(angles) / math.sqrt(width)
    imag = -np.sin(angles) / math.sqrt(width)
    forward = np.block([[real, imag], [-imag, real]]).astype(np.float32)
    backward = np.block([[real, -imag], [imag, real]]).astype(np.float32)
    parts = []
    for table in (forward, backward):
        high = table.astype(BF16)
        parts += [high, (table - high.astype(np.float32)).astype(BF16)]
    return jnp.asarray(np.stack(parts))


def split(value):
    high = value.astype(BF16)
    return high, (value - high.astype(F32)).astype(BF16)


def dot(a, b):
    return jnp.dot(a, b, preferred_element_type=F32)


def product(left, right):
    (left_high, left_low), (right_high, right_low) = left, right
    return dot(left_high, right_high) + dot(left_high, right_low) + dot(left_low, right_high)


def lane_of(shape):
    return lax.broadcasted_iota(jnp.int32, shape, len(shape) - 1)


def window_place(starts, j, tile_rows, tile_cols, width, fast, slow):
    rim = width // 2
    row = starts[0, j, 0] - fast * tile_rows + rim
    col = starts[1, j, 0] - slow * tile_cols
    lane = jnp.where(col < 0, col + tile_cols + width, col)
    block = jnp.minimum(row // 8, (tile_rows + width - width - 8) // 8)
    return block * 8, row - block * 8, lane


def gradients(
    object_ref, probe, descan_rows, starts, measured_ref, tables_ref, gradient_ref, wave_ref, far_ref, sizes
):
    tile_rows, tile_cols, width, modes, count, n_fast, n_slow, fast, slow = sizes
    ext_cols = tile_cols + width
    high = width + 8
    probe_real, probe_imag = probe
    lane_row = lane_of((1, width)).astype(F32)
    centred = (lane_row - width // 2) / width
    tables = [tables_ref[k] for k in range(4)]
    forward, backward = (tables[0], tables[1]), (tables[2], tables[3])

    fractions = []
    phases = []
    for j in range(count):
        frac_row = jnp.full((1, width), starts[0, j, 0], jnp.int32).astype(F32) / (tile_rows * n_fast)
        frac_col = jnp.full((1, width), starts[1, j, 0], jnp.int32).astype(F32) / (tile_cols * n_slow)
        fractions.append((frac_row, frac_col))
        for k in range(2):
            d = descan_rows[3 * k : 3 * k + 3]
            phases.append((2 * math.pi) * ((d[0] + d[1] * frac_row + d[2] * frac_col) * centred))
    while len(phases) % 8:
        phases.append(jnp.zeros((1, width), F32))
    phases = jnp.concatenate(phases, axis=0)
    cosines, sines = jnp.cos(phases), jnp.sin(phases)

    def along_rows(row):
        return jnp.transpose(jnp.broadcast_to(row, (width, width)))

    lits = []
    ramps = []
    for j in range(count):
        row_start, row_shift, lane = window_place(starts, j, tile_rows, tile_cols, width, fast, slow)
        row_start = pl.multiple_of(row_start, 8)
        row_cos, row_sin = along_rows(cosines[2 * j : 2 * j + 1]), along_rows(sines[2 * j : 2 * j + 1])
        col_cos, col_sin = cosines[2 * j + 1 : 2 * j + 2], sines[2 * j + 1 : 2 * j + 2]
        ramp_real = row_cos * col_cos - row_sin * col_sin
        ramp_imag = row_cos * col_sin + row_sin * col_cos
        patch = []
        for part in range(2):
            rows = object_ref[part, pl.ds(row_start, high), :]
            rows = pltpu.roll(rows, lax.rem(ext_cols - lane, ext_cols), 1)[:, :width]
            patch.append(pltpu.roll(rows, lax.rem(high - row_shift, high), 0)[:width])
        lit_real = patch[0] * ramp_real - patch[1] * ramp_imag
        lit_imag = patch[0] * ramp_imag + patch[1] * ramp_real
        lits.append((lit_real, lit_imag))
        ramps.append((ramp_real, ramp_imag))
        for m in range(modes):
            p_real = probe_real[m * width : (m + 1) * width]
            p_imag = probe_imag[m * width : (m + 1) * width]
            at = (j * modes + m) * width
            wave_ref[at : at + width, :width] = p_real * lit_real - p_imag * lit_imag
            wave_ref[at : at + width, width:] = p_real * lit_imag + p_imag * lit_real

    half = product(split(wave_ref[...]), forward)
    for w in range(count * modes):
        at = w * width
        far_ref[:width, at : at + width] = half[at : at + width, :width]
        far_ref[width:, at : at + width] = half[at : at + width, width:]
    far = product(backward, split(far_ref[...]))
    far_ref[...] = far
    for j in range(count):
        intensity = None
        for m in range(modes):
            at = (j * modes + m) * width
            real, imag = far_ref[:width, at : at + width], far_ref[width:, at : at + width]
            power = real * real + imag * imag
            intensity = power if intensity is None else intensity + power
        factor = 1.0 - measured_ref[j] / jnp.sqrt(jnp.maximum(intensity, FLOOR_LEVEL))
        for m in range(modes):
            at = (j * modes + m) * width
            far_ref[:width, at : at + width] *= factor
            far_ref[width:, at : at + width] *= factor
    half = product(forward, split(far_ref[...]))
    for w in range(count * modes):
        at = w * width
        wave_ref[at : at + width, :width] = half[:width, at : at + width]
        wave_ref[at : at + width, width:] = half[width:, at : at + width]
    wave_ref[...] = product(split(wave_ref[...]), backward)

    gradient_ref[...] = jnp.zeros(gradient_ref.shape, F32)
    probe_grad = [[None] * modes, [None] * modes]
    descan_grad = [None] * 6
    centred_rows = along_rows(centred)
    for j in range(count):
        lit_real, lit_imag = lits[j]
        ramp_real, ramp_imag = ramps[j]
        sum_real = sum_imag = None
        for m in range(modes):
            p_real = probe_real[m * width : (m + 1) * width]
            p_imag = probe_imag[m * width : (m + 1) * width]
            at = (j * modes + m) * width
            real, imag = wave_ref[at : at + width, :width], wave_ref[at : at + width, width:]
            q_real = lit_real * real + lit_imag * imag
            q_imag = lit_real * imag - lit_imag * real
            probe_grad[0][m] = q_real if j == 0 else probe_grad[0][m] + q_real
            probe_grad[1][m] = q_imag if j == 0 else probe_grad[1][m] + q_imag
            h_real = p_real * real + p_imag * imag
            h_imag = p_real * imag - p_imag * real
            sum_real = h_real if m == 0 else sum_real + h_real
            sum_imag = h_imag if m == 0 else sum_imag + h_imag
        twist = lit_imag * sum_real - lit_real * sum_imag
        totals = (
            jnp.sum(jnp.sum(twist * centred_rows, axis=0, keepdims=True), axis=1, keepdims=True),
            jnp.sum(jnp.sum(twist, axis=0, keepdims=True) * centred, axis=1, keepdims=True),
        )
        frac_row, frac_col = fractions[j]
        for k in range(2):
            base = jnp.broadcast_to(-4 * math.pi * totals[k], (1, width))
            for n, term in enumerate((base, base * frac_row, base * frac_col)):
                descan_grad[3 * k + n] = term if j == 0 else descan_grad[3 * k + n] + term
        row_start, row_shift, lane = window_place(starts, j, tile_rows, tile_cols, width, fast, slow)
        row_start = pl.multiple_of(row_start, 8)
        parts = (
            ramp_real * sum_real + ramp_imag * sum_imag,
            ramp_real * sum_imag - ramp_imag * sum_real,
        )
        for part in range(2):
            value = jnp.concatenate([parts[part], jnp.zeros((8, width), F32)], axis=0)
            value = pltpu.roll(value, row_shift, 0)
            value = jnp.concatenate([value, jnp.zeros((high, ext_cols - width), F32)], axis=1)
            gradient_ref[part, pl.ds(row_start, high), :] += pltpu.roll(value, lane, 1)
    return probe_grad, descan_grad


def put_sums(probe_grad, descan_grad, keep_ref, send_ref, core, width, modes):
    for m in range(modes):
        real, imag = probe_grad[0][m], probe_grad[1][m]
        keep_ref[m * width : (m + 1) * width] = jnp.where(core == 0, real, imag)
        send_ref[m * width : (m + 1) * width] = jnp.where(core == 0, imag, real)
    block = jnp.concatenate(descan_grad + [jnp.zeros((EXTRA - 6, width), F32)], axis=0)
    keep_ref[modes * width :] = block
    send_ref[modes * width :] = block


def updated_probe(probe_ref, mine_ref, other_ref, core, total, width, modes):
    rows = modes * width
    mine, other = mine_ref[:rows], other_ref[...]
    real = probe_ref[0].reshape(rows, width) - PROBE_STEP / total * jnp.where(core == 0, mine, other)
    imag = probe_ref[1].reshape(rows, width) - PROBE_STEP / total * jnp.where(core == 0, other, mine)
    power = jnp.sum(jnp.sum(real * real + imag * imag, axis=0, keepdims=True), axis=1, keepdims=True)
    scale = jnp.sqrt(PROBE_POWER * rows * width / power)
    return real * scale, imag * scale


def halo_blocks(right, left, width):
    rim = width // 2
    low = lane_of(right.shape) < rim
    return jnp.where(low, right, pltpu.roll(left, rim, 1)), jnp.where(low, pltpu.roll(right, rim, 1), left)


def first_kernel(
    sizes, where_ref, starts, descan_ref, object_ref, probe_ref, measured_ref, tables_ref,
    top_ref, bottom_ref, right_refs, left_refs,
    extended_ref, gradient_ref, strip_right_ref, strip_left_ref, keep_ref, send_ref, wave_ref, far_ref,
):
    tile_rows, tile_cols, width, modes, count, n_fast, n_slow = sizes
    fast, slow = where_ref[0], where_ref[1]
    rim = width // 2
    for part in range(2):
        extended_ref[part, rim : rim + tile_rows, :tile_cols] = object_ref[part]
        extended_ref[part, :rim, :tile_cols] = top_ref[part]
        extended_ref[part, rim + tile_rows :, :tile_cols] = bottom_ref[part]
    at = 0
    for right, left in zip(right_refs, left_refs):
        real, imag = halo_blocks(right[...], left[...], width)
        extended_ref[0, at : at + right.shape[0], tile_cols:] = real
        extended_ref[1, at : at + right.shape[0], tile_cols:] = imag
        at += right.shape[0]
    descan_rows = [jnp.full((1, width), descan_ref[k, n], F32) for k in range(2) for n in range(3)]
    probe = tuple(probe_ref[part].reshape(modes * width, width) for part in range(2))
    probe_grad, descan_grad = gradients(
        extended_ref, probe, descan_rows, starts, measured_ref, tables_ref, gradient_ref, wave_ref, far_ref,
        sizes + (fast, slow),
    )
    put_sums(probe_grad, descan_grad, keep_ref, send_ref, lax.rem(fast, 2), width, modes)
    halo = gradient_ref[:, :, tile_cols:]
    low = lane_of(halo.shape) < rim
    strip_right_ref[...] = jnp.where(low, halo, gradient_ref[:, :, tile_cols - width : tile_cols])
    strip_left_ref[...] = jnp.where(low, gradient_ref[:, :, :width], halo)


def add_columns(gradient, right, left, tile_cols, width):
    rim = width // 2
    low = lane_of(right.shape) < rim
    zero = jnp.zeros(right.shape, F32)
    blocks = [gradient[:, :, k : k + width] for k in range(0, tile_cols + width, width)]
    blocks[0] = blocks[0] + jnp.where(low, left, zero)
    blocks[-2] = blocks[-2] + jnp.where(low, zero, right)
    blocks[-1] = blocks[-1] + jnp.where(low, right, left)
    return jnp.concatenate(blocks, axis=2)


def masked(where_ref, right, left, n_slow):
    slow = where_ref[1]
    return (
        jnp.where(slow < n_slow - 1, right, jnp.zeros_like(right)),
        jnp.where(slow > 0, left, jnp.zeros_like(left)),
    )


def rows_kernel(sizes, where_ref, gradient_ref, right_ref, left_ref, up_ref, down_ref):
    tile_rows, tile_cols, width, modes, count, n_fast, n_slow = sizes
    for out_ref, at in ((up_ref, 0), (down_ref, tile_rows)):
        right, left = masked(where_ref, right_ref[:, at : at + width], left_ref[:, at : at + width], n_slow)
        out_ref[...] = add_columns(gradient_ref[:, at : at + width], right, left, tile_cols, width)


def second_kernel(
    sizes, total, where_ref, starts, descan_ref, extended_ref, gradient_in_ref, probe_ref, measured_ref, tables_ref,
    right_ref, left_ref, above_ref, below_ref, mine_ref, other_ref,
    base_ref, up_ref, down_ref, strip_right_ref, strip_left_ref, keep_ref, send_ref, probe_out_ref, descan_out_ref,
    object_ref, gradient_ref, wave_ref, far_ref,
):
    tile_rows, tile_cols, width, modes, count, n_fast, n_slow = sizes
    fast, slow = where_ref[0], where_ref[1]
    core = lax.rem(fast, 2)
    rim = width // 2
    right, left = masked(where_ref, right_ref[...], left_ref[...], n_slow)
    object_ref[...] = extended_ref[...] - OBJECT_STEP * add_columns(
        gradient_in_ref[...], right, left, tile_cols, width
    )
    object_ref[:, :width] -= OBJECT_STEP * above_ref[...]
    object_ref[:, tile_rows:] -= OBJECT_STEP * below_ref[...]
    probe = updated_probe(probe_ref, mine_ref, other_ref, core, total, width, modes)
    probe_out_ref[0] = probe[0].reshape(modes, width, width)
    probe_out_ref[1] = probe[1].reshape(modes, width, width)
    at = modes * width
    descan_rows = [
        descan_ref[k // 3, k % 3] - DESCAN_STEP / total * mine_ref[at + k : at + k + 1] for k in range(6)
    ]
    descan_out_ref[...] = jnp.concatenate(descan_rows + [jnp.zeros((EXTRA - 6, width), F32)], axis=0)
    probe_grad, descan_grad = gradients(
        object_ref, probe, descan_rows, starts, measured_ref, tables_ref, gradient_ref, wave_ref, far_ref,
        sizes + (fast, slow),
    )
    put_sums(probe_grad, descan_grad, keep_ref, send_ref, core, width, modes)
    base_ref[...] = (
        object_ref[:, rim : rim + tile_rows, :tile_cols]
        - OBJECT_STEP * gradient_ref[:, rim : rim + tile_rows, :tile_cols]
    )
    up_ref[...] = gradient_ref[:, :rim, :tile_cols]
    down_ref[...] = gradient_ref[:, rim + tile_rows :, :tile_cols]
    real, imag = gradient_ref[0, :, tile_cols:], gradient_ref[1, :, tile_cols:]
    low = lane_of(real.shape) < rim
    strip_right_ref[...] = jnp.where(low, real, pltpu.roll(imag, rim, 1))
    strip_left_ref[...] = jnp.where(low, pltpu.roll(real, rim, 1), imag)


def edge_blocks(where_ref, right, left, n_slow, width):
    rim = width // 2
    right, left = masked(where_ref, right, left, n_slow)
    low = lane_of(right.shape) < rim
    zero = jnp.zeros(right.shape, F32)
    first = (jnp.where(low, left, zero), jnp.where(low, pltpu.roll(left, rim, 1), zero))
    last = (jnp.where(low, zero, pltpu.roll(right, rim, 1)), jnp.where(low, zero, right))
    return first, last


def last_rows_kernel(sizes, where_ref, up_in_ref, down_in_ref, right_ref, left_ref, up_ref, down_ref):
    tile_rows, tile_cols, width, modes, count, n_fast, n_slow = sizes
    rim = width // 2
    for in_ref, out_ref, at in ((up_in_ref, up_ref, 0), (down_in_ref, down_ref, rim + tile_rows)):
        out_ref[...] = in_ref[...]
        first, last = edge_blocks(where_ref, right_ref[at : at + rim], left_ref[at : at + rim], n_slow, width)
        for part in range(2):
            out_ref[part, :, :width] += first[part]
            out_ref[part, :, tile_cols - width :] += last[part]


def object_kernel(sizes, where_ref, base_ref, right_ref, left_ref, above_ref, below_ref, out_ref):
    tile_rows, tile_cols, width, modes, count, n_fast, n_slow = sizes
    rim = width // 2
    out_ref[...] = base_ref[...]
    first, last = edge_blocks(
        where_ref, right_ref[rim : rim + tile_rows], left_ref[rim : rim + tile_rows], n_slow, width
    )
    for part in range(2):
        out_ref[part, :, :width] -= OBJECT_STEP * first[part]
        out_ref[part, :, tile_cols - width :] -= OBJECT_STEP * last[part]
    out_ref[:, :rim] -= OBJECT_STEP * above_ref[...]
    out_ref[:, tile_rows - rim :] -= OBJECT_STEP * below_ref[...]


def probe_kernel(sizes, total, where_ref, probe_ref, descan_ref, mine_ref, other_ref, probe_out_ref, descan_out_ref):
    tile_rows, tile_cols, width, modes, count, n_fast, n_slow = sizes
    core = lax.rem(where_ref[0], 2)
    real, imag = updated_probe(probe_ref, mine_ref, other_ref, core, total, width, modes)
    probe_out_ref[0] = real.reshape(modes, width, width)
    probe_out_ref[1] = imag.reshape(modes, width, width)
    at = modes * width
    rows = descan_ref[...] - DESCAN_STEP / total * mine_ref[at : at + EXTRA]
    lane = lane_of((1, width))
    for k in range(2):
        values = [rows[3 * k + n : 3 * k + n + 1] for n in range(3)]
        row = jnp.where(lane == 0, values[0], jnp.where(lane == 1, values[1], values[2]))
        descan_out_ref[k : k + 1, :] = row[:, :3]


def call(kernel, outs, scratch, *operands, smem=0):
    return pl.pallas_call(
        kernel,
        out_shape=[jax.ShapeDtypeStruct(shape, F32) for shape in outs],
        in_specs=[SMEM] * smem + [VMEM] * (len(operands) - smem),
        out_specs=[VMEM] * len(outs),
        scratch_shapes=[pltpu.VMEM(shape, F32) for shape in scratch],
        compiler_params=pltpu.CompilerParams(vmem_limit_bytes=LIMIT),
    )(*operands)


def on_device(object_field, probe_modes, descan, scan_positions, amplitudes):
    width = amplitudes.shape[-1]
    rim = width // 2
    modes = probe_modes.shape[1]
    count = scan_positions.shape[1]
    tile_rows, tile_cols = object_field.shape[1:]
    n_fast, n_slow = lax.axis_size("fast"), lax.axis_size("slow")
    total = count * n_fast * n_slow
    sizes = (tile_rows, tile_cols, width, modes, count, n_fast, n_slow)
    fast, slow = lax.axis_index("fast"), lax.axis_index("slow")
    where = jnp.stack([fast, slow]).astype(jnp.int32)
    tables = transform_tables(width)
    ext_rows, ext_cols = tile_rows + width, tile_cols + width
    half_rows = modes * width

    def moved(value, step_fast, step_slow):
        pairs = []
        for f in range(n_fast):
            for s in range(n_slow):
                to_fast, to_slow = f + step_fast, s + step_slow
                if 0 <= to_fast < n_fast and 0 <= to_slow < n_slow:
                    pairs.append((f * n_slow + s, to_fast * n_slow + to_slow))
        return lax.ppermute(value, AXES, pairs)

    def across(to_right, to_left, step_fast):
        if n_slow == 2:
            pairs = [
                (f * 2 + s, (f + step_fast) * 2 + 1 - s)
                for f in range(n_fast)
                for s in range(2)
                if 0 <= f + step_fast < n_fast
            ]
            got = lax.ppermute(jnp.where(slow == 0, to_right, to_left), AXES, pairs)
            return got, got
        return moved(to_left, step_fast, -1), moved(to_right, step_fast, 1)

    def swapped(value, axis, bit):
        return lax.ppermute(value, axis, [(i, i ^ bit) for i in range(lax.axis_size(axis))])

    def summed(keep, send):
        if n_fast & (n_fast - 1) or n_slow & (n_slow - 1) or n_fast < 2:
            core = lax.rem(fast, 2)
            real = lax.psum(jnp.where(core == 0, keep, send), AXES)
            imag = lax.psum(jnp.where(core == 0, send, keep), AXES)
            return jnp.where(core == 0, real, imag), jnp.where(core == 0, imag, real)[:half_rows]
        mine = keep + swapped(send, "fast", 1)
        bit = 1
        while bit < n_slow:
            mine = mine + swapped(mine, "slow", bit)
            bit *= 2
        bit = 2
        while bit < n_fast:
            mine = mine + swapped(mine, "fast", bit)
            bit *= 2
        return mine, swapped(mine[:half_rows], "fast", 1)

    last = object_field[:, :, tile_cols - rim :]
    initial = object_field[:, :, :rim]
    to_right = jnp.concatenate([last[0], last[1]], axis=1)
    to_left = jnp.concatenate([initial[0], initial[1]], axis=1)
    top = moved(object_field[:, tile_rows - rim :], 1, 0)
    bottom = moved(object_field[:, :rim], -1, 0)
    right_mid, left_mid = across(to_right, to_left, 0)
    right_top, left_top = across(to_right[tile_rows - rim :], to_left[tile_rows - rim :], 1)
    right_bottom, left_bottom = across(to_right[:rim], to_left[:rim], -1)

    def first(where_ref, starts, descan_ref, object_ref, probe_ref, measured_ref, tables_ref, top_ref, bottom_ref,
              r0, r1, r2, l0, l1, l2, *rest):
        first_kernel(sizes, where_ref, starts, descan_ref, object_ref, probe_ref, measured_ref, tables_ref,
                     top_ref, bottom_ref, (r0, r1, r2), (l0, l1, l2), *rest)

    scratch = [(count * modes * width, 2 * width), (2 * width, count * modes * width)]
    sums = [(half_rows + EXTRA, width)] * 2
    extended, gradient, strip_right, strip_left, keep, send = call(
        first,
        [(2, ext_rows, ext_cols)] * 2 + [(2, ext_rows, width)] * 2 + sums,
        scratch,
        where, scan_positions, descan, object_field, probe_modes, amplitudes, tables, top, bottom,
        right_top, right_mid, right_bottom, left_top, left_mid, left_bottom,
        smem=3,
    )
    from_right, from_left = across(strip_right, strip_left, 0)
    up, down = call(
        functools.partial(rows_kernel, sizes), [(2, width, ext_cols)] * 2, [],
        where, gradient, from_right, from_left, smem=1,
    )
    above, below = moved(down, 1, 0), moved(up, -1, 0)
    mine, other = summed(keep, send)
    base, up, down, strip_right, strip_left, keep, send, probes, descan_rows = call(
        functools.partial(second_kernel, sizes, total),
        [(2, tile_rows, tile_cols)] + [(2, rim, tile_cols)] * 2 + [(ext_rows, width)] * 2 + sums
        + [probe_modes.shape, (EXTRA, width)],
        [(2, ext_rows, ext_cols)] * 2 + scratch,
        where, scan_positions, descan, extended, gradient, probe_modes, amplitudes, tables,
        from_right, from_left, above, below, mine, other,
        smem=3,
    )
    from_right, from_left = across(strip_right, strip_left, 0)
    up, down = call(
        functools.partial(last_rows_kernel, sizes), [(2, rim, tile_cols)] * 2, [],
        where, up, down, from_right, from_left, smem=1,
    )
    above, below = moved(down, 1, 0), moved(up, -1, 0)
    (objects,) = call(
        functools.partial(object_kernel, sizes), [(2, tile_rows, tile_cols)], [],
        where, base, from_right, from_left, above, below, smem=1,
    )
    mine, other = summed(keep, send)
    probes, descan_out = call(
        functools.partial(probe_kernel, sizes, total), [probe_modes.shape, descan.shape], [],
        where, probes, descan_rows, mine, other, smem=1,
    )
    return objects, probes, descan_out


def solution(mesh):
    placed = (P(None, "fast", "slow"), P(), P(), P(None, "fast", "slow"), P("fast", "slow", None))
    return jax.shard_map(
        on_device,
        mesh=mesh,
        in_specs=placed,
        out_specs=(P(None, "fast", "slow"), P(), P()),
        check_vma=False,
    )
```

```python
import functools
import math

import jax
import jax.numpy as jnp
import numpy as np
from jax import lax
from jax.experimental import pallas as pl
from jax.experimental.pallas import tpu as pltpu
from jax.sharding import PartitionSpec as P

OBJECT_STEP = 0.1
PROBE_STEP = 8.0
DESCAN_STEP = 0.02
FLOOR_LEVEL = 0.25
PROBE_POWER = 0.5
EXTRA = 8
AXES = ("fast", "slow")
F32 = jnp.float32
BF16 = jnp.bfloat16
VMEM = pl.BlockSpec(memory_space=pltpu.VMEM)
SMEM = pl.BlockSpec(memory_space=pltpu.SMEM)
HBM = pl.BlockSpec(memory_space=pltpu.HBM)
LIMIT = 40 * 1024 * 1024
WORK = 2_000_000_000


def transform_tables(width):
    counter = np.arange(width)
    angles = 2.0 * np.pi / width * (counter[:, None] * counter[None, :] % width)
    real = np.cos(angles) / math.sqrt(width)
    imag = -np.sin(angles) / math.sqrt(width)
    forward = np.block([[real, imag], [-imag, real]]).astype(np.float32)
    backward = np.block([[real, -imag], [imag, real]]).astype(np.float32)
    parts = []
    for table in (forward, backward):
        high = table.astype(BF16)
        parts += [high, (table - high.astype(np.float32)).astype(BF16)]
    return jnp.asarray(np.stack(parts))


def split(value):
    high = value.astype(BF16)
    return high, (value - high.astype(F32)).astype(BF16)


def dot(a, b):
    return jnp.dot(a, b, preferred_element_type=F32)


def product(left, right):
    (left_high, left_low), (right_high, right_low) = left, right
    return dot(left_high, right_high) + dot(left_high, right_low) + dot(left_low, right_high)


def lane_of(shape):
    return lax.broadcasted_iota(jnp.int32, shape, len(shape) - 1)


def window_place(starts, j, tile_rows, tile_cols, width, fast, slow):
    rim = width // 2
    row = starts[0, 0, j] - fast * tile_rows + rim
    col = starts[1, 0, j] - slow * tile_cols
    lane = jnp.where(col < 0, col + tile_cols + width, col)
    block = jnp.minimum(row // 8, (tile_rows + width - width - 8) // 8)
    return block * 8, row - block * 8, lane


def gradients(
    object_ref, probe, descan_rows, starts, measured_ref, tables_ref, gradient_ref, wave_ref, far_ref, sizes
):
    tile_rows, tile_cols, width, modes, count, n_fast, n_slow, fast, slow = sizes
    ext_cols = tile_cols + width
    high = width + 8
    probe_real, probe_imag = probe
    lane_row = lane_of((1, width)).astype(F32)
    centred = (lane_row - width // 2) / width
    tables = [tables_ref[k] for k in range(4)]
    forward, backward = (tables[0], tables[1]), (tables[2], tables[3])

    fractions = []
    phases = []
    for j in range(count):
        frac_row = jnp.full((1, width), starts[0, 0, j], jnp.int32).astype(F32) / (tile_rows * n_fast)
        frac_col = jnp.full((1, width), starts[1, 0, j], jnp.int32).astype(F32) / (tile_cols * n_slow)
        fractions.append((frac_row, frac_col))
        for k in range(2):
            d = descan_rows[3 * k : 3 * k + 3]
            phases.append((2 * math.pi) * ((d[0] + d[1] * frac_row + d[2] * frac_col) * centred))
    while len(phases) % 8:
        phases.append(jnp.zeros((1, width), F32))
    phases = jnp.concatenate(phases, axis=0)
    cosines, sines = jnp.cos(phases), jnp.sin(phases)

    def along_rows(row):
        return jnp.transpose(jnp.broadcast_to(row, (width, width)))

    lits = []
    ramps = []
    for j in range(count):
        row_start, row_shift, lane = window_place(starts, j, tile_rows, tile_cols, width, fast, slow)
        row_start = pl.multiple_of(row_start, 8)
        row_cos, row_sin = along_rows(cosines[2 * j : 2 * j + 1]), along_rows(sines[2 * j : 2 * j + 1])
        col_cos, col_sin = cosines[2 * j + 1 : 2 * j + 2], sines[2 * j + 1 : 2 * j + 2]
        ramp_real = row_cos * col_cos - row_sin * col_sin
        ramp_imag = row_cos * col_sin + row_sin * col_cos
        patch = []
        for part in range(2):
            rows = object_ref[part, pl.ds(row_start, high), :]
            rows = pltpu.roll(rows, lax.rem(ext_cols - lane, ext_cols), 1)[:, :width]
            patch.append(pltpu.roll(rows, lax.rem(high - row_shift, high), 0)[:width])
        lit_real = patch[0] * ramp_real - patch[1] * ramp_imag
        lit_imag = patch[0] * ramp_imag + patch[1] * ramp_real
        lits.append((lit_real, lit_imag))
        ramps.append((ramp_real, ramp_imag))
        for m in range(modes):
            p_real = probe_real[m * width : (m + 1) * width]
            p_imag = probe_imag[m * width : (m + 1) * width]
            at = (j * modes + m) * width
            wave_ref[at : at + width, :width] = p_real * lit_real - p_imag * lit_imag
            wave_ref[at : at + width, width:] = p_real * lit_imag + p_imag * lit_real

    half = product(split(wave_ref[...]), forward)
    for w in range(count * modes):
        at = w * width
        far_ref[:width, at : at + width] = half[at : at + width, :width]
        far_ref[width:, at : at + width] = half[at : at + width, width:]
    far = product(backward, split(far_ref[...]))
    far_ref[...] = far
    for j in range(count):
        intensity = None
        for m in range(modes):
            at = (j * modes + m) * width
            real, imag = far_ref[:width, at : at + width], far_ref[width:, at : at + width]
            power = real * real + imag * imag
            intensity = power if intensity is None else intensity + power
        factor = 1.0 - measured_ref[j] / jnp.sqrt(jnp.maximum(intensity, FLOOR_LEVEL))
        for m in range(modes):
            at = (j * modes + m) * width
            far_ref[:width, at : at + width] *= factor
            far_ref[width:, at : at + width] *= factor
    half = product(forward, split(far_ref[...]))
    for w in range(count * modes):
        at = w * width
        wave_ref[at : at + width, :width] = half[:width, at : at + width]
        wave_ref[at : at + width, width:] = half[width:, at : at + width]
    wave_ref[...] = product(split(wave_ref[...]), backward)

    gradient_ref[...] = jnp.zeros(gradient_ref.shape, F32)
    probe_grad = [[None] * modes, [None] * modes]
    descan_grad = [None] * 6
    centred_rows = along_rows(centred)
    for j in range(count):
        lit_real, lit_imag = lits[j]
        ramp_real, ramp_imag = ramps[j]
        sum_real = sum_imag = None
        for m in range(modes):
            p_real = probe_real[m * width : (m + 1) * width]
            p_imag = probe_imag[m * width : (m + 1) * width]
            at = (j * modes + m) * width
            real, imag = wave_ref[at : at + width, :width], wave_ref[at : at + width, width:]
            q_real = lit_real * real + lit_imag * imag
            q_imag = lit_real * imag - lit_imag * real
            probe_grad[0][m] = q_real if j == 0 else probe_grad[0][m] + q_real
            probe_grad[1][m] = q_imag if j == 0 else probe_grad[1][m] + q_imag
            h_real = p_real * real + p_imag * imag
            h_imag = p_real * imag - p_imag * real
            sum_real = h_real if m == 0 else sum_real + h_real
            sum_imag = h_imag if m == 0 else sum_imag + h_imag
        twist = lit_imag * sum_real - lit_real * sum_imag
        totals = (
            jnp.sum(jnp.sum(twist * centred_rows, axis=0, keepdims=True), axis=1, keepdims=True),
            jnp.sum(jnp.sum(twist, axis=0, keepdims=True) * centred, axis=1, keepdims=True),
        )
        frac_row, frac_col = fractions[j]
        for k in range(2):
            base = jnp.broadcast_to(-4 * math.pi * totals[k], (1, width))
            for n, term in enumerate((base, base * frac_row, base * frac_col)):
                descan_grad[3 * k + n] = term if j == 0 else descan_grad[3 * k + n] + term
        row_start, row_shift, lane = window_place(starts, j, tile_rows, tile_cols, width, fast, slow)
        row_start = pl.multiple_of(row_start, 8)
        parts = (
            ramp_real * sum_real + ramp_imag * sum_imag,
            ramp_real * sum_imag - ramp_imag * sum_real,
        )
        for part in range(2):
            value = jnp.concatenate([parts[part], jnp.zeros((8, width), F32)], axis=0)
            value = pltpu.roll(value, row_shift, 0)
            value = jnp.concatenate([value, jnp.zeros((high, ext_cols - width), F32)], axis=1)
            gradient_ref[part, pl.ds(row_start, high), :] += pltpu.roll(value, lane, 1)
    return probe_grad, descan_grad


def pick(parity, when_even, when_odd):
    return jnp.where(parity == 0, when_even, when_odd)


def both_sides(parity, even_ref, odd_ref, index=Ellipsis):
    even = even_ref[index]
    odd = jnp.zeros_like(even) if odd_ref is None else odd_ref[index]
    return pick(parity, even, odd), pick(parity, odd, even)


def put_sums(probe_grad, descan_grad, keep_ref, send_ref, core, width, modes):
    for m in range(modes):
        real, imag = probe_grad[0][m], probe_grad[1][m]
        keep_ref[m * width : (m + 1) * width] = jnp.where(core == 0, real, imag)
        send_ref[m * width : (m + 1) * width] = jnp.where(core == 0, imag, real)
    block = jnp.concatenate(descan_grad + [jnp.zeros((EXTRA - 6, width), F32)], axis=0)
    keep_ref[modes * width :] = block
    send_ref[modes * width :] = block


def updated_probe(probe_ref, mine_ref, other_ref, core, total, width, modes):
    rows = modes * width
    mine, other = mine_ref[:rows], other_ref[...]
    real = probe_ref[0].reshape(rows, width) - PROBE_STEP / total * jnp.where(core == 0, mine, other)
    imag = probe_ref[1].reshape(rows, width) - PROBE_STEP / total * jnp.where(core == 0, other, mine)
    power = jnp.sum(jnp.sum(real * real + imag * imag, axis=0, keepdims=True), axis=1, keepdims=True)
    scale = jnp.sqrt(PROBE_POWER * rows * width / power)
    return real * scale, imag * scale


def halo_blocks(right, left, width):
    rim = width // 2
    low = lane_of(right.shape) < rim
    return jnp.where(low, right, pltpu.roll(left, rim, 1)), jnp.where(low, pltpu.roll(right, rim, 1), left)


def pack_kernel(sizes, where_ref, object_ref, extended_ref, rows_even_ref, rows_odd_ref, *rest):
    tile_rows, tile_cols, width, modes, count, n_fast, n_slow = sizes
    rim = width // 2
    *rest, semaphore = rest
    inner = extended_ref.at[:, rim : rim + tile_rows, :tile_cols]
    copy = pltpu.make_async_copy(object_ref, inner, semaphore)
    copy.start()
    copy.wait()
    fast, slow = lax.rem(where_ref[0], 2), lax.rem(where_ref[1], 2)
    initial, final = extended_ref[:, rim:width, :tile_cols], extended_ref[:, tile_rows : rim + tile_rows, :tile_cols]
    rows_even_ref[...] = pick(fast, final, initial)
    rows_odd_ref[...] = pick(fast, initial, final)
    low = lane_of((tile_rows, width)) < rim
    end = extended_ref[:, rim : rim + tile_rows, tile_cols - width : tile_cols]
    start = extended_ref[:, rim : rim + tile_rows, :width]
    to_right = jnp.where(low, pltpu.roll(end[0], rim, 1), end[1])
    to_left = jnp.where(low, start[0], pltpu.roll(start[1], rim, 1))
    strips = (pick(slow, to_right, to_left), pick(slow, to_left, to_right))
    for k in range(len(rest) // 3):
        strip = strips[k]
        rest[3 * k][...] = strip
        rest[3 * k + 1][...] = pick(fast, strip[tile_rows - rim :], strip[:rim])
        rest[3 * k + 2][...] = pick(fast, strip[:rim], strip[tile_rows - rim :])


def first_kernel(
    sizes, info, starts, descan_ref, extended_in_ref, probe_ref, measured_ref, tables_ref,
    rows_even_ref, rows_odd_ref, halos,
    extended_ref, gradient_ref, strips, keep_ref, send_ref, wave_ref, far_ref,
):
    tile_rows, tile_cols, width, modes, count, n_fast, n_slow = sizes
    fast, slow = info[0], info[1]
    core = lax.rem(fast, 2)
    rim = width // 2
    below, above = both_sides(core, rows_even_ref, rows_odd_ref)
    extended_ref[:, :rim, :tile_cols] = above
    extended_ref[:, rim + tile_rows :, :tile_cols] = below
    columns = []
    for middle_ref, even_ref, odd_ref in halos:
        after, before = both_sides(core, even_ref, odd_ref)
        columns.append(((0, before), (rim, middle_ref[...]), (rim + tile_rows, after)))
    for piece in range(3):
        at, even = columns[0][piece]
        odd = columns[-1][piece][1]
        real, imag = halo_blocks(pick(lax.rem(slow, 2), even, odd), pick(lax.rem(slow, 2), odd, even), width)
        extended_ref[0, at : at + even.shape[0], tile_cols:] = real
        extended_ref[1, at : at + even.shape[0], tile_cols:] = imag
    descan_rows = [jnp.full((1, width), descan_ref[k // 3, k % 3], F32) for k in range(6)]
    probe = tuple(probe_ref[part].reshape(modes * width, width) for part in range(2))
    probe_grad, descan_grad = gradients(
        extended_ref, probe, descan_rows, starts, measured_ref, tables_ref, gradient_ref, wave_ref, far_ref,
        sizes + (fast, slow),
    )
    put_sums(probe_grad, descan_grad, keep_ref, send_ref, core, width, modes)
    halo = gradient_ref[:, :, tile_cols:]
    low = lane_of(halo.shape) < rim
    to_right = jnp.where(low, halo, gradient_ref[:, :, tile_cols - width : tile_cols])
    to_left = jnp.where(low, gradient_ref[:, :, :width], halo)
    put_strips(slow, to_right, to_left, strips)


def put_strips(place, to_next, to_previous, refs):
    parity = lax.rem(place, 2)
    refs[0][...] = pick(parity, to_next, to_previous)
    if len(refs) > 1:
        refs[1][...] = pick(parity, to_previous, to_next)


def add_columns(gradient, right, left, tile_cols, width):
    rim = width // 2
    low = lane_of(right.shape) < rim
    zero = jnp.zeros(right.shape, F32)
    blocks = [gradient[:, :, k : k + width] for k in range(0, tile_cols + width, width)]
    blocks[0] = blocks[0] + jnp.where(low, left, zero)
    blocks[-2] = blocks[-2] + jnp.where(low, zero, right)
    blocks[-1] = blocks[-1] + jnp.where(low, right, left)
    return jnp.concatenate(blocks, axis=2)


def rows_kernel(sizes, where_ref, gradient_ref, columns, token_ref, even_ref, odd_ref):
    tile_rows, tile_cols, width, modes, count, n_fast, n_slow = sizes
    slow = lax.rem(where_ref[1], 2)
    edges = []
    for at in (0, tile_rows):
        index = (slice(None), slice(at, at + width))
        right, left = both_sides(slow, *columns, index)
        edges.append(add_columns(gradient_ref[index], right, left, tile_cols, width))
    put_strips(where_ref[0], edges[1], edges[0], (even_ref, odd_ref))


def second_kernel(
    sizes, total, where_ref, starts, descan_ref, extended_ref, gradient_in_ref, probe_ref, measured_ref, tables_ref,
    columns, rows_even_ref, rows_odd_ref, mine_ref, other_ref,
    base_ref, up_ref, down_ref, strips, keep_ref, send_ref, probe_out_ref, descan_out_ref,
    object_ref, gradient_ref, wave_ref, far_ref,
):
    tile_rows, tile_cols, width, modes, count, n_fast, n_slow = sizes
    fast, slow = where_ref[0], where_ref[1]
    core = lax.rem(fast, 2)
    rim = width // 2
    right, left = both_sides(lax.rem(slow, 2), *columns)
    object_ref[...] = extended_ref[...] - OBJECT_STEP * add_columns(
        gradient_in_ref[...], right, left, tile_cols, width
    )
    below, above = both_sides(core, rows_even_ref, rows_odd_ref)
    object_ref[:, :width] -= OBJECT_STEP * above
    object_ref[:, tile_rows:] -= OBJECT_STEP * below
    probe = updated_probe(probe_ref, mine_ref, other_ref, core, total, width, modes)
    probe_out_ref[0] = probe[0].reshape(modes, width, width)
    probe_out_ref[1] = probe[1].reshape(modes, width, width)
    at = modes * width
    descan_rows = [
        descan_ref[k // 3, k % 3] - DESCAN_STEP / total * mine_ref[at + k : at + k + 1] for k in range(6)
    ]
    descan_out_ref[...] = jnp.concatenate(descan_rows + [jnp.zeros((EXTRA - 6, width), F32)], axis=0)
    probe_grad, descan_grad = gradients(
        object_ref, probe, descan_rows, starts, measured_ref, tables_ref, gradient_ref, wave_ref, far_ref,
        sizes + (fast, slow),
    )
    put_sums(probe_grad, descan_grad, keep_ref, send_ref, core, width, modes)
    base_ref[...] = (
        object_ref[:, rim : rim + tile_rows, :tile_cols]
        - OBJECT_STEP * gradient_ref[:, rim : rim + tile_rows, :tile_cols]
    )
    up_ref[...] = gradient_ref[:, :rim, :tile_cols]
    down_ref[...] = gradient_ref[:, rim + tile_rows :, :tile_cols]
    real, imag = gradient_ref[0, :, tile_cols:], gradient_ref[1, :, tile_cols:]
    low = lane_of(real.shape) < rim
    to_right = jnp.where(low, real, pltpu.roll(imag, rim, 1))
    to_left = jnp.where(low, pltpu.roll(real, rim, 1), imag)
    put_strips(slow, to_right, to_left, strips)


def edge_blocks(slow, columns, rows, width):
    rim = width // 2
    right, left = both_sides(lax.rem(slow, 2), *columns, rows)
    low = lane_of(right.shape) < rim
    zero = jnp.zeros(right.shape, F32)
    first = (jnp.where(low, left, zero), jnp.where(low, pltpu.roll(left, rim, 1), zero))
    last = (jnp.where(low, zero, pltpu.roll(right, rim, 1)), jnp.where(low, zero, right))
    return first, last


def last_rows_kernel(sizes, where_ref, up_ref, down_ref, columns, token_ref, even_ref, odd_ref):
    tile_rows, tile_cols, width, modes, count, n_fast, n_slow = sizes
    rim = width // 2
    edges = []
    for in_ref, at in ((up_ref, 0), (down_ref, rim + tile_rows)):
        first, last = edge_blocks(where_ref[1], columns, slice(at, at + rim), width)
        rows = []
        for part in range(2):
            blocks = [in_ref[part, :, k : k + width] for k in range(0, tile_cols, width)]
            blocks[0] = blocks[0] + first[part]
            blocks[-1] = blocks[-1] + last[part]
            rows.append(jnp.concatenate(blocks, axis=1))
        edges.append(jnp.stack(rows))
    put_strips(where_ref[0], edges[1], edges[0], (even_ref, odd_ref))


def object_kernel(sizes, where_ref, base_ref, columns, rows_even_ref, rows_odd_ref, out_ref):
    tile_rows, tile_cols, width, modes, count, n_fast, n_slow = sizes
    rim = width // 2
    out_ref[...] = base_ref[...]
    first, last = edge_blocks(where_ref[1], columns, slice(rim, rim + tile_rows), width)
    for part in range(2):
        out_ref[part, :, :width] -= OBJECT_STEP * first[part]
        out_ref[part, :, tile_cols - width :] -= OBJECT_STEP * last[part]
    below, above = both_sides(lax.rem(where_ref[0], 2), rows_even_ref, rows_odd_ref)
    out_ref[:, :rim] -= OBJECT_STEP * above
    out_ref[:, tile_rows - rim :] -= OBJECT_STEP * below


def probe_kernel(sizes, total, where_ref, probe_ref, descan_ref, mine_ref, other_ref, probe_out_ref, descan_out_ref):
    tile_rows, tile_cols, width, modes, count, n_fast, n_slow = sizes
    core = lax.rem(where_ref[0], 2)
    real, imag = updated_probe(probe_ref, mine_ref, other_ref, core, total, width, modes)
    probe_out_ref[0] = real.reshape(modes, width, width)
    probe_out_ref[1] = imag.reshape(modes, width, width)
    at = modes * width
    rows = descan_ref[...] - DESCAN_STEP / total * mine_ref[at : at + EXTRA]
    lane = lane_of((1, width))
    for k in range(2):
        values = [rows[3 * k + n : 3 * k + n + 1] for n in range(3)]
        row = jnp.where(lane == 0, values[0], jnp.where(lane == 1, values[1], values[2]))
        descan_out_ref[k : k + 1, :] = row[:, :3]


def call(kernel, outs, scratch, *operands, smem=0, hbm=False, semaphores=(), aliases=None, work=0):
    return pl.pallas_call(
        kernel,
        out_shape=[out if isinstance(out, jax.ShapeDtypeStruct) else jax.ShapeDtypeStruct(out, F32) for out in outs],
        in_specs=[SMEM] * smem + [HBM if hbm else VMEM] * (len(operands) - smem),
        out_specs=[VMEM] * len(outs),
        scratch_shapes=[pltpu.VMEM(shape, F32) for shape in scratch]
        + [pltpu.SemaphoreType.DMA(shape) for shape in semaphores],
        input_output_aliases=aliases or {},
        compiler_params=pltpu.CompilerParams(vmem_limit_bytes=LIMIT),
        cost_estimate=pl.CostEstimate(flops=work, bytes_accessed=work // 100, transcendentals=0) if work else None,
    )(*operands)


def on_device(object_field, probe_modes, descan, scan_positions, amplitudes):
    width = amplitudes.shape[-1]
    rim = width // 2
    modes = probe_modes.shape[1]
    count = scan_positions.shape[1]
    tile_rows, tile_cols = object_field.shape[1:]
    n_fast, n_slow = lax.axis_size("fast"), lax.axis_size("slow")
    total = count * n_fast * n_slow
    sizes = (tile_rows, tile_cols, width, modes, count, n_fast, n_slow)
    fast, slow = lax.axis_index("fast"), lax.axis_index("slow")
    where = jnp.stack([fast, slow]).astype(jnp.int32)
    starts = scan_positions.transpose(0, 2, 1)
    tables = transform_tables(width)
    ext_rows, ext_cols = tile_rows + width, tile_cols + width
    half_rows = modes * width
    swaps = 1 if n_slow == 2 else 2

    def partner(place, odd, length):
        other = place ^ 1 if not odd else ((place + 1) ^ 1) - 1
        return other if 0 <= other < length else None

    def exchanged(value, fast_swap=None, slow_swap=None):
        pairs = []
        for f in range(n_fast):
            for s in range(n_slow):
                to_fast = f if fast_swap is None else partner(f, fast_swap, n_fast)
                to_slow = s if slow_swap is None else partner(s, slow_swap, n_slow)
                if to_fast is not None and to_slow is not None:
                    pairs.append((f * n_slow + s, to_fast * n_slow + to_slow))
        return lax.ppermute(value, AXES, pairs)

    def swapped(value, axis, bit):
        return lax.ppermute(value, axis, [(i, i ^ bit) for i in range(lax.axis_size(axis))])

    assert n_fast >= 4 and n_slow >= 2 and not n_fast % 2 and not n_slow % 2
    regular = not (n_fast & (n_fast - 1) or n_slow & (n_slow - 1))
    fast_bits = [1 << k for k in range(1, n_fast.bit_length() - 1)]
    slow_bits = [1 << k for k in range(n_slow.bit_length() - 1)]

    def sum_begun(keep, send):
        mine = keep + swapped(send, "fast", 1)
        if regular:
            for bit in fast_bits[:-1]:
                mine = mine + swapped(mine, "fast", bit)
        return mine

    def sum_ended(mine):
        if regular:
            mine = mine + swapped(mine, "fast", fast_bits[-1])
            for bit in slow_bits:
                mine = mine + swapped(mine, "slow", bit)
        else:
            core = lax.rem(fast, 2)
            every = lax.psum(jnp.where(jnp.arange(2)[:, None, None] == core, mine, 0.0), AXES) * 0.5
            mine = lax.dynamic_index_in_dim(every, core, keepdims=False)
        return mine, swapped(mine[:half_rows], "fast", 1)

    def pairwise(refs):
        return refs if swaps == 2 else (refs[0], None)

    extended, rows_even, rows_odd, *packed = call(
        functools.partial(pack_kernel, sizes),
        [(2, ext_rows, ext_cols)] + [(2, rim, tile_cols)] * 2
        + [(tile_rows, width), (rim, width), (rim, width)] * swaps, [],
        where, object_field, smem=1, hbm=True, semaphores=[()], work=WORK,
    )
    halos = []
    rows_odd = exchanged(rows_odd, 1)
    for k in range(swaps):
        corner_odd = exchanged(packed[3 * k + 2], 1, k)
        middle = exchanged(packed[3 * k], None, k)
        halos += [middle, exchanged(packed[3 * k + 1], 0, k), corner_odd]
    rows_even = exchanged(rows_even, 0)
    def first(info_ref, starts_ref, descan_ref, extended_ref, probe_ref, measured_ref, tables_ref, *rest):
        halo_refs = [rest[2 + 3 * k : 5 + 3 * k] for k in range(swaps)]
        extended_out_ref, gradient_ref, *rest_out = rest[2 + 3 * swaps :]
        first_kernel(sizes, info_ref, starts_ref, descan_ref, extended_ref, probe_ref, measured_ref, tables_ref,
                     *rest[:2], halo_refs, extended_out_ref, gradient_ref, rest_out[:swaps], *rest_out[swaps:])

    scratch = [(count * modes * width, 2 * width), (2 * width, count * modes * width)]
    sums = [(half_rows + EXTRA, width)] * 2
    extended, gradient, *strips, keep, send = call(
        first,
        [(2, ext_rows, ext_cols)] * 2 + [(2, ext_rows, width)] * swaps + sums,
        scratch,
        where, starts, descan, extended, probe_modes, amplitudes, tables, rows_even, rows_odd, *halos,
        smem=3, aliases={3: 0},
    )
    columns = [exchanged(strip, None, k) for k, strip in enumerate(strips)]
    mine = sum_begun(keep, send)

    def rows(where_ref, gradient_ref, *rest):
        rows_kernel(sizes, where_ref, gradient_ref, pairwise(rest[:swaps]), *rest[swaps:])

    rows_even, rows_odd = call(rows, [(2, width, ext_cols)] * 2, [], where, gradient, *columns, mine, smem=1)
    rows_odd = exchanged(rows_odd, 1)
    rows_even = exchanged(rows_even, 0)
    mine, other = sum_ended(mine)

    def second(where_ref, starts_ref, descan_ref, extended_ref, gradient_ref, probe_ref, measured_ref, tables_ref, *rest):
        base_ref, up_ref, down_ref, *rest_out = rest[swaps + 4 :]
        second_kernel(sizes, total, where_ref, starts_ref, descan_ref, extended_ref, gradient_ref, probe_ref,
                      measured_ref, tables_ref, pairwise(rest[:swaps]), *rest[swaps : swaps + 4],
                      base_ref, up_ref, down_ref, rest_out[:swaps], *rest_out[swaps:])

    base, up, down, *strips, keep, send, probes, descan_rows = call(
        second,
        [(2, tile_rows, tile_cols)] + [(2, rim, tile_cols)] * 2 + [(ext_rows, width)] * swaps + sums
        + [probe_modes.shape, (EXTRA, width)],
        [(2, ext_rows, ext_cols)] * 2 + scratch,
        where, starts, descan, extended, gradient, probe_modes, amplitudes, tables,
        *columns, rows_even, rows_odd, mine, other,
        smem=3,
    )
    columns = [exchanged(strip, None, k) for k, strip in enumerate(strips)]
    mine = sum_begun(keep, send)

    def last_rows(where_ref, up_ref, down_ref, *rest):
        last_rows_kernel(sizes, where_ref, up_ref, down_ref, pairwise(rest[:swaps]), *rest[swaps:])

    rows_even, rows_odd = call(last_rows, [(2, rim, tile_cols)] * 2, [], where, up, down, *columns, mine, smem=1)
    rows_odd = exchanged(rows_odd, 1)
    rows_even = exchanged(rows_even, 0)
    mine, other = sum_ended(mine)

    def objects_of(where_ref, base_ref, *rest):
        object_kernel(sizes, where_ref, base_ref, pairwise(rest[:swaps]), *rest[swaps:])

    (objects,) = call(
        objects_of, [(2, tile_rows, tile_cols)], [], where, base, *columns, rows_even, rows_odd, smem=1,
    )
    probes, descan_out = call(
        functools.partial(probe_kernel, sizes, total), [probe_modes.shape, descan.shape], [],
        where, probes, descan_rows, mine, other, smem=1,
    )
    return objects, probes, descan_out


def solution(mesh):
    placed = (P(None, "fast", "slow"), P(), P(), P(None, "fast", "slow"), P("fast", "slow", None))
    return jax.shard_map(
        on_device,
        mesh=mesh,
        in_specs=placed,
        out_specs=(P(None, "fast", "slow"), P(), P()),
        check_vma=False,
    )
```

```python
import functools
import math

import jax
import jax.numpy as jnp
import numpy as np
from jax import lax
from jax.experimental import pallas as pl
from jax.experimental.pallas import tpu as pltpu
from jax.sharding import PartitionSpec as P

OBJECT_STEP = 0.1
PROBE_STEP = 8.0
DESCAN_STEP = 0.02
FLOOR_LEVEL = 0.25
PROBE_POWER = 0.5
EXTRA = 8
AXES = ("fast", "slow")
F32 = jnp.float32
BF16 = jnp.bfloat16
VMEM = pl.BlockSpec(memory_space=pltpu.VMEM)
SMEM = pl.BlockSpec(memory_space=pltpu.SMEM)
HBM = pl.BlockSpec(memory_space=pltpu.HBM)
LIMIT = 40 * 1024 * 1024
WORK = 2_000_000_000


def transform_tables(width):
    counter = np.arange(width)
    angles = 2.0 * np.pi / width * (counter[:, None] * counter[None, :] % width)
    real = np.cos(angles) / math.sqrt(width)
    imag = -np.sin(angles) / math.sqrt(width)
    forward = np.block([[real, imag], [-imag, real]]).astype(np.float32)
    backward = np.block([[real, -imag], [imag, real]]).astype(np.float32)
    parts = []
    for table in (forward, backward):
        high = table.astype(BF16)
        parts += [high, (table - high.astype(np.float32)).astype(BF16)]
    return jnp.asarray(np.stack(parts))


def split(value):
    high = value.astype(BF16)
    return high, (value - high.astype(F32)).astype(BF16)


def dot(a, b):
    return jnp.dot(a, b, preferred_element_type=F32)


def product(left, right):
    (left_high, left_low), (right_high, right_low) = left, right
    return dot(left_high, right_high) + dot(left_high, right_low) + dot(left_low, right_high)


def lane_of(shape):
    return lax.broadcasted_iota(jnp.int32, shape, len(shape) - 1)


def window_place(starts, j, tile_rows, tile_cols, width, fast, slow):
    rim = width // 2
    row = starts[0, 0, j] - fast * tile_rows + rim
    col = starts[1, 0, j] - slow * tile_cols
    lane = jnp.where(col < 0, col + tile_cols + width, col)
    block = jnp.minimum(row // 8, (tile_rows + width - width - 8) // 8)
    return block * 8, row - block * 8, lane


def gradients(
    object_ref, probe, descan_rows, starts, measured_ref, tables_ref, gradient_ref, wave_ref, far_ref, sizes
):
    tile_rows, tile_cols, width, modes, count, n_fast, n_slow, fast, slow = sizes
    ext_cols = tile_cols + width
    high = width + 8
    probe_real, probe_imag = probe
    lane_row = lane_of((1, width)).astype(F32)
    centred = (lane_row - width // 2) / width
    tables = [tables_ref[k] for k in range(4)]
    forward, backward = (tables[0], tables[1]), (tables[2], tables[3])

    fractions = []
    phases = []
    for j in range(count):
        frac_row = jnp.full((1, width), starts[0, 0, j], jnp.int32).astype(F32) / (tile_rows * n_fast)
        frac_col = jnp.full((1, width), starts[1, 0, j], jnp.int32).astype(F32) / (tile_cols * n_slow)
        fractions.append((frac_row, frac_col))
        for k in range(2):
            d = descan_rows[3 * k : 3 * k + 3]
            phases.append((2 * math.pi) * ((d[0] + d[1] * frac_row + d[2] * frac_col) * centred))
    while len(phases) % 8:
        phases.append(jnp.zeros((1, width), F32))
    phases = jnp.concatenate(phases, axis=0)
    cosines, sines = jnp.cos(phases), jnp.sin(phases)

    def along_rows(row):
        return jnp.transpose(jnp.broadcast_to(row, (width, width)))

    lits = []
    ramps = []
    for j in range(count):
        row_start, row_shift, lane = window_place(starts, j, tile_rows, tile_cols, width, fast, slow)
        row_start = pl.multiple_of(row_start, 8)
        row_cos, row_sin = along_rows(cosines[2 * j : 2 * j + 1]), along_rows(sines[2 * j : 2 * j + 1])
        col_cos, col_sin = cosines[2 * j + 1 : 2 * j + 2], sines[2 * j + 1 : 2 * j + 2]
        ramp_real = row_cos * col_cos - row_sin * col_sin
        ramp_imag = row_cos * col_sin + row_sin * col_cos
        patch = []
        for part in range(2):
            rows = object_ref[part, pl.ds(row_start, high), :]
            rows = pltpu.roll(rows, lax.rem(ext_cols - lane, ext_cols), 1)[:, :width]
            patch.append(pltpu.roll(rows, lax.rem(high - row_shift, high), 0)[:width])
        lit_real = patch[0] * ramp_real - patch[1] * ramp_imag
        lit_imag = patch[0] * ramp_imag + patch[1] * ramp_real
        lits.append((lit_real, lit_imag))
        ramps.append((ramp_real, ramp_imag))
        for m in range(modes):
            p_real = probe_real[m * width : (m + 1) * width]
            p_imag = probe_imag[m * width : (m + 1) * width]
            at = (j * modes + m) * width
            wave_ref[at : at + width, :width] = p_real * lit_real - p_imag * lit_imag
            wave_ref[at : at + width, width:] = p_real * lit_imag + p_imag * lit_real

    half = product(split(wave_ref[...]), forward)
    for w in range(count * modes):
        at = w * width
        far_ref[:width, at : at + width] = half[at : at + width, :width]
        far_ref[width:, at : at + width] = half[at : at + width, width:]
    far = product(backward, split(far_ref[...]))
    far_ref[...] = far
    for j in range(count):
        intensity = None
        for m in range(modes):
            at = (j * modes + m) * width
            real, imag = far_ref[:width, at : at + width], far_ref[width:, at : at + width]
            power = real * real + imag * imag
            intensity = power if intensity is None else intensity + power
        factor = 1.0 - measured_ref[j] / jnp.sqrt(jnp.maximum(intensity, FLOOR_LEVEL))
        for m in range(modes):
            at = (j * modes + m) * width
            far_ref[:width, at : at + width] *= factor
            far_ref[width:, at : at + width] *= factor
    half = product(forward, split(far_ref[...]))
    for w in range(count * modes):
        at = w * width
        wave_ref[at : at + width, :width] = half[:width, at : at + width]
        wave_ref[at : at + width, width:] = half[width:, at : at + width]
    wave_ref[...] = product(split(wave_ref[...]), backward)

    gradient_ref[...] = jnp.zeros(gradient_ref.shape, F32)
    probe_grad = [[None] * modes, [None] * modes]
    descan_grad = [None] * 6
    centred_rows = along_rows(centred)
    for j in range(count):
        lit_real, lit_imag = lits[j]
        ramp_real, ramp_imag = ramps[j]
        sum_real = sum_imag = None
        for m in range(modes):
            p_real = probe_real[m * width : (m + 1) * width]
            p_imag = probe_imag[m * width : (m + 1) * width]
            at = (j * modes + m) * width
            real, imag = wave_ref[at : at + width, :width], wave_ref[at : at + width, width:]
            q_real = lit_real * real + lit_imag * imag
            q_imag = lit_real * imag - lit_imag * real
            probe_grad[0][m] = q_real if j == 0 else probe_grad[0][m] + q_real
            probe_grad[1][m] = q_imag if j == 0 else probe_grad[1][m] + q_imag
            h_real = p_real * real + p_imag * imag
            h_imag = p_real * imag - p_imag * real
            sum_real = h_real if m == 0 else sum_real + h_real
            sum_imag = h_imag if m == 0 else sum_imag + h_imag
        twist = lit_imag * sum_real - lit_real * sum_imag
        totals = (
            jnp.sum(jnp.sum(twist * centred_rows, axis=0, keepdims=True), axis=1, keepdims=True),
            jnp.sum(jnp.sum(twist, axis=0, keepdims=True) * centred, axis=1, keepdims=True),
        )
        frac_row, frac_col = fractions[j]
        for k in range(2):
            base = jnp.broadcast_to(-4 * math.pi * totals[k], (1, width))
            for n, term in enumerate((base, base * frac_row, base * frac_col)):
                descan_grad[3 * k + n] = term if j == 0 else descan_grad[3 * k + n] + term
        row_start, row_shift, lane = window_place(starts, j, tile_rows, tile_cols, width, fast, slow)
        row_start = pl.multiple_of(row_start, 8)
        parts = (
            ramp_real * sum_real + ramp_imag * sum_imag,
            ramp_real * sum_imag - ramp_imag * sum_real,
        )
        for part in range(2):
            value = jnp.concatenate([parts[part], jnp.zeros((8, width), F32)], axis=0)
            value = pltpu.roll(value, row_shift, 0)
            value = jnp.concatenate([value, jnp.zeros((high, ext_cols - width), F32)], axis=1)
            gradient_ref[part, pl.ds(row_start, high), :] += pltpu.roll(value, lane, 1)
    return probe_grad, descan_grad


def pick(parity, when_even, when_odd):
    return jnp.where(parity == 0, when_even, when_odd)


def both_sides(parity, even_ref, odd_ref, index=Ellipsis):
    even = even_ref[index]
    odd = jnp.zeros_like(even) if odd_ref is None else odd_ref[index]
    return pick(parity, even, odd), pick(parity, odd, even)


def put_sums(probe_grad, descan_grad, keep_ref, send_ref, core, width, modes):
    for m in range(modes):
        real, imag = probe_grad[0][m], probe_grad[1][m]
        keep_ref[m * width : (m + 1) * width] = jnp.where(core == 0, real, imag)
        send_ref[m * width : (m + 1) * width] = jnp.where(core == 0, imag, real)
    block = jnp.concatenate(descan_grad + [jnp.zeros((EXTRA - 6, width), F32)], axis=0)
    keep_ref[modes * width :] = block
    send_ref[modes * width :] = block


def put_quarters(probe_grad, descan_grad, mine_ref, beside_ref, send_ref, core, slow, width, modes):
    rows = modes * width
    real, imag = jnp.concatenate(probe_grad[0], axis=0), jnp.concatenate(probe_grad[1], axis=0)
    keep, send = pick(core, real, imag), pick(core, imag, real)
    half = rows // 2
    block = jnp.concatenate(descan_grad + [jnp.zeros((EXTRA - 6, width), F32)], axis=0)
    low, high = keep[:half], keep[half:]
    mine_ref[:half] = pick(slow, low, high)
    mine_ref[half:] = block
    beside_ref[:half] = pick(slow, high, low)
    beside_ref[half:] = block
    low, high = send[:half], send[half:]
    send_ref[0, :half] = pick(slow, low, high)
    send_ref[0, half:] = block
    send_ref[1, :half] = pick(slow, high, low)
    send_ref[1, half:] = block


def of_halves(halves, core, slow, rows):
    mine, other = halves[0][:rows], halves[1][...]
    return pick(core, mine, other), pick(core, other, mine)


def of_quarters(quarters, core, slow, rows):
    part = rows // 2
    values = [quarters[0][:part], quarters[1][...], quarters[2][:part], quarters[2][part:]]
    sums = []
    for own, beside in (
        (pick(core, values[0], values[2]), pick(core, values[1], values[3])),
        (pick(core, values[2], values[0]), pick(core, values[3], values[1])),
    ):
        sums.append(jnp.concatenate([pick(slow, own, beside), pick(slow, beside, own)], axis=0))
    return sums


def updated_probe(probe_ref, sums, total, width, modes):
    rows = modes * width
    real = probe_ref[0].reshape(rows, width) - PROBE_STEP / total * sums[0]
    imag = probe_ref[1].reshape(rows, width) - PROBE_STEP / total * sums[1]
    power = jnp.sum(jnp.sum(real * real + imag * imag, axis=0, keepdims=True), axis=1, keepdims=True)
    scale = jnp.sqrt(PROBE_POWER * rows * width / power)
    return real * scale, imag * scale


def halo_blocks(right, left, width):
    rim = width // 2
    low = lane_of(right.shape) < rim
    return jnp.where(low, right, pltpu.roll(left, rim, 1)), jnp.where(low, pltpu.roll(right, rim, 1), left)


def pack_kernel(sizes, where_ref, object_ref, extended_ref, rows_even_ref, rows_odd_ref, *rest):
    tile_rows, tile_cols, width, modes, count, n_fast, n_slow = sizes
    rim = width // 2
    *rest, semaphore = rest
    inner = extended_ref.at[:, rim : rim + tile_rows, :tile_cols]
    copy = pltpu.make_async_copy(object_ref, inner, semaphore)
    copy.start()
    copy.wait()
    fast, slow = lax.rem(where_ref[0], 2), lax.rem(where_ref[1], 2)
    initial, final = extended_ref[:, rim:width, :tile_cols], extended_ref[:, tile_rows : rim + tile_rows, :tile_cols]
    rows_even_ref[...] = pick(fast, final, initial)
    rows_odd_ref[...] = pick(fast, initial, final)
    low = lane_of((tile_rows, width)) < rim
    end = extended_ref[:, rim : rim + tile_rows, tile_cols - width : tile_cols]
    start = extended_ref[:, rim : rim + tile_rows, :width]
    to_right = jnp.where(low, pltpu.roll(end[0], rim, 1), end[1])
    to_left = jnp.where(low, start[0], pltpu.roll(start[1], rim, 1))
    strips = (pick(slow, to_right, to_left), pick(slow, to_left, to_right))
    for k in range(len(rest) // 3):
        strip = strips[k]
        rest[3 * k][...] = strip
        rest[3 * k + 1][...] = pick(fast, strip[tile_rows - rim :], strip[:rim])
        rest[3 * k + 2][...] = pick(fast, strip[:rim], strip[tile_rows - rim :])


def first_kernel(
    sizes, info, starts, descan_ref, extended_in_ref, probe_ref, measured_ref, tables_ref,
    rows_even_ref, rows_odd_ref, halos,
    extended_ref, gradient_ref, strips, keep_ref, send_ref, wave_ref, far_ref,
):
    tile_rows, tile_cols, width, modes, count, n_fast, n_slow = sizes
    fast, slow = info[0], info[1]
    core = lax.rem(fast, 2)
    rim = width // 2
    below, above = both_sides(core, rows_even_ref, rows_odd_ref)
    extended_ref[:, :rim, :tile_cols] = above
    extended_ref[:, rim + tile_rows :, :tile_cols] = below
    columns = []
    for middle_ref, even_ref, odd_ref in halos:
        after, before = both_sides(core, even_ref, odd_ref)
        columns.append(((0, before), (rim, middle_ref[...]), (rim + tile_rows, after)))
    for piece in range(3):
        at, even = columns[0][piece]
        odd = columns[-1][piece][1]
        real, imag = halo_blocks(pick(lax.rem(slow, 2), even, odd), pick(lax.rem(slow, 2), odd, even), width)
        extended_ref[0, at : at + even.shape[0], tile_cols:] = real
        extended_ref[1, at : at + even.shape[0], tile_cols:] = imag
    descan_rows = [jnp.full((1, width), descan_ref[k // 3, k % 3], F32) for k in range(6)]
    probe = tuple(probe_ref[part].reshape(modes * width, width) for part in range(2))
    probe_grad, descan_grad = gradients(
        extended_ref, probe, descan_rows, starts, measured_ref, tables_ref, gradient_ref, wave_ref, far_ref,
        sizes + (fast, slow),
    )
    put_sums(probe_grad, descan_grad, keep_ref, send_ref, core, width, modes)
    halo = gradient_ref[:, :, tile_cols:]
    low = lane_of(halo.shape) < rim
    to_right = jnp.where(low, halo, gradient_ref[:, :, tile_cols - width : tile_cols])
    to_left = jnp.where(low, gradient_ref[:, :, :width], halo)
    put_strips(slow, to_right, to_left, strips)


def put_strips(place, to_next, to_previous, refs):
    parity = lax.rem(place, 2)
    refs[0][...] = pick(parity, to_next, to_previous)
    if len(refs) > 1:
        refs[1][...] = pick(parity, to_previous, to_next)


def add_columns(gradient, right, left, tile_cols, width):
    rim = width // 2
    low = lane_of(right.shape) < rim
    zero = jnp.zeros(right.shape, F32)
    blocks = [gradient[:, :, k : k + width] for k in range(0, tile_cols + width, width)]
    blocks[0] = blocks[0] + jnp.where(low, left, zero)
    blocks[-2] = blocks[-2] + jnp.where(low, zero, right)
    blocks[-1] = blocks[-1] + jnp.where(low, right, left)
    return jnp.concatenate(blocks, axis=2)


def rows_kernel(sizes, where_ref, gradient_ref, columns, token_ref, even_ref, odd_ref):
    tile_rows, tile_cols, width, modes, count, n_fast, n_slow = sizes
    slow = lax.rem(where_ref[1], 2)
    edges = []
    for at in (0, tile_rows):
        index = (slice(None), slice(at, at + width))
        right, left = both_sides(slow, *columns, index)
        edges.append(add_columns(gradient_ref[index], right, left, tile_cols, width))
    put_strips(where_ref[0], edges[1], edges[0], (even_ref, odd_ref))


def second_kernel(
    sizes, total, where_ref, starts, descan_ref, extended_ref, gradient_in_ref, probe_ref, measured_ref, tables_ref,
    columns, rows_even_ref, rows_odd_ref, mine_ref, other_ref,
    base_ref, up_ref, down_ref, strips, own_ref, beside_ref, send_ref, probe_out_ref, descan_out_ref,
    object_ref, gradient_ref, wave_ref, far_ref,
):
    tile_rows, tile_cols, width, modes, count, n_fast, n_slow = sizes
    fast, slow = where_ref[0], where_ref[1]
    core = lax.rem(fast, 2)
    rim = width // 2
    right, left = both_sides(lax.rem(slow, 2), *columns)
    object_ref[...] = extended_ref[...] - OBJECT_STEP * add_columns(
        gradient_in_ref[...], right, left, tile_cols, width
    )
    below, above = both_sides(core, rows_even_ref, rows_odd_ref)
    object_ref[:, :width] -= OBJECT_STEP * above
    object_ref[:, tile_rows:] -= OBJECT_STEP * below
    sums = of_halves((mine_ref, other_ref), core, slow, modes * width)
    probe = updated_probe(probe_ref, sums, total, width, modes)
    probe_out_ref[0] = probe[0].reshape(modes, width, width)
    probe_out_ref[1] = probe[1].reshape(modes, width, width)
    at = modes * width
    descan_rows = [
        descan_ref[k // 3, k % 3] - DESCAN_STEP / total * mine_ref[at + k : at + k + 1] for k in range(6)
    ]
    descan_out_ref[...] = jnp.concatenate(descan_rows + [jnp.zeros((EXTRA - 6, width), F32)], axis=0)
    probe_grad, descan_grad = gradients(
        object_ref, probe, descan_rows, starts, measured_ref, tables_ref, gradient_ref, wave_ref, far_ref,
        sizes + (fast, slow),
    )
    put_quarters(probe_grad, descan_grad, own_ref, beside_ref, send_ref, core, lax.rem(slow, 2), width, modes)
    base_ref[...] = (
        object_ref[:, rim : rim + tile_rows, :tile_cols]
        - OBJECT_STEP * gradient_ref[:, rim : rim + tile_rows, :tile_cols]
    )
    up_ref[...] = gradient_ref[:, :rim, :tile_cols]
    down_ref[...] = gradient_ref[:, rim + tile_rows :, :tile_cols]
    real, imag = gradient_ref[0, :, tile_cols:], gradient_ref[1, :, tile_cols:]
    low = lane_of(real.shape) < rim
    to_right = jnp.where(low, real, pltpu.roll(imag, rim, 1))
    to_left = jnp.where(low, pltpu.roll(real, rim, 1), imag)
    put_strips(slow, to_right, to_left, strips)


def edge_blocks(slow, columns, rows, width):
    rim = width // 2
    right, left = both_sides(lax.rem(slow, 2), *columns, rows)
    low = lane_of(right.shape) < rim
    zero = jnp.zeros(right.shape, F32)
    first = (jnp.where(low, left, zero), jnp.where(low, pltpu.roll(left, rim, 1), zero))
    last = (jnp.where(low, zero, pltpu.roll(right, rim, 1)), jnp.where(low, zero, right))
    return first, last


def last_rows_kernel(sizes, where_ref, up_ref, down_ref, columns, mine_ref, arrived_ref, even_ref, odd_ref, sum_ref):
    tile_rows, tile_cols, width, modes, count, n_fast, n_slow = sizes
    rim = width // 2
    sum_ref[...] = mine_ref[...] + arrived_ref[...]
    edges = []
    for in_ref, at in ((up_ref, 0), (down_ref, rim + tile_rows)):
        first, last = edge_blocks(where_ref[1], columns, slice(at, at + rim), width)
        rows = []
        for part in range(2):
            blocks = [in_ref[part, :, k : k + width] for k in range(0, tile_cols, width)]
            blocks[0] = blocks[0] + first[part]
            blocks[-1] = blocks[-1] + last[part]
            rows.append(jnp.concatenate(blocks, axis=1))
        edges.append(jnp.stack(rows))
    put_strips(where_ref[0], edges[1], edges[0], (even_ref, odd_ref))


def join_kernel(own_ref, beside_ref, *rest):
    rows = own_ref.shape[0]
    rest[-1][:rows] = own_ref[...]
    rest[-1][rows:] = beside_ref[...]


def object_kernel(sizes, where_ref, base_ref, columns, rows_even_ref, rows_odd_ref, out_ref):
    tile_rows, tile_cols, width, modes, count, n_fast, n_slow = sizes
    rim = width // 2
    out_ref[...] = base_ref[...]
    first, last = edge_blocks(where_ref[1], columns, slice(rim, rim + tile_rows), width)
    for part in range(2):
        out_ref[part, :, :width] -= OBJECT_STEP * first[part]
        out_ref[part, :, tile_cols - width :] -= OBJECT_STEP * last[part]
    below, above = both_sides(lax.rem(where_ref[0], 2), rows_even_ref, rows_odd_ref)
    out_ref[:, :rim] -= OBJECT_STEP * above
    out_ref[:, tile_rows - rim :] -= OBJECT_STEP * below


def probe_kernel(sizes, total, where_ref, probe_ref, descan_ref, quarters, probe_out_ref, descan_out_ref):
    tile_rows, tile_cols, width, modes, count, n_fast, n_slow = sizes
    core, slow = lax.rem(where_ref[0], 2), lax.rem(where_ref[1], 2)
    sums = of_quarters(quarters, core, slow, modes * width)
    real, imag = updated_probe(probe_ref, sums, total, width, modes)
    probe_out_ref[0] = real.reshape(modes, width, width)
    probe_out_ref[1] = imag.reshape(modes, width, width)
    at = modes * width // 2
    rows = descan_ref[...] - DESCAN_STEP / total * quarters[0][at : at + EXTRA]
    lane = lane_of((1, width))
    for k in range(2):
        values = [rows[3 * k + n : 3 * k + n + 1] for n in range(3)]
        row = jnp.where(lane == 0, values[0], jnp.where(lane == 1, values[1], values[2]))
        descan_out_ref[k : k + 1, :] = row[:, :3]


def call(kernel, outs, scratch, *operands, smem=0, hbm=False, semaphores=(), aliases=None, work=0):
    return pl.pallas_call(
        kernel,
        out_shape=[out if isinstance(out, jax.ShapeDtypeStruct) else jax.ShapeDtypeStruct(out, F32) for out in outs],
        in_specs=[SMEM] * smem + [HBM if hbm else VMEM] * (len(operands) - smem),
        out_specs=[VMEM] * len(outs),
        scratch_shapes=[pltpu.VMEM(shape, F32) for shape in scratch]
        + [pltpu.SemaphoreType.DMA(shape) for shape in semaphores],
        input_output_aliases=aliases or {},
        compiler_params=pltpu.CompilerParams(vmem_limit_bytes=LIMIT),
        cost_estimate=pl.CostEstimate(flops=work, bytes_accessed=work // 100, transcendentals=0) if work else None,
    )(*operands)


def on_device(object_field, probe_modes, descan, scan_positions, amplitudes):
    width = amplitudes.shape[-1]
    rim = width // 2
    modes = probe_modes.shape[1]
    count = scan_positions.shape[1]
    tile_rows, tile_cols = object_field.shape[1:]
    n_fast, n_slow = lax.axis_size("fast"), lax.axis_size("slow")
    total = count * n_fast * n_slow
    sizes = (tile_rows, tile_cols, width, modes, count, n_fast, n_slow)
    fast, slow = lax.axis_index("fast"), lax.axis_index("slow")
    where = jnp.stack([fast, slow]).astype(jnp.int32)
    starts = scan_positions.transpose(0, 2, 1)
    tables = transform_tables(width)
    ext_rows, ext_cols = tile_rows + width, tile_cols + width
    half_rows = modes * width
    swaps = 1 if n_slow == 2 else 2

    def partner(place, odd, length):
        other = place ^ 1 if not odd else ((place + 1) ^ 1) - 1
        return other if 0 <= other < length else None

    def exchanged(value, fast_swap=None, slow_swap=None):
        pairs = []
        for f in range(n_fast):
            for s in range(n_slow):
                to_fast = f if fast_swap is None else partner(f, fast_swap, n_fast)
                to_slow = s if slow_swap is None else partner(s, slow_swap, n_slow)
                if to_fast is not None and to_slow is not None:
                    pairs.append((f * n_slow + s, to_fast * n_slow + to_slow))
        return lax.ppermute(value, AXES, pairs)

    def swapped(value, axis, bit):
        return lax.ppermute(value, axis, [(i, i ^ bit) for i in range(lax.axis_size(axis))])

    assert n_fast >= 4 and n_slow >= 2 and not n_fast % 2 and not n_slow % 2
    regular = not (n_fast & (n_fast - 1) or n_slow & (n_slow - 1))
    fast_bits = [1 << k for k in range(1, n_fast.bit_length() - 1)]
    slow_bits = [1 << k for k in range(n_slow.bit_length() - 1)]

    def sum_begun(keep, send):
        mine = keep + swapped(send, "fast", 1)
        if regular:
            for bit in fast_bits[:-1]:
                mine = mine + swapped(mine, "fast", bit)
        return mine

    def sum_ended(mine):
        if regular:
            mine = mine + swapped(mine, "fast", fast_bits[-1])
            for bit in slow_bits:
                mine = mine + swapped(mine, "slow", bit)
        else:
            core = lax.rem(fast, 2)
            every = lax.psum(jnp.where(jnp.arange(2)[:, None, None] == core, mine, 0.0), AXES) * 0.5
            mine = lax.dynamic_index_in_dim(every, core, keepdims=False)
        return mine, swapped(mine[:half_rows], "fast", 1)

    def pairwise(refs):
        return refs if swaps == 2 else (refs[0], None)

    extended, rows_even, rows_odd, *packed = call(
        functools.partial(pack_kernel, sizes),
        [(2, ext_rows, ext_cols)] + [(2, rim, tile_cols)] * 2
        + [(tile_rows, width), (rim, width), (rim, width)] * swaps, [],
        where, object_field, smem=1, hbm=True, semaphores=[()], work=WORK,
    )
    halos = []
    rows_odd = exchanged(rows_odd, 1)
    for k in range(swaps):
        corner_odd = exchanged(packed[3 * k + 2], 1, k)
        middle = exchanged(packed[3 * k], None, k)
        halos += [middle, exchanged(packed[3 * k + 1], 0, k), corner_odd]
    rows_even = exchanged(rows_even, 0)
    def first(info_ref, starts_ref, descan_ref, extended_ref, probe_ref, measured_ref, tables_ref, *rest):
        halo_refs = [rest[2 + 3 * k : 5 + 3 * k] for k in range(swaps)]
        extended_out_ref, gradient_ref, *rest_out = rest[2 + 3 * swaps :]
        first_kernel(sizes, info_ref, starts_ref, descan_ref, extended_ref, probe_ref, measured_ref, tables_ref,
                     *rest[:2], halo_refs, extended_out_ref, gradient_ref, rest_out[:swaps], *rest_out[swaps:])

    scratch = [(count * modes * width, 2 * width), (2 * width, count * modes * width)]
    sums = [(half_rows + EXTRA, width)] * 2
    extended, gradient, *strips, keep, send = call(
        first,
        [(2, ext_rows, ext_cols)] * 2 + [(2, ext_rows, width)] * swaps + sums,
        scratch,
        where, starts, descan, extended, probe_modes, amplitudes, tables, rows_even, rows_odd, *halos,
        smem=3, aliases={3: 0},
    )
    columns = [exchanged(strip, None, k) for k, strip in enumerate(strips)]
    mine = sum_begun(keep, send)

    def rows(where_ref, gradient_ref, *rest):
        rows_kernel(sizes, where_ref, gradient_ref, pairwise(rest[:swaps]), *rest[swaps:])

    rows_even, rows_odd = call(rows, [(2, width, ext_cols)] * 2, [], where, gradient, *columns, mine, smem=1)
    rows_odd = exchanged(rows_odd, 1)
    rows_even = exchanged(rows_even, 0)
    mine, other = sum_ended(mine)

    def second(where_ref, starts_ref, descan_ref, extended_ref, gradient_ref, probe_ref, measured_ref, tables_ref, *rest):
        base_ref, up_ref, down_ref, *rest_out = rest[swaps + 4 :]
        second_kernel(sizes, total, where_ref, starts_ref, descan_ref, extended_ref, gradient_ref, probe_ref,
                      measured_ref, tables_ref, pairwise(rest[:swaps]), *rest[swaps : swaps + 4],
                      base_ref, up_ref, down_ref, rest_out[:swaps], *rest_out[swaps:])

    part = (half_rows // 2 + EXTRA, width)
    base, up, down, *strips, mine, beside, send, probes, descan_rows = call(
        second,
        [(2, tile_rows, tile_cols)] + [(2, rim, tile_cols)] * 2 + [(ext_rows, width)] * swaps + [part, part, (2, *part)]
        + [probe_modes.shape, (EXTRA, width)],
        [(2, ext_rows, ext_cols)] * 2 + scratch,
        where, starts, descan, extended, gradient, probe_modes, amplitudes, tables,
        *columns, rows_even, rows_odd, mine, other,
        smem=3,
    )
    columns = [exchanged(strip, None, k) for k, strip in enumerate(strips)]
    core_part = swapped(send, "fast", 1)
    mine = mine + core_part[0] + swapped(beside + core_part[1], "slow", 1)
    steps = [("fast", bit) for bit in fast_bits] + [("slow", bit) for bit in slow_bits[1:]]

    def last_rows(where_ref, up_ref, down_ref, *rest):
        last_rows_kernel(sizes, where_ref, up_ref, down_ref, pairwise(rest[:swaps]), *rest[swaps:])

    arrived = swapped(mine, *steps[0]) if regular else jnp.zeros_like(mine)
    rows_even, rows_odd, mine = call(
        last_rows, [(2, rim, tile_cols)] * 2 + [part], [], where, up, down, *columns, mine, arrived, smem=1,
    )
    rows_odd = exchanged(rows_odd, 1)
    rows_even = exchanged(rows_even, 0)
    if regular:
        for step in steps[1:]:
            mine = mine + swapped(mine, *step)
    else:
        place = 2 * lax.rem(fast, 2) + lax.rem(slow, 2)
        every = lax.psum(jnp.where(jnp.arange(4)[:, None, None] == place, mine, 0.0), AXES)
        mine = lax.dynamic_index_in_dim(every, place, keepdims=False)
    own = mine[: half_rows // 2]
    beside = swapped(own, "slow", 1)
    (both,) = call(join_kernel, [(half_rows, width)], [], own, beside, rows_even, rows_odd)
    other = swapped(both, "fast", 1)

    def objects_of(where_ref, base_ref, *rest):
        object_kernel(sizes, where_ref, base_ref, pairwise(rest[:swaps]), *rest[swaps:])

    (objects,) = call(
        objects_of, [(2, tile_rows, tile_cols)], [], where, base, *columns, rows_even, rows_odd, smem=1,
    )

    def probe_of(where_ref, probe_ref, descan_ref, q0, q1, q2, *outs):
        probe_kernel(sizes, total, where_ref, probe_ref, descan_ref, (q0, q1, q2), *outs)

    probes, descan_out = call(
        probe_of, [probe_modes.shape, descan.shape], [],
        where, probes, descan_rows, mine, beside, other, smem=1,
    )
    return objects, probes, descan_out


def solution(mesh):
    placed = (P(None, "fast", "slow"), P(), P(), P(None, "fast", "slow"), P("fast", "slow", None))
    return jax.shard_map(
        on_device,
        mesh=mesh,
        in_specs=placed,
        out_specs=(P(None, "fast", "slow"), P(), P()),
        check_vma=False,
    )
```

```python
import functools
import math

import jax
import jax.numpy as jnp
import numpy as np
from jax import lax
from jax.experimental import pallas as pl
from jax.experimental.pallas import tpu as pltpu
from jax.sharding import PartitionSpec as P

OBJECT_STEP = 0.1
PROBE_STEP = 8.0
DESCAN_STEP = 0.02
FLOOR_LEVEL = 0.25
PROBE_POWER = 0.5
EXTRA = 8
AXES = ("fast", "slow")
F32 = jnp.float32
BF16 = jnp.bfloat16
VMEM = pl.BlockSpec(memory_space=pltpu.VMEM)
SMEM = pl.BlockSpec(memory_space=pltpu.SMEM)
HBM = pl.BlockSpec(memory_space=pltpu.HBM)
LIMIT = 40 * 1024 * 1024
WORK = 2_000_000_000


def transform_tables(width):
    counter = np.arange(width)
    angles = 2.0 * np.pi / width * (counter[:, None] * counter[None, :] % width)
    real = np.cos(angles) / math.sqrt(width)
    imag = -np.sin(angles) / math.sqrt(width)
    forward = np.block([[real, imag], [-imag, real]]).astype(np.float32)
    backward = np.block([[real, -imag], [imag, real]]).astype(np.float32)
    parts = []
    for table in (forward, backward):
        high = table.astype(BF16)
        parts += [high, (table - high.astype(np.float32)).astype(BF16)]
    return jnp.asarray(np.stack(parts))


def split(value):
    high = value.astype(BF16)
    return high, (value - high.astype(F32)).astype(BF16)


def dot(a, b):
    return jnp.dot(a, b, preferred_element_type=F32)


def product(left, right):
    (left_high, left_low), (right_high, right_low) = left, right
    return dot(left_high, right_high) + dot(left_high, right_low) + dot(left_low, right_high)


def lane_of(shape):
    return lax.broadcasted_iota(jnp.int32, shape, len(shape) - 1)


def window_place(starts, j, tile_rows, tile_cols, width, fast, slow):
    rim = width // 2
    row = starts[0, 0, j] - fast * tile_rows + rim
    col = starts[1, 0, j] - slow * tile_cols
    lane = jnp.where(col < 0, col + tile_cols + width, col)
    block = jnp.minimum(row // 8, (tile_rows + width - width - 8) // 8)
    return block * 8, row - block * 8, lane


def gradients(
    object_ref, probe, descan_rows, starts, measured_ref, tables_ref, gradient_ref, wave_ref, far_ref, sizes
):
    tile_rows, tile_cols, width, modes, count, n_fast, n_slow, fast, slow = sizes
    ext_cols = tile_cols + width
    high = width + 8
    probe_real, probe_imag = probe
    lane_row = lane_of((1, width)).astype(F32)
    centred = (lane_row - width // 2) / width
    tables = [tables_ref[k] for k in range(4)]
    forward, backward = (tables[0], tables[1]), (tables[2], tables[3])

    fractions = []
    phases = []
    for j in range(count):
        frac_row = jnp.full((1, width), starts[0, 0, j], jnp.int32).astype(F32) / (tile_rows * n_fast)
        frac_col = jnp.full((1, width), starts[1, 0, j], jnp.int32).astype(F32) / (tile_cols * n_slow)
        fractions.append((frac_row, frac_col))
        for k in range(2):
            d = descan_rows[3 * k : 3 * k + 3]
            phases.append((2 * math.pi) * ((d[0] + d[1] * frac_row + d[2] * frac_col) * centred))
    while len(phases) % 8:
        phases.append(jnp.zeros((1, width), F32))
    phases = jnp.concatenate(phases, axis=0)
    cosines, sines = jnp.cos(phases), jnp.sin(phases)

    def along_rows(row):
        return jnp.transpose(jnp.broadcast_to(row, (width, width)))

    lits = []
    ramps = []
    for j in range(count):
        row_start, row_shift, lane = window_place(starts, j, tile_rows, tile_cols, width, fast, slow)
        row_start = pl.multiple_of(row_start, 8)
        row_cos, row_sin = along_rows(cosines[2 * j : 2 * j + 1]), along_rows(sines[2 * j : 2 * j + 1])
        col_cos, col_sin = cosines[2 * j + 1 : 2 * j + 2], sines[2 * j + 1 : 2 * j + 2]
        ramp_real = row_cos * col_cos - row_sin * col_sin
        ramp_imag = row_cos * col_sin + row_sin * col_cos
        patch = []
        for part in range(2):
            rows = object_ref[part, pl.ds(row_start, high), :]
            rows = pltpu.roll(rows, lax.rem(ext_cols - lane, ext_cols), 1)[:, :width]
            patch.append(pltpu.roll(rows, lax.rem(high - row_shift, high), 0)[:width])
        lit_real = patch[0] * ramp_real - patch[1] * ramp_imag
        lit_imag = patch[0] * ramp_imag + patch[1] * ramp_real
        lits.append((lit_real, lit_imag))
        ramps.append((ramp_real, ramp_imag))
        for m in range(modes):
            p_real = probe_real[m * width : (m + 1) * width]
            p_imag = probe_imag[m * width : (m + 1) * width]
            at = (j * modes + m) * width
            wave_ref[at : at + width, :width] = p_real * lit_real - p_imag * lit_imag
            wave_ref[at : at + width, width:] = p_real * lit_imag + p_imag * lit_real

    half = product(split(wave_ref[...]), forward)
    for w in range(count * modes):
        at = w * width
        far_ref[:width, at : at + width] = half[at : at + width, :width]
        far_ref[width:, at : at + width] = half[at : at + width, width:]
    far = product(backward, split(far_ref[...]))
    far_ref[...] = far
    for j in range(count):
        intensity = None
        for m in range(modes):
            at = (j * modes + m) * width
            real, imag = far_ref[:width, at : at + width], far_ref[width:, at : at + width]
            power = real * real + imag * imag
            intensity = power if intensity is None else intensity + power
        factor = 1.0 - measured_ref[j] / jnp.sqrt(jnp.maximum(intensity, FLOOR_LEVEL))
        for m in range(modes):
            at = (j * modes + m) * width
            far_ref[:width, at : at + width] *= factor
            far_ref[width:, at : at + width] *= factor
    half = product(forward, split(far_ref[...]))
    for w in range(count * modes):
        at = w * width
        wave_ref[at : at + width, :width] = half[:width, at : at + width]
        wave_ref[at : at + width, width:] = half[width:, at : at + width]
    wave_ref[...] = product(split(wave_ref[...]), backward)

    gradient_ref[...] = jnp.zeros(gradient_ref.shape, F32)
    probe_grad = [[None] * modes, [None] * modes]
    descan_grad = [None] * 6
    centred_rows = along_rows(centred)
    for j in range(count):
        lit_real, lit_imag = lits[j]
        ramp_real, ramp_imag = ramps[j]
        sum_real = sum_imag = None
        for m in range(modes):
            p_real = probe_real[m * width : (m + 1) * width]
            p_imag = probe_imag[m * width : (m + 1) * width]
            at = (j * modes + m) * width
            real, imag = wave_ref[at : at + width, :width], wave_ref[at : at + width, width:]
            q_real = lit_real * real + lit_imag * imag
            q_imag = lit_real * imag - lit_imag * real
            probe_grad[0][m] = q_real if j == 0 else probe_grad[0][m] + q_real
            probe_grad[1][m] = q_imag if j == 0 else probe_grad[1][m] + q_imag
            h_real = p_real * real + p_imag * imag
            h_imag = p_real * imag - p_imag * real
            sum_real = h_real if m == 0 else sum_real + h_real
            sum_imag = h_imag if m == 0 else sum_imag + h_imag
        twist = lit_imag * sum_real - lit_real * sum_imag
        totals = (
            jnp.sum(jnp.sum(twist * centred_rows, axis=0, keepdims=True), axis=1, keepdims=True),
            jnp.sum(jnp.sum(twist, axis=0, keepdims=True) * centred, axis=1, keepdims=True),
        )
        frac_row, frac_col = fractions[j]
        for k in range(2):
            base = jnp.broadcast_to(-4 * math.pi * totals[k], (1, width))
            for n, term in enumerate((base, base * frac_row, base * frac_col)):
                descan_grad[3 * k + n] = term if j == 0 else descan_grad[3 * k + n] + term
        row_start, row_shift, lane = window_place(starts, j, tile_rows, tile_cols, width, fast, slow)
        row_start = pl.multiple_of(row_start, 8)
        parts = (
            ramp_real * sum_real + ramp_imag * sum_imag,
            ramp_real * sum_imag - ramp_imag * sum_real,
        )
        for part in range(2):
            value = jnp.concatenate([parts[part], jnp.zeros((8, width), F32)], axis=0)
            value = pltpu.roll(value, row_shift, 0)
            value = jnp.concatenate([value, jnp.zeros((high, ext_cols - width), F32)], axis=1)
            gradient_ref[part, pl.ds(row_start, high), :] += pltpu.roll(value, lane, 1)
    return probe_grad, descan_grad


def pick(parity, when_even, when_odd):
    return jnp.where(parity == 0, when_even, when_odd)


def both_sides(parity, even_ref, odd_ref, index=Ellipsis):
    even = even_ref[index]
    odd = jnp.zeros_like(even) if odd_ref is None else odd_ref[index]
    return pick(parity, even, odd), pick(parity, odd, even)


def put_sums(probe_grad, descan_grad, keep_ref, send_ref, core, width, modes):
    for m in range(modes):
        real, imag = probe_grad[0][m], probe_grad[1][m]
        keep_ref[m * width : (m + 1) * width] = jnp.where(core == 0, real, imag)
        send_ref[m * width : (m + 1) * width] = jnp.where(core == 0, imag, real)
    block = jnp.concatenate(descan_grad + [jnp.zeros((EXTRA - 6, width), F32)], axis=0)
    keep_ref[modes * width :] = block
    send_ref[modes * width :] = block


def put_quarters(probe_grad, descan_grad, mine_ref, beside_ref, send_ref, core, slow, width, modes):
    rows = modes * width
    real, imag = jnp.concatenate(probe_grad[0], axis=0), jnp.concatenate(probe_grad[1], axis=0)
    keep, send = pick(core, real, imag), pick(core, imag, real)
    half = rows // 2
    block = jnp.concatenate(descan_grad + [jnp.zeros((EXTRA - 6, width), F32)], axis=0)
    low, high = keep[:half], keep[half:]
    mine_ref[:half] = pick(slow, low, high)
    mine_ref[half:] = block
    beside_ref[:half] = pick(slow, high, low)
    beside_ref[half:] = block
    low, high = send[:half], send[half:]
    send_ref[0, :half] = pick(slow, low, high)
    send_ref[0, half:] = block
    send_ref[1, :half] = pick(slow, high, low)
    send_ref[1, half:] = block


def of_halves(halves, core, slow, rows):
    mine, other = halves[0][:rows], halves[1][...]
    return pick(core, mine, other), pick(core, other, mine)


def of_quarters(quarters, core, slow, rows):
    part = rows // 2
    values = [quarters[0][:part], quarters[1][...], quarters[2][:part], quarters[2][part:]]
    sums = []
    for own, beside in (
        (pick(core, values[0], values[2]), pick(core, values[1], values[3])),
        (pick(core, values[2], values[0]), pick(core, values[3], values[1])),
    ):
        sums.append(jnp.concatenate([pick(slow, own, beside), pick(slow, beside, own)], axis=0))
    return sums


def updated_probe(probe_ref, sums, total, width, modes):
    rows = modes * width
    real = probe_ref[0].reshape(rows, width) - PROBE_STEP / total * sums[0]
    imag = probe_ref[1].reshape(rows, width) - PROBE_STEP / total * sums[1]
    power = jnp.sum(jnp.sum(real * real + imag * imag, axis=0, keepdims=True), axis=1, keepdims=True)
    scale = jnp.sqrt(PROBE_POWER * rows * width / power)
    return real * scale, imag * scale


def halo_blocks(right, left, width):
    rim = width // 2
    low = lane_of(right.shape) < rim
    return jnp.where(low, right, pltpu.roll(left, rim, 1)), jnp.where(low, pltpu.roll(right, rim, 1), left)


def pack_kernel(sizes, object_ref, extended_ref, rows_even_ref, rows_odd_ref, *rest):
    tile_rows, tile_cols, width, modes, count, n_fast, n_slow = sizes
    rim = width // 2
    *rest, semaphore = rest
    inner = extended_ref.at[:, rim : rim + tile_rows, :tile_cols]
    copy = pltpu.make_async_copy(object_ref, inner, semaphore)
    copy.start()
    copy.wait()
    fast, slow = lax.rem(lax.axis_index("fast"), 2), lax.rem(lax.axis_index("slow"), 2)
    initial, final = extended_ref[:, rim:width, :tile_cols], extended_ref[:, tile_rows : rim + tile_rows, :tile_cols]
    rows_even_ref[...] = pick(fast, final, initial)
    rows_odd_ref[...] = pick(fast, initial, final)
    low = lane_of((tile_rows, width)) < rim
    end = extended_ref[:, rim : rim + tile_rows, tile_cols - width : tile_cols]
    start = extended_ref[:, rim : rim + tile_rows, :width]
    to_right = jnp.where(low, pltpu.roll(end[0], rim, 1), end[1])
    to_left = jnp.where(low, start[0], pltpu.roll(start[1], rim, 1))
    strips = (pick(slow, to_right, to_left), pick(slow, to_left, to_right))
    for k in range(len(rest) // 3):
        strip = strips[k]
        rest[3 * k][...] = strip
        rest[3 * k + 1][...] = pick(fast, strip[tile_rows - rim :], strip[:rim])
        rest[3 * k + 2][...] = pick(fast, strip[:rim], strip[tile_rows - rim :])


def first_kernel(
    sizes, starts, descan_ref, extended_in_ref, probe_ref, measured_ref, tables_ref,
    rows_even_ref, rows_odd_ref, halos,
    extended_ref, gradient_ref, strips, keep_ref, send_ref, wave_ref, far_ref,
):
    tile_rows, tile_cols, width, modes, count, n_fast, n_slow = sizes
    fast, slow = lax.axis_index("fast"), lax.axis_index("slow")
    core = lax.rem(fast, 2)
    rim = width // 2
    below, above = both_sides(core, rows_even_ref, rows_odd_ref)
    extended_ref[:, :rim, :tile_cols] = above
    extended_ref[:, rim + tile_rows :, :tile_cols] = below
    columns = []
    for middle_ref, even_ref, odd_ref in halos:
        after, before = both_sides(core, even_ref, odd_ref)
        columns.append(((0, before), (rim, middle_ref[...]), (rim + tile_rows, after)))
    for piece in range(3):
        at, even = columns[0][piece]
        odd = columns[-1][piece][1]
        real, imag = halo_blocks(pick(lax.rem(slow, 2), even, odd), pick(lax.rem(slow, 2), odd, even), width)
        extended_ref[0, at : at + even.shape[0], tile_cols:] = real
        extended_ref[1, at : at + even.shape[0], tile_cols:] = imag
    descan_rows = [jnp.broadcast_to(descan_ref[k // 3 : k // 3 + 1, k % 3 : k % 3 + 1], (1, width)) for k in range(6)]
    probe = tuple(probe_ref[part].reshape(modes * width, width) for part in range(2))
    probe_grad, descan_grad = gradients(
        extended_ref, probe, descan_rows, starts, measured_ref, tables_ref, gradient_ref, wave_ref, far_ref,
        sizes + (fast, slow),
    )
    put_sums(probe_grad, descan_grad, keep_ref, send_ref, core, width, modes)
    halo = gradient_ref[:, :, tile_cols:]
    low = lane_of(halo.shape) < rim
    to_right = jnp.where(low, halo, gradient_ref[:, :, tile_cols - width : tile_cols])
    to_left = jnp.where(low, gradient_ref[:, :, :width], halo)
    put_strips(slow, to_right, to_left, strips)


def put_strips(place, to_next, to_previous, refs):
    parity = lax.rem(place, 2)
    refs[0][...] = pick(parity, to_next, to_previous)
    if len(refs) > 1:
        refs[1][...] = pick(parity, to_previous, to_next)


def add_columns(gradient, right, left, tile_cols, width):
    rim = width // 2
    low = lane_of(right.shape) < rim
    zero = jnp.zeros(right.shape, F32)
    blocks = [gradient[:, :, k : k + width] for k in range(0, tile_cols + width, width)]
    blocks[0] = blocks[0] + jnp.where(low, left, zero)
    blocks[-2] = blocks[-2] + jnp.where(low, zero, right)
    blocks[-1] = blocks[-1] + jnp.where(low, right, left)
    return jnp.concatenate(blocks, axis=2)


def toward_next(odd):
    return lax.rem(lax.axis_index("fast"), 2) == (1 if odd else 0)


def packed_halo(halo):
    rim = halo.shape[-1] // 2
    low = lane_of(halo.shape[1:]) < rim
    return jnp.where(low, halo[0], pltpu.roll(halo[1], rim, 1)), jnp.where(low, pltpu.roll(halo[0], rim, 1), halo[1])


def rows_shape(sizes):
    tile_rows, tile_cols, width, modes, count, n_fast, n_slow = sizes
    return (width, 2 * tile_cols + width) if n_slow == 2 else (2, width, tile_cols + width)


def rows_of(sizes, value):
    tile_rows, tile_cols, width, modes, count, n_fast, n_slow = sizes
    if n_slow > 2:
        return value[0], value[1]
    real, imag = halo_blocks(value[:, 2 * tile_cols :], value[:, 2 * tile_cols :], width)
    return (
        jnp.concatenate([value[:, :tile_cols], real], axis=1),
        jnp.concatenate([value[:, tile_cols : 2 * tile_cols], imag], axis=1),
    )


def rows_kernel(sizes, odd, gradient_ref, columns, token_ref, out_ref):
    tile_rows, tile_cols, width, modes, count, n_fast, n_slow = sizes
    slow = lax.rem(lax.axis_index("slow"), 2)
    at = pl.multiple_of(jnp.where(toward_next(odd), tile_rows, 0), 8)
    index = (slice(None), pl.ds(at, width))
    right, left = both_sides(slow, *columns, index)
    value = add_columns(gradient_ref[index], right, left, tile_cols, width)
    if n_slow > 2:
        out_ref[...] = value
        return
    out_ref[:, :tile_cols] = value[0, :, :tile_cols]
    out_ref[:, tile_cols : 2 * tile_cols] = value[1, :, :tile_cols]
    out_ref[:, 2 * tile_cols :] = pick(slow, *packed_halo(value[:, :, tile_cols:]))


def second_kernel(
    sizes, total, starts, descan_ref, extended_ref, gradient_in_ref, probe_ref, measured_ref, tables_ref,
    columns, rows_even_ref, rows_odd_ref, mine_ref, other_ref,
    base_ref, up_ref, down_ref, strips, own_ref, beside_ref, send_ref, probe_out_ref, descan_out_ref,
    object_ref, gradient_ref, wave_ref, far_ref,
):
    tile_rows, tile_cols, width, modes, count, n_fast, n_slow = sizes
    fast, slow = lax.axis_index("fast"), lax.axis_index("slow")
    core = lax.rem(fast, 2)
    rim = width // 2
    right, left = both_sides(lax.rem(slow, 2), *columns)
    object_ref[...] = extended_ref[...] - OBJECT_STEP * add_columns(
        gradient_in_ref[...], right, left, tile_cols, width
    )
    below, above = both_sides(core, rows_even_ref, rows_odd_ref)
    above, below = rows_of(sizes, above), rows_of(sizes, below)
    for part in range(2):
        object_ref[part, :width] -= OBJECT_STEP * above[part]
        object_ref[part, tile_rows:] -= OBJECT_STEP * below[part]
    sums = of_halves((mine_ref, other_ref), core, slow, modes * width)
    probe = updated_probe(probe_ref, sums, total, width, modes)
    probe_out_ref[0] = probe[0].reshape(modes, width, width)
    probe_out_ref[1] = probe[1].reshape(modes, width, width)
    at = modes * width
    descan_rows = [
        descan_ref[k // 3 : k // 3 + 1, k % 3 : k % 3 + 1] - DESCAN_STEP / total * mine_ref[at + k : at + k + 1]
        for k in range(6)
    ]
    descan_out_ref[...] = jnp.concatenate(descan_rows + [jnp.zeros((EXTRA - 6, width), F32)], axis=0)
    probe_grad, descan_grad = gradients(
        object_ref, probe, descan_rows, starts, measured_ref, tables_ref, gradient_ref, wave_ref, far_ref,
        sizes + (fast, slow),
    )
    put_quarters(probe_grad, descan_grad, own_ref, beside_ref, send_ref, core, lax.rem(slow, 2), width, modes)
    base_ref[...] = (
        object_ref[:, rim : rim + tile_rows, :tile_cols]
        - OBJECT_STEP * gradient_ref[:, rim : rim + tile_rows, :tile_cols]
    )
    up_ref[...] = gradient_ref[:, :rim, :tile_cols]
    down_ref[...] = gradient_ref[:, rim + tile_rows :, :tile_cols]
    real, imag = gradient_ref[0, :, tile_cols:], gradient_ref[1, :, tile_cols:]
    low = lane_of(real.shape) < rim
    to_right = jnp.where(low, real, pltpu.roll(imag, rim, 1))
    to_left = jnp.where(low, pltpu.roll(real, rim, 1), imag)
    put_strips(slow, to_right, to_left, strips)


def edge_blocks(slow, columns, rows, width):
    rim = width // 2
    right, left = both_sides(lax.rem(slow, 2), *columns, rows)
    low = lane_of(right.shape) < rim
    zero = jnp.zeros(right.shape, F32)
    first = (jnp.where(low, left, zero), jnp.where(low, pltpu.roll(left, rim, 1), zero))
    last = (jnp.where(low, zero, pltpu.roll(right, rim, 1)), jnp.where(low, zero, right))
    return first, last


def last_rows_kernel(sizes, odd, up_ref, down_ref, columns, mine_ref, *rest):
    tile_rows, tile_cols, width, modes, count, n_fast, n_slow = sizes
    rim = width // 2
    out_ref = rest[-1]
    if odd:
        arrived_ref, sum_ref, out_ref = rest
        sum_ref[...] = mine_ref[...] + arrived_ref[...]
    following = toward_next(odd)
    at = pl.multiple_of(jnp.where(following, rim + tile_rows, 0), 8)
    out_ref[...] = jnp.where(following, down_ref[...], up_ref[...])
    first, last = edge_blocks(lax.axis_index("slow"), columns, pl.ds(at, rim), width)
    for part in range(2):
        out_ref[part, :, :width] += first[part]
        out_ref[part, :, tile_cols - width :] += last[part]


def join_kernel(own_ref, beside_ref, *rest):
    rows = own_ref.shape[0]
    rest[-1][:rows] = own_ref[...]
    rest[-1][rows:] = beside_ref[...]


def object_kernel(sizes, base_ref, columns, rows_even_ref, rows_odd_ref, out_ref):
    tile_rows, tile_cols, width, modes, count, n_fast, n_slow = sizes
    rim = width // 2
    out_ref[...] = base_ref[...]
    first, last = edge_blocks(lax.axis_index("slow"), columns, slice(rim, rim + tile_rows), width)
    for part in range(2):
        out_ref[part, :, :width] -= OBJECT_STEP * first[part]
        out_ref[part, :, tile_cols - width :] -= OBJECT_STEP * last[part]
    below, above = both_sides(lax.rem(lax.axis_index("fast"), 2), rows_even_ref, rows_odd_ref)
    out_ref[:, :rim] -= OBJECT_STEP * above
    out_ref[:, tile_rows - rim :] -= OBJECT_STEP * below


def probe_kernel(sizes, total, probe_ref, descan_ref, quarters, probe_out_ref, descan_out_ref):
    tile_rows, tile_cols, width, modes, count, n_fast, n_slow = sizes
    core, slow = lax.rem(lax.axis_index("fast"), 2), lax.rem(lax.axis_index("slow"), 2)
    sums = of_quarters(quarters, core, slow, modes * width)
    real, imag = updated_probe(probe_ref, sums, total, width, modes)
    probe_out_ref[0] = real.reshape(modes, width, width)
    probe_out_ref[1] = imag.reshape(modes, width, width)
    at = modes * width // 2
    rows = descan_ref[...] - DESCAN_STEP / total * quarters[0][at : at + EXTRA]
    lane = lane_of((1, width))
    for k in range(2):
        values = [rows[3 * k + n : 3 * k + n + 1] for n in range(3)]
        row = jnp.where(lane == 0, values[0], jnp.where(lane == 1, values[1], values[2]))
        descan_out_ref[k : k + 1, :] = row[:, :3]


def call(kernel, outs, scratch, *operands, smem=0, hbm=False, semaphores=(), aliases=None, work=0):
    return pl.pallas_call(
        kernel,
        out_shape=[out if isinstance(out, jax.ShapeDtypeStruct) else jax.ShapeDtypeStruct(out, F32) for out in outs],
        in_specs=[SMEM] * smem + [HBM if hbm else VMEM] * (len(operands) - smem),
        out_specs=[VMEM] * len(outs),
        scratch_shapes=[pltpu.VMEM(shape, F32) for shape in scratch]
        + [pltpu.SemaphoreType.DMA(shape) for shape in semaphores],
        input_output_aliases=aliases or {},
        compiler_params=pltpu.CompilerParams(vmem_limit_bytes=LIMIT),
        cost_estimate=pl.CostEstimate(flops=work, bytes_accessed=work // 100, transcendentals=0) if work else None,
    )(*operands)


def on_device(object_field, probe_modes, descan, scan_positions, amplitudes):
    width = amplitudes.shape[-1]
    rim = width // 2
    modes = probe_modes.shape[1]
    count = scan_positions.shape[1]
    tile_rows, tile_cols = object_field.shape[1:]
    n_fast, n_slow = lax.axis_size("fast"), lax.axis_size("slow")
    total = count * n_fast * n_slow
    sizes = (tile_rows, tile_cols, width, modes, count, n_fast, n_slow)
    fast, slow = lax.axis_index("fast"), lax.axis_index("slow")
    starts = scan_positions.transpose(0, 2, 1)
    tables = transform_tables(width)
    ext_rows, ext_cols = tile_rows + width, tile_cols + width
    half_rows = modes * width
    swaps = 1 if n_slow == 2 else 2

    def partner(place, odd, length):
        other = place ^ 1 if not odd else ((place + 1) ^ 1) - 1
        return other if 0 <= other < length else None

    def exchanged(value, fast_swap=None, slow_swap=None):
        pairs = []
        for f in range(n_fast):
            for s in range(n_slow):
                to_fast = f if fast_swap is None else partner(f, fast_swap, n_fast)
                to_slow = s if slow_swap is None else partner(s, slow_swap, n_slow)
                if to_fast is not None and to_slow is not None:
                    pairs.append((f * n_slow + s, to_fast * n_slow + to_slow))
        return lax.ppermute(value, AXES, pairs)

    def swapped(value, axis, bit):
        return lax.ppermute(value, axis, [(i, i ^ bit) for i in range(lax.axis_size(axis))])

    assert n_fast >= 4 and n_slow >= 2 and not n_fast % 2 and not n_slow % 2
    regular = not (n_fast & (n_fast - 1) or n_slow & (n_slow - 1))
    fast_bits = [1 << k for k in range(1, n_fast.bit_length() - 1)]
    slow_bits = [1 << k for k in range(n_slow.bit_length() - 1)]

    def sum_begun(keep, send):
        mine = keep + swapped(send, "fast", 1)
        if regular:
            for bit in fast_bits[:-1]:
                mine = mine + swapped(mine, "fast", bit)
        return mine

    def fast_ended(mine):
        return mine + swapped(mine, "fast", fast_bits[-1]) if regular else mine

    def sum_ended(mine):
        if regular:
            for bit in slow_bits:
                mine = mine + swapped(mine, "slow", bit)
        else:
            core = lax.rem(fast, 2)
            every = lax.psum(jnp.where(jnp.arange(2)[:, None, None] == core, mine, 0.0), AXES) * 0.5
            mine = lax.dynamic_index_in_dim(every, core, keepdims=False)
        return mine, swapped(mine[:half_rows], "fast", 1)

    def pairwise(refs):
        return refs if swaps == 2 else (refs[0], None)

    extended, rows_even, rows_odd, *packed = call(
        functools.partial(pack_kernel, sizes),
        [(2, ext_rows, ext_cols)] + [(2, rim, tile_cols)] * 2
        + [(tile_rows, width), (rim, width), (rim, width)] * swaps, [],
        object_field, hbm=True, semaphores=[()], work=WORK,
    )
    halos = []
    rows_odd = exchanged(rows_odd, 1)
    for k in range(swaps):
        corner_odd = exchanged(packed[3 * k + 2], 1, k)
        middle = exchanged(packed[3 * k], None, k)
        halos += [middle, exchanged(packed[3 * k + 1], 0, k), corner_odd]
    rows_even = exchanged(rows_even, 0)
    def first(starts_ref, descan_ref, extended_ref, probe_ref, measured_ref, tables_ref, *rest):
        halo_refs = [rest[2 + 3 * k : 5 + 3 * k] for k in range(swaps)]
        extended_out_ref, gradient_ref, *rest_out = rest[2 + 3 * swaps :]
        first_kernel(sizes, starts_ref, descan_ref, extended_ref, probe_ref, measured_ref, tables_ref,
                     *rest[:2], halo_refs, extended_out_ref, gradient_ref, rest_out[:swaps], *rest_out[swaps:])

    scratch = [(count * modes * width, 2 * width), (2 * width, count * modes * width)]
    sums = [(half_rows + EXTRA, width)] * 2
    extended, gradient, *strips, keep, send = call(
        first,
        [(2, ext_rows, ext_cols)] * 2 + [(2, ext_rows, width)] * swaps + sums,
        scratch,
        starts, descan, extended, probe_modes, amplitudes, tables, rows_even, rows_odd, *halos,
        smem=1, aliases={2: 0},
    )
    columns = [exchanged(strip, None, k) for k, strip in enumerate(strips)]
    mine = sum_begun(keep, send)

    def rows(odd, gradient_ref, *rest):
        rows_kernel(sizes, odd, gradient_ref, pairwise(rest[:swaps]), *rest[swaps:])

    def rows_for(odd, token):
        return call(functools.partial(rows, odd), [rows_shape(sizes)], [], gradient, *columns, token)[0]

    rows_odd = exchanged(rows_for(True, mine), 1)
    rows_even = exchanged(rows_for(False, mine), 0)
    mine = fast_ended(mine)
    mine, other = sum_ended(mine)

    def second(starts_ref, descan_ref, extended_ref, gradient_ref, probe_ref, measured_ref, tables_ref, *rest):
        base_ref, up_ref, down_ref, *rest_out = rest[swaps + 4 :]
        second_kernel(sizes, total, starts_ref, descan_ref, extended_ref, gradient_ref, probe_ref,
                      measured_ref, tables_ref, pairwise(rest[:swaps]), *rest[swaps : swaps + 4],
                      base_ref, up_ref, down_ref, rest_out[:swaps], *rest_out[swaps:])

    part = (half_rows // 2 + EXTRA, width)
    base, up, down, *strips, mine, beside, send, probes, descan_rows = call(
        second,
        [(2, tile_rows, tile_cols)] + [(2, rim, tile_cols)] * 2 + [(ext_rows, width)] * swaps + [part, part, (2, *part)]
        + [probe_modes.shape, (EXTRA, width)],
        [(2, ext_rows, ext_cols)] * 2 + scratch,
        starts, descan, extended, gradient, probe_modes, amplitudes, tables,
        *columns, rows_even, rows_odd, mine, other,
        smem=1,
    )
    columns = [exchanged(strip, None, k) for k, strip in enumerate(strips)]
    core_part = swapped(send, "fast", 1)
    mine = mine + core_part[0] + swapped(beside + core_part[1], "slow", 1)
    steps = [("fast", bit) for bit in fast_bits] + [("slow", bit) for bit in slow_bits[1:]]

    def last_rows(odd, up_ref, down_ref, *rest):
        last_rows_kernel(sizes, odd, up_ref, down_ref, pairwise(rest[:swaps]), *rest[swaps:])

    arrived = swapped(mine, *steps[0]) if regular else jnp.zeros_like(mine)
    mine, rows_odd = call(
        functools.partial(last_rows, True), [part, (2, rim, tile_cols)], [], up, down, *columns, mine, arrived,
    )
    rows_odd = exchanged(rows_odd, 1)
    if regular:
        for step in steps[1:]:
            mine = mine + swapped(mine, *step)
    else:
        place = 2 * lax.rem(fast, 2) + lax.rem(slow, 2)
        every = lax.psum(jnp.where(jnp.arange(4)[:, None, None] == place, mine, 0.0), AXES)
        mine = lax.dynamic_index_in_dim(every, place, keepdims=False)
    (rows_even,) = call(
        functools.partial(last_rows, False), [(2, rim, tile_cols)], [], up, down, *columns, mine,
    )
    rows_even = exchanged(rows_even, 0)
    own = mine[: half_rows // 2]
    beside = swapped(own, "slow", 1)
    (both,) = call(join_kernel, [(half_rows, width)], [], own, beside, rows_even, rows_odd)
    other = swapped(both, "fast", 1)

    def objects_of(base_ref, *rest):
        object_kernel(sizes, base_ref, pairwise(rest[:swaps]), *rest[swaps:])

    (objects,) = call(
        objects_of, [(2, tile_rows, tile_cols)], [], base, *columns, rows_even, rows_odd,
    )

    def probe_of(probe_ref, descan_ref, q0, q1, q2, *outs):
        probe_kernel(sizes, total, probe_ref, descan_ref, (q0, q1, q2), *outs)

    probes, descan_out = call(
        probe_of, [probe_modes.shape, descan.shape], [],
        probes, descan_rows, mine, beside, other,
    )
    return objects, probes, descan_out


def solution(mesh):
    placed = (P(None, "fast", "slow"), P(), P(), P(None, "fast", "slow"), P("fast", "slow", None))
    return jax.shard_map(
        on_device,
        mesh=mesh,
        in_specs=placed,
        out_specs=(P(None, "fast", "slow"), P(), P()),
        check_vma=False,
    )
```

```python
import functools
import math

import jax
import jax.numpy as jnp
import numpy as np
from jax import lax
from jax.experimental import pallas as pl
from jax.experimental.pallas import tpu as pltpu
from jax.sharding import PartitionSpec as P

OBJECT_STEP = 0.1
PROBE_STEP = 8.0
DESCAN_STEP = 0.02
FLOOR_LEVEL = 0.25
PROBE_POWER = 0.5
EXTRA = 8
AXES = ("fast", "slow")
F32 = jnp.float32
BF16 = jnp.bfloat16
VMEM = pl.BlockSpec(memory_space=pltpu.VMEM)
SMEM = pl.BlockSpec(memory_space=pltpu.SMEM)
HBM = pl.BlockSpec(memory_space=pltpu.HBM)
LIMIT = 40 * 1024 * 1024
WORK = 2_000_000_000


def transform_tables(width):
    counter = np.arange(width)
    angles = 2.0 * np.pi / width * (counter[:, None] * counter[None, :] % width)
    real = np.cos(angles) / math.sqrt(width)
    imag = -np.sin(angles) / math.sqrt(width)
    forward = np.block([[real, imag], [-imag, real]])
    backward = np.block([[real, -imag], [imag, real]])
    parts = []
    for table in (forward, backward):
        for _ in range(3):
            parts.append(table.astype(BF16))
            table = table - parts[-1].astype(np.float64)
    return jnp.asarray(np.stack(parts))


def split(value):
    high = value.astype(BF16)
    value = value - high.astype(F32)
    middle = value.astype(BF16)
    return high, middle, (value - middle.astype(F32)).astype(BF16)


def dot(a, b):
    return jnp.dot(a, b, preferred_element_type=F32)


def product(left, right):
    (a, b, c), (d, e, f) = left, right
    return dot(a, d) + (dot(a, e) + dot(b, d) + (dot(b, e) + dot(a, f) + dot(c, d)))


def lane_of(shape):
    return lax.broadcasted_iota(jnp.int32, shape, len(shape) - 1)


def window_place(starts, j, tile_rows, tile_cols, width, fast, slow):
    rim = width // 2
    row = starts[0, 0, j] - fast * tile_rows + rim
    col = starts[1, 0, j] - slow * tile_cols
    lane = jnp.where(col < 0, col + tile_cols + width, col)
    block = jnp.minimum(row // 8, (tile_rows + width - width - 8) // 8)
    return block * 8, row - block * 8, lane


def gradients(
    object_ref, probe, descan_rows, starts, measured_ref, tables_ref, gradient_ref, wave_ref, far_ref, sizes
):
    tile_rows, tile_cols, width, modes, count, n_fast, n_slow, fast, slow = sizes
    ext_cols = tile_cols + width
    high = width + 8
    probe_real, probe_imag = probe
    lane_row = lane_of((1, width)).astype(F32)
    centred = (lane_row - width // 2) / width
    tables = [tables_ref[k] for k in range(6)]
    forward, backward = tables[:3], tables[3:]

    fractions = []
    phases = []
    for j in range(count):
        frac_row = jnp.full((1, width), starts[0, 0, j], jnp.int32).astype(F32) / (tile_rows * n_fast)
        frac_col = jnp.full((1, width), starts[1, 0, j], jnp.int32).astype(F32) / (tile_cols * n_slow)
        fractions.append((frac_row, frac_col))
        for k in range(2):
            d = descan_rows[3 * k : 3 * k + 3]
            phases.append((2 * math.pi) * ((d[0] + d[1] * frac_row + d[2] * frac_col) * centred))
    while len(phases) % 8:
        phases.append(jnp.zeros((1, width), F32))
    phases = jnp.concatenate(phases, axis=0)
    cosines, sines = jnp.cos(phases), jnp.sin(phases)

    def along_rows(row):
        return jnp.transpose(jnp.broadcast_to(row, (width, width)))

    lits = []
    ramps = []
    for j in range(count):
        row_start, row_shift, lane = window_place(starts, j, tile_rows, tile_cols, width, fast, slow)
        row_start = pl.multiple_of(row_start, 8)
        row_cos, row_sin = along_rows(cosines[2 * j : 2 * j + 1]), along_rows(sines[2 * j : 2 * j + 1])
        col_cos, col_sin = cosines[2 * j + 1 : 2 * j + 2], sines[2 * j + 1 : 2 * j + 2]
        ramp_real = row_cos * col_cos - row_sin * col_sin
        ramp_imag = row_cos * col_sin + row_sin * col_cos
        patch = []
        for part in range(2):
            rows = object_ref[part, pl.ds(row_start, high), :]
            rows = pltpu.roll(rows, lax.rem(ext_cols - lane, ext_cols), 1)[:, :width]
            patch.append(pltpu.roll(rows, lax.rem(high - row_shift, high), 0)[:width])
        lit_real = patch[0] * ramp_real - patch[1] * ramp_imag
        lit_imag = patch[0] * ramp_imag + patch[1] * ramp_real
        lits.append((lit_real, lit_imag))
        ramps.append((ramp_real, ramp_imag))
        for m in range(modes):
            p_real = probe_real[m * width : (m + 1) * width]
            p_imag = probe_imag[m * width : (m + 1) * width]
            at = (j * modes + m) * width
            wave_ref[at : at + width, :width] = p_real * lit_real - p_imag * lit_imag
            wave_ref[at : at + width, width:] = p_real * lit_imag + p_imag * lit_real

    half = product(split(wave_ref[...]), forward)
    for w in range(count * modes):
        at = w * width
        far_ref[:width, at : at + width] = half[at : at + width, :width]
        far_ref[width:, at : at + width] = half[at : at + width, width:]
    far = product(backward, split(far_ref[...]))
    far_ref[...] = far
    for j in range(count):
        intensity = None
        for m in range(modes):
            at = (j * modes + m) * width
            real, imag = far_ref[:width, at : at + width], far_ref[width:, at : at + width]
            power = real * real + imag * imag
            intensity = power if intensity is None else intensity + power
        factor = 1.0 - measured_ref[j] / jnp.sqrt(jnp.maximum(intensity, FLOOR_LEVEL))
        for m in range(modes):
            at = (j * modes + m) * width
            far_ref[:width, at : at + width] *= factor
            far_ref[width:, at : at + width] *= factor
    half = product(forward, split(far_ref[...]))
    for w in range(count * modes):
        at = w * width
        wave_ref[at : at + width, :width] = half[:width, at : at + width]
        wave_ref[at : at + width, width:] = half[width:, at : at + width]
    wave_ref[...] = product(split(wave_ref[...]), backward)

    gradient_ref[...] = jnp.zeros(gradient_ref.shape, F32)
    probe_grad = [[None] * modes, [None] * modes]
    descan_grad = [None] * 6
    centred_rows = along_rows(centred)
    for j in range(count):
        lit_real, lit_imag = lits[j]
        ramp_real, ramp_imag = ramps[j]
        sum_real = sum_imag = None
        for m in range(modes):
            p_real = probe_real[m * width : (m + 1) * width]
            p_imag = probe_imag[m * width : (m + 1) * width]
            at = (j * modes + m) * width
            real, imag = wave_ref[at : at + width, :width], wave_ref[at : at + width, width:]
            q_real = lit_real * real + lit_imag * imag
            q_imag = lit_real * imag - lit_imag * real
            probe_grad[0][m] = q_real if j == 0 else probe_grad[0][m] + q_real
            probe_grad[1][m] = q_imag if j == 0 else probe_grad[1][m] + q_imag
            h_real = p_real * real + p_imag * imag
            h_imag = p_real * imag - p_imag * real
            sum_real = h_real if m == 0 else sum_real + h_real
            sum_imag = h_imag if m == 0 else sum_imag + h_imag
        twist = lit_imag * sum_real - lit_real * sum_imag
        totals = (
            jnp.sum(jnp.sum(twist * centred_rows, axis=0, keepdims=True), axis=1, keepdims=True),
            jnp.sum(jnp.sum(twist, axis=0, keepdims=True) * centred, axis=1, keepdims=True),
        )
        frac_row, frac_col = fractions[j]
        for k in range(2):
            base = jnp.broadcast_to(-4 * math.pi * totals[k], (1, width))
            for n, term in enumerate((base, base * frac_row, base * frac_col)):
                descan_grad[3 * k + n] = term if j == 0 else descan_grad[3 * k + n] + term
        row_start, row_shift, lane = window_place(starts, j, tile_rows, tile_cols, width, fast, slow)
        row_start = pl.multiple_of(row_start, 8)
        parts = (
            ramp_real * sum_real + ramp_imag * sum_imag,
            ramp_real * sum_imag - ramp_imag * sum_real,
        )
        for part in range(2):
            value = jnp.concatenate([parts[part], jnp.zeros((8, width), F32)], axis=0)
            value = pltpu.roll(value, row_shift, 0)
            value = jnp.concatenate([value, jnp.zeros((high, ext_cols - width), F32)], axis=1)
            gradient_ref[part, pl.ds(row_start, high), :] += pltpu.roll(value, lane, 1)
    return probe_grad, descan_grad


def pick(parity, when_even, when_odd):
    return jnp.where(parity == 0, when_even, when_odd)


def both_sides(parity, even_ref, odd_ref, index=Ellipsis):
    even = even_ref[index]
    odd = jnp.zeros_like(even) if odd_ref is None else odd_ref[index]
    return pick(parity, even, odd), pick(parity, odd, even)


def put_sums(probe_grad, descan_grad, keep_ref, send_ref, core, width, modes):
    for m in range(modes):
        real, imag = probe_grad[0][m], probe_grad[1][m]
        keep_ref[m * width : (m + 1) * width] = jnp.where(core == 0, real, imag)
        send_ref[m * width : (m + 1) * width] = jnp.where(core == 0, imag, real)
    block = jnp.concatenate(descan_grad + [jnp.zeros((EXTRA - 6, width), F32)], axis=0)
    keep_ref[modes * width :] = block
    send_ref[modes * width :] = block


def put_quarters(probe_grad, descan_grad, mine_ref, beside_ref, send_ref, core, slow, width, modes):
    rows = modes * width
    real, imag = jnp.concatenate(probe_grad[0], axis=0), jnp.concatenate(probe_grad[1], axis=0)
    keep, send = pick(core, real, imag), pick(core, imag, real)
    half = rows // 2
    block = jnp.concatenate(descan_grad + [jnp.zeros((EXTRA - 6, width), F32)], axis=0)
    low, high = keep[:half], keep[half:]
    mine_ref[:half] = pick(slow, low, high)
    mine_ref[half:] = block
    beside_ref[:half] = pick(slow, high, low)
    beside_ref[half:] = block
    low, high = send[:half], send[half:]
    send_ref[0, :half] = pick(slow, low, high)
    send_ref[0, half:] = block
    send_ref[1, :half] = pick(slow, high, low)
    send_ref[1, half:] = block


def of_halves(halves, core, slow, rows):
    mine, other = halves[0][:rows], halves[1][...]
    return pick(core, mine, other), pick(core, other, mine)


def of_quarters(quarters, core, slow, rows):
    part = rows // 2
    values = [quarters[0][:part], quarters[1][...], quarters[2][:part], quarters[2][part:]]
    sums = []
    for own, beside in (
        (pick(core, values[0], values[2]), pick(core, values[1], values[3])),
        (pick(core, values[2], values[0]), pick(core, values[3], values[1])),
    ):
        sums.append(jnp.concatenate([pick(slow, own, beside), pick(slow, beside, own)], axis=0))
    return sums


def updated_probe(probe_ref, sums, total, width, modes):
    rows = modes * width
    real = probe_ref[0].reshape(rows, width) - PROBE_STEP / total * sums[0]
    imag = probe_ref[1].reshape(rows, width) - PROBE_STEP / total * sums[1]
    power = jnp.sum(jnp.sum(real * real + imag * imag, axis=0, keepdims=True), axis=1, keepdims=True)
    scale = jnp.sqrt(PROBE_POWER * rows * width / power)
    return real * scale, imag * scale


def halo_blocks(right, left, width):
    rim = width // 2
    low = lane_of(right.shape) < rim
    return jnp.where(low, right, pltpu.roll(left, rim, 1)), jnp.where(low, pltpu.roll(right, rim, 1), left)


def pack_kernel(sizes, object_ref, extended_ref, rows_even_ref, rows_odd_ref, *rest):
    tile_rows, tile_cols, width, modes, count, n_fast, n_slow = sizes
    rim = width // 2
    extended_ref[:, rim : rim + tile_rows, :tile_cols] = object_ref[...]
    fast = lax.rem(lax.axis_index("fast"), 2)
    initial, final = object_ref[:, :rim], object_ref[:, tile_rows - rim :]
    rows_even_ref[...] = pick(fast, final, initial)
    rows_odd_ref[...] = pick(fast, initial, final)
    swaps = len(rest) // 3
    put_edges(sizes, object_ref[...], rest[::3])
    for k in range(swaps):
        first, last = rest[3 * k][:rim], rest[3 * k][tile_rows - rim :]
        rest[3 * k + 1][...] = pick(fast, last, first)
        rest[3 * k + 2][...] = pick(fast, first, last)


def put_edges(sizes, rows, refs):
    tile_rows, tile_cols, width, modes, count, n_fast, n_slow = sizes
    rim = width // 2
    end, start = rows[:, :, tile_cols - width :], rows[:, :, :width]
    low = lane_of(end.shape[1:]) < rim
    to_right = jnp.where(low, pltpu.roll(end[0], rim, 1), end[1])
    to_left = jnp.where(low, start[0], pltpu.roll(start[1], rim, 1))
    put_strips(lax.axis_index("slow"), to_right, to_left, refs)


def first_kernel(
    sizes, starts, descan_ref, extended_in_ref, probe_ref, measured_ref, tables_ref,
    rows_even_ref, rows_odd_ref, halos,
    extended_ref, gradient_ref, strips, keep_ref, send_ref, wave_ref, far_ref,
):
    tile_rows, tile_cols, width, modes, count, n_fast, n_slow = sizes
    fast, slow = lax.axis_index("fast"), lax.axis_index("slow")
    core = lax.rem(fast, 2)
    rim = width // 2
    below, above = both_sides(core, rows_even_ref, rows_odd_ref)
    extended_ref[:, :rim, :tile_cols] = above
    extended_ref[:, rim + tile_rows :, :tile_cols] = below
    columns = []
    for middle_ref, even_ref, odd_ref in halos:
        after, before = both_sides(core, even_ref, odd_ref)
        columns.append(((0, before), (rim, middle_ref[...]), (rim + tile_rows, after)))
    for piece in range(3):
        at, even = columns[0][piece]
        odd = columns[-1][piece][1]
        real, imag = halo_blocks(pick(lax.rem(slow, 2), even, odd), pick(lax.rem(slow, 2), odd, even), width)
        extended_ref[0, at : at + even.shape[0], tile_cols:] = real
        extended_ref[1, at : at + even.shape[0], tile_cols:] = imag
    descan_rows = [jnp.broadcast_to(descan_ref[k // 3 : k // 3 + 1, k % 3 : k % 3 + 1], (1, width)) for k in range(6)]
    probe = tuple(probe_ref[part].reshape(modes * width, width) for part in range(2))
    probe_grad, descan_grad = gradients(
        extended_ref, probe, descan_rows, starts, measured_ref, tables_ref, gradient_ref, wave_ref, far_ref,
        sizes + (fast, slow),
    )
    put_sums(probe_grad, descan_grad, keep_ref, send_ref, core, width, modes)
    halo = gradient_ref[:, :, tile_cols:]
    low = lane_of(halo.shape) < rim
    to_right = jnp.where(low, halo, gradient_ref[:, :, tile_cols - width : tile_cols])
    to_left = jnp.where(low, gradient_ref[:, :, :width], halo)
    put_strips(slow, to_right, to_left, strips)


def put_strips(place, to_next, to_previous, refs):
    parity = lax.rem(place, 2)
    refs[0][...] = pick(parity, to_next, to_previous)
    if len(refs) > 1:
        refs[1][...] = pick(parity, to_previous, to_next)


def add_columns(gradient, right, left, tile_cols, width):
    rim = width // 2
    low = lane_of(right.shape) < rim
    zero = jnp.zeros(right.shape, F32)
    blocks = [gradient[:, :, k : k + width] for k in range(0, tile_cols + width, width)]
    blocks[0] = blocks[0] + jnp.where(low, left, zero)
    blocks[-2] = blocks[-2] + jnp.where(low, zero, right)
    blocks[-1] = blocks[-1] + jnp.where(low, right, left)
    return jnp.concatenate(blocks, axis=2)


def toward_next(odd):
    return lax.rem(lax.axis_index("fast"), 2) == (1 if odd else 0)


def packed_halo(halo):
    rim = halo.shape[-1] // 2
    low = lane_of(halo.shape[1:]) < rim
    return jnp.where(low, halo[0], pltpu.roll(halo[1], rim, 1)), jnp.where(low, pltpu.roll(halo[0], rim, 1), halo[1])


def rows_shape(sizes):
    tile_rows, tile_cols, width, modes, count, n_fast, n_slow = sizes
    return (width, 2 * tile_cols + width) if n_slow == 2 else (2, width, tile_cols + width)


def rows_of(sizes, value):
    tile_rows, tile_cols, width, modes, count, n_fast, n_slow = sizes
    if n_slow > 2:
        return value[0], value[1]
    real, imag = halo_blocks(value[:, 2 * tile_cols :], value[:, 2 * tile_cols :], width)
    return (
        jnp.concatenate([value[:, :tile_cols], real], axis=1),
        jnp.concatenate([value[:, tile_cols : 2 * tile_cols], imag], axis=1),
    )


def rows_kernel(sizes, odd, gradient_ref, columns, token_ref, out_ref):
    tile_rows, tile_cols, width, modes, count, n_fast, n_slow = sizes
    slow = lax.rem(lax.axis_index("slow"), 2)
    at = pl.multiple_of(jnp.where(toward_next(odd), tile_rows, 0), 8)
    index = (slice(None), pl.ds(at, width))
    right, left = both_sides(slow, *columns, index)
    value = add_columns(gradient_ref[index], right, left, tile_cols, width)
    if n_slow > 2:
        out_ref[...] = value
        return
    out_ref[:, :tile_cols] = value[0, :, :tile_cols]
    out_ref[:, tile_cols : 2 * tile_cols] = value[1, :, :tile_cols]
    out_ref[:, 2 * tile_cols :] = pick(slow, *packed_halo(value[:, :, tile_cols:]))


def update_kernel(sizes, extended_ref, gradient_ref, columns, rows_even_ref, rows_odd_ref, object_ref):
    tile_rows, tile_cols, width, modes, count, n_fast, n_slow = sizes
    right, left = both_sides(lax.rem(lax.axis_index("slow"), 2), *columns)
    object_ref[...] = extended_ref[...] - OBJECT_STEP * add_columns(gradient_ref[...], right, left, tile_cols, width)
    below, above = both_sides(lax.rem(lax.axis_index("fast"), 2), rows_even_ref, rows_odd_ref)
    above, below = rows_of(sizes, above), rows_of(sizes, below)
    for part in range(2):
        object_ref[part, :width] -= OBJECT_STEP * above[part]
        object_ref[part, tile_rows:] -= OBJECT_STEP * below[part]


def second_kernel(
    sizes, total, starts, descan_ref, object_ref, probe_ref, measured_ref, tables_ref, mine_ref, other_ref,
    gradient_ref, strips, own_ref, beside_ref, send_ref, probe_out_ref, descan_out_ref, wave_ref, far_ref,
):
    tile_rows, tile_cols, width, modes, count, n_fast, n_slow = sizes
    fast, slow = lax.axis_index("fast"), lax.axis_index("slow")
    core = lax.rem(fast, 2)
    rim = width // 2
    sums = of_halves((mine_ref, other_ref), core, slow, modes * width)
    probe = updated_probe(probe_ref, sums, total, width, modes)
    probe_out_ref[0] = probe[0].reshape(modes, width, width)
    probe_out_ref[1] = probe[1].reshape(modes, width, width)
    at = modes * width
    descan_rows = [
        descan_ref[k // 3 : k // 3 + 1, k % 3 : k % 3 + 1] - DESCAN_STEP / total * mine_ref[at + k : at + k + 1]
        for k in range(6)
    ]
    descan_out_ref[...] = jnp.concatenate(descan_rows + [jnp.zeros((EXTRA - 6, width), F32)], axis=0)
    probe_grad, descan_grad = gradients(
        object_ref, probe, descan_rows, starts, measured_ref, tables_ref, gradient_ref, wave_ref, far_ref,
        sizes + (fast, slow),
    )
    put_quarters(probe_grad, descan_grad, own_ref, beside_ref, send_ref, core, lax.rem(slow, 2), width, modes)
    real, imag = gradient_ref[0, :, tile_cols:], gradient_ref[1, :, tile_cols:]
    low = lane_of(real.shape) < rim
    to_right = jnp.where(low, real, pltpu.roll(imag, rim, 1))
    to_left = jnp.where(low, pltpu.roll(real, rim, 1), imag)
    put_strips(slow, to_right, to_left, strips)


def edge_blocks(slow, columns, rows, width):
    rim = width // 2
    right, left = both_sides(lax.rem(slow, 2), *columns, rows)
    low = lane_of(right.shape) < rim
    zero = jnp.zeros(right.shape, F32)
    first = (jnp.where(low, left, zero), jnp.where(low, pltpu.roll(left, rim, 1), zero))
    last = (jnp.where(low, zero, pltpu.roll(right, rim, 1)), jnp.where(low, zero, right))
    return first, last


def last_rows_kernel(sizes, odd, gradient_ref, columns, mine_ref, *rest):
    tile_rows, tile_cols, width, modes, count, n_fast, n_slow = sizes
    rim = width // 2
    out_ref = rest[-1]
    if odd:
        arrived_ref, sum_ref, out_ref = rest
        sum_ref[...] = mine_ref[...] + arrived_ref[...]
    at = pl.multiple_of(jnp.where(toward_next(odd), rim + tile_rows, 0), 8)
    out_ref[...] = gradient_ref[:, pl.ds(at, rim), :tile_cols]
    first, last = edge_blocks(lax.axis_index("slow"), columns, pl.ds(at, rim), width)
    for part in range(2):
        out_ref[part, :, :width] += first[part]
        out_ref[part, :, tile_cols - width :] += last[part]


def join_kernel(own_ref, beside_ref, *rest):
    rows = own_ref.shape[0]
    rest[-1][:rows] = own_ref[...]
    rest[-1][rows:] = beside_ref[...]


def object_kernel(sizes, object_ref, gradient_ref, columns, rows_even_ref, rows_odd_ref, out_ref):
    tile_rows, tile_cols, width, modes, count, n_fast, n_slow = sizes
    rim = width // 2
    inner = (slice(None), slice(rim, rim + tile_rows), slice(0, tile_cols))
    out_ref[...] = object_ref[inner] - OBJECT_STEP * gradient_ref[inner]
    first, last = edge_blocks(lax.axis_index("slow"), columns, slice(rim, rim + tile_rows), width)
    for part in range(2):
        out_ref[part, :, :width] -= OBJECT_STEP * first[part]
        out_ref[part, :, tile_cols - width :] -= OBJECT_STEP * last[part]
    below, above = both_sides(lax.rem(lax.axis_index("fast"), 2), rows_even_ref, rows_odd_ref)
    out_ref[:, :rim] -= OBJECT_STEP * above
    out_ref[:, tile_rows - rim :] -= OBJECT_STEP * below


def probe_kernel(sizes, total, probe_ref, descan_ref, quarters, probe_out_ref, descan_out_ref):
    tile_rows, tile_cols, width, modes, count, n_fast, n_slow = sizes
    core, slow = lax.rem(lax.axis_index("fast"), 2), lax.rem(lax.axis_index("slow"), 2)
    sums = of_quarters(quarters, core, slow, modes * width)
    real, imag = updated_probe(probe_ref, sums, total, width, modes)
    probe_out_ref[0] = real.reshape(modes, width, width)
    probe_out_ref[1] = imag.reshape(modes, width, width)
    at = modes * width // 2
    rows = descan_ref[...] - DESCAN_STEP / total * quarters[0][at : at + EXTRA]
    lane = lane_of((1, width))
    for k in range(2):
        values = [rows[3 * k + n : 3 * k + n + 1] for n in range(3)]
        row = jnp.where(lane == 0, values[0], jnp.where(lane == 1, values[1], values[2]))
        descan_out_ref[k : k + 1, :] = row[:, :3]


def call(kernel, outs, scratch, *operands, smem=0, hbm=False, semaphores=(), aliases=None, work=0):
    return pl.pallas_call(
        kernel,
        out_shape=[out if isinstance(out, jax.ShapeDtypeStruct) else jax.ShapeDtypeStruct(out, F32) for out in outs],
        in_specs=[SMEM] * smem + [HBM if hbm else VMEM] * (len(operands) - smem),
        out_specs=[VMEM] * len(outs),
        scratch_shapes=[pltpu.VMEM(shape, F32) for shape in scratch]
        + [pltpu.SemaphoreType.DMA(shape) for shape in semaphores],
        input_output_aliases=aliases or {},
        compiler_params=pltpu.CompilerParams(vmem_limit_bytes=LIMIT),
        cost_estimate=pl.CostEstimate(flops=work, bytes_accessed=work // 100, transcendentals=0) if work else None,
    )(*operands)


def on_device(object_field, probe_modes, descan, scan_positions, amplitudes):
    width = amplitudes.shape[-1]
    rim = width // 2
    modes = probe_modes.shape[1]
    count = scan_positions.shape[1]
    tile_rows, tile_cols = object_field.shape[1:]
    n_fast, n_slow = lax.axis_size("fast"), lax.axis_size("slow")
    total = count * n_fast * n_slow
    sizes = (tile_rows, tile_cols, width, modes, count, n_fast, n_slow)
    fast, slow = lax.axis_index("fast"), lax.axis_index("slow")
    starts = scan_positions.transpose(0, 2, 1)
    tables = transform_tables(width)
    ext_rows, ext_cols = tile_rows + width, tile_cols + width
    half_rows = modes * width
    swaps = 1 if n_slow == 2 else 2

    def partner(place, odd, length):
        other = place ^ 1 if not odd else ((place + 1) ^ 1) - 1
        return other if 0 <= other < length else None

    def exchanged(value, fast_swap=None, slow_swap=None):
        pairs = []
        for f in range(n_fast):
            for s in range(n_slow):
                to_fast = f if fast_swap is None else partner(f, fast_swap, n_fast)
                to_slow = s if slow_swap is None else partner(s, slow_swap, n_slow)
                if to_fast is not None and to_slow is not None:
                    pairs.append((f * n_slow + s, to_fast * n_slow + to_slow))
        return lax.ppermute(value, AXES, pairs)

    def swapped(value, axis, bit):
        return lax.ppermute(value, axis, [(i, i ^ bit) for i in range(lax.axis_size(axis))])

    assert n_fast >= 4 and n_slow >= 2 and not n_fast % 2 and not n_slow % 2
    regular = not (n_fast & (n_fast - 1) or n_slow & (n_slow - 1))
    fast_bits = [1 << k for k in range(1, n_fast.bit_length() - 1)]
    slow_bits = [1 << k for k in range(n_slow.bit_length() - 1)]

    def sum_begun(keep, send):
        mine = keep + swapped(send, "fast", 1)
        if regular:
            for bit in fast_bits[:-1]:
                mine = mine + swapped(mine, "fast", bit)
        return mine

    def fast_ended(mine):
        return mine + swapped(mine, "fast", fast_bits[-1]) if regular else mine

    def sum_ended(mine):
        if regular:
            for bit in slow_bits:
                mine = mine + swapped(mine, "slow", bit)
        else:
            core = lax.rem(fast, 2)
            every = lax.psum(jnp.where(jnp.arange(2)[:, None, None] == core, mine, 0.0), AXES) * 0.5
            mine = lax.dynamic_index_in_dim(every, core, keepdims=False)
        return mine, swapped(mine[:half_rows], "fast", 1)

    def pairwise(refs):
        return refs if swaps == 2 else (refs[0], None)

    extended, rows_even, rows_odd, *packed = call(
        functools.partial(pack_kernel, sizes),
        [(2, ext_rows, ext_cols)] + [(2, rim, tile_cols)] * 2
        + [(tile_rows, width), (rim, width), (rim, width)] * swaps, [],
        object_field, work=WORK,
    )
    halos = []
    rows_odd = exchanged(rows_odd, 1)
    for k in range(swaps):
        corner_odd = exchanged(packed[3 * k + 2], 1, k)
        middle = exchanged(packed[3 * k], None, k)
        halos += [middle, exchanged(packed[3 * k + 1], 0, k), corner_odd]
    rows_even = exchanged(rows_even, 0)
    def first(starts_ref, descan_ref, extended_ref, probe_ref, measured_ref, tables_ref, *rest):
        halo_refs = [rest[2 + 3 * k : 5 + 3 * k] for k in range(swaps)]
        extended_out_ref, gradient_ref, *rest_out = rest[2 + 3 * swaps :]
        first_kernel(sizes, starts_ref, descan_ref, extended_ref, probe_ref, measured_ref, tables_ref,
                     *rest[:2], halo_refs, extended_out_ref, gradient_ref, rest_out[:swaps], *rest_out[swaps:])

    scratch = [(count * modes * width, 2 * width), (2 * width, count * modes * width)]
    sums = [(half_rows + EXTRA, width)] * 2
    extended, gradient, *strips, keep, send = call(
        first,
        [(2, ext_rows, ext_cols)] * 2 + [(2, ext_rows, width)] * swaps + sums,
        scratch,
        starts, descan, extended, probe_modes, amplitudes, tables, rows_even, rows_odd, *halos,
        smem=1, aliases={2: 0},
    )
    columns = [exchanged(strip, None, k) for k, strip in enumerate(strips)]
    mine = sum_begun(keep, send)

    def rows(odd, gradient_ref, *rest):
        rows_kernel(sizes, odd, gradient_ref, pairwise(rest[:swaps]), *rest[swaps:])

    def rows_for(odd, token):
        return call(functools.partial(rows, odd), [rows_shape(sizes)], [], gradient, *columns, token)[0]

    rows_odd = exchanged(rows_for(True, mine), 1)
    rows_even = exchanged(rows_for(False, mine), 0)
    mine = fast_ended(mine)
    mine, other = sum_ended(mine)

    def update(extended_ref, gradient_ref, *rest):
        update_kernel(sizes, extended_ref, gradient_ref, pairwise(rest[:swaps]), *rest[swaps:])

    (extended,) = call(
        update, [(2, ext_rows, ext_cols)], [], extended, gradient, *columns, rows_even, rows_odd, aliases={0: 0},
    )

    def second(starts_ref, descan_ref, object_ref, probe_ref, measured_ref, tables_ref, mine_ref, other_ref, *rest):
        gradient_ref, *rest_out = rest
        second_kernel(sizes, total, starts_ref, descan_ref, object_ref, probe_ref, measured_ref, tables_ref,
                      mine_ref, other_ref, gradient_ref, rest_out[:swaps], *rest_out[swaps:])

    part = (half_rows // 2 + EXTRA, width)
    gradient, *strips, mine, beside, send, probes, descan_rows = call(
        second,
        [(2, ext_rows, ext_cols)] + [(ext_rows, width)] * swaps + [part, part, (2, *part)]
        + [probe_modes.shape, (EXTRA, width)],
        scratch,
        starts, descan, extended, probe_modes, amplitudes, tables, mine, other,
        smem=1,
    )
    columns = [exchanged(strip, None, k) for k, strip in enumerate(strips)]
    core_part = swapped(send, "fast", 1)
    mine = mine + core_part[0] + swapped(beside + core_part[1], "slow", 1)
    steps = [("fast", bit) for bit in fast_bits] + [("slow", bit) for bit in slow_bits[1:]]

    def last_rows(odd, gradient_ref, *rest):
        last_rows_kernel(sizes, odd, gradient_ref, pairwise(rest[:swaps]), *rest[swaps:])

    arrived = swapped(mine, *steps[0]) if regular else jnp.zeros_like(mine)
    mine, rows_odd = call(
        functools.partial(last_rows, True), [part, (2, rim, tile_cols)], [], gradient, *columns, mine, arrived,
    )
    rows_odd = exchanged(rows_odd, 1)
    if regular:
        for step in steps[1:]:
            mine = mine + swapped(mine, *step)
    else:
        place = 2 * lax.rem(fast, 2) + lax.rem(slow, 2)
        every = lax.psum(jnp.where(jnp.arange(4)[:, None, None] == place, mine, 0.0), AXES)
        mine = lax.dynamic_index_in_dim(every, place, keepdims=False)
    (rows_even,) = call(
        functools.partial(last_rows, False), [(2, rim, tile_cols)], [], gradient, *columns, mine,
    )
    rows_even = exchanged(rows_even, 0)
    own = mine[: half_rows // 2]
    beside = swapped(own, "slow", 1)
    (both,) = call(join_kernel, [(half_rows, width)], [], own, beside, rows_even, rows_odd)
    other = swapped(both, "fast", 1)

    def objects_of(object_ref, gradient_ref, *rest):
        object_kernel(sizes, object_ref, gradient_ref, pairwise(rest[:swaps]), *rest[swaps:])

    (objects,) = call(
        objects_of, [(2, tile_rows, tile_cols)], [], extended, gradient, *columns, rows_even, rows_odd,
    )

    def probe_of(probe_ref, descan_ref, q0, q1, q2, *outs):
        probe_kernel(sizes, total, probe_ref, descan_ref, (q0, q1, q2), *outs)

    probes, descan_out = call(
        probe_of, [probe_modes.shape, descan.shape], [],
        probes, descan_rows, mine, beside, other,
    )
    return objects, probes, descan_out


def solution(mesh):
    placed = (P(None, "fast", "slow"), P(), P(), P(None, "fast", "slow"), P("fast", "slow", None))
    return jax.shard_map(
        on_device,
        mesh=mesh,
        in_specs=placed,
        out_specs=(P(None, "fast", "slow"), P(), P()),
        check_vma=False,
    )
```

```python
import functools
import math

import jax
import jax.numpy as jnp
import numpy as np
from jax import lax
from jax.experimental import pallas as pl
from jax.experimental.pallas import tpu as pltpu
from jax.sharding import PartitionSpec as P

OBJECT_STEP = 0.1
PROBE_STEP = 8.0
DESCAN_STEP = 0.02
FLOOR_LEVEL = 0.25
PROBE_POWER = 0.5
EXTRA = 8
FIRST, SECOND = 3, 2
AXES = ("fast", "slow")
F32 = jnp.float32
BF16 = jnp.bfloat16
VMEM = pl.BlockSpec(memory_space=pltpu.VMEM)
SMEM = pl.BlockSpec(memory_space=pltpu.SMEM)
HBM = pl.BlockSpec(memory_space=pltpu.HBM)
LIMIT = 40 * 1024 * 1024
WORK = 2_000_000_000


def transform_tables(width):
    counter = np.arange(width)
    angles = 2.0 * np.pi / width * (counter[:, None] * counter[None, :] % width)
    real = np.cos(angles) / math.sqrt(width)
    imag = -np.sin(angles) / math.sqrt(width)
    forward = np.block([[real, imag], [-imag, real]])
    backward = np.block([[real, -imag], [imag, real]])
    parts = []
    for table in (forward, backward):
        for _ in range(3):
            parts.append(table.astype(BF16))
            table = table - parts[-1].astype(np.float64)
    return jnp.asarray(np.stack(parts))


def split(value):
    high = value.astype(BF16)
    value = value - high.astype(F32)
    middle = value.astype(BF16)
    return high, middle, (value - middle.astype(F32)).astype(BF16)


def dot(a, b):
    return jnp.dot(a, b, preferred_element_type=F32)


def product(left, right):
    (a, b, *c), (d, e, *f) = left, right
    if not c or not f:
        return dot(a, d) + (dot(a, e) + dot(b, d))
    (c,), (f,) = c, f
    return dot(a, d) + (dot(a, e) + dot(b, d) + (dot(b, e) + dot(a, f) + dot(c, d)))


def lane_of(shape):
    return lax.broadcasted_iota(jnp.int32, shape, len(shape) - 1)


def window_place(starts, j, tile_rows, tile_cols, width, fast, slow):
    rim = width // 2
    row = starts[0, 0, j] - fast * tile_rows + rim
    col = starts[1, 0, j] - slow * tile_cols
    lane = jnp.where(col < 0, col + tile_cols + width, col)
    block = jnp.minimum(row // 8, (tile_rows + width - width - 8) // 8)
    return block * 8, row - block * 8, lane


def gradients(
    object_ref, probe, descan_rows, starts, measured_ref, tables_ref, gradient_ref, wave_ref, far_ref, sizes, parts
):
    tile_rows, tile_cols, width, modes, count, n_fast, n_slow, fast, slow = sizes
    ext_cols = tile_cols + width
    high = width + 8
    probe_real, probe_imag = probe
    lane_row = lane_of((1, width)).astype(F32)
    centred = (lane_row - width // 2) / width
    tables = [tables_ref[k] for k in range(6)]
    forward, backward = tables[:parts], tables[3 : 3 + parts]

    fractions = []
    phases = []
    for j in range(count):
        frac_row = jnp.full((1, width), starts[0, 0, j], jnp.int32).astype(F32) / (tile_rows * n_fast)
        frac_col = jnp.full((1, width), starts[1, 0, j], jnp.int32).astype(F32) / (tile_cols * n_slow)
        fractions.append((frac_row, frac_col))
        for k in range(2):
            d = descan_rows[3 * k : 3 * k + 3]
            phases.append((2 * math.pi) * ((d[0] + d[1] * frac_row + d[2] * frac_col) * centred))
    while len(phases) % 8:
        phases.append(jnp.zeros((1, width), F32))
    phases = jnp.concatenate(phases, axis=0)
    cosines, sines = jnp.cos(phases), jnp.sin(phases)

    def along_rows(row):
        return jnp.transpose(jnp.broadcast_to(row, (width, width)))

    lits = []
    ramps = []
    for j in range(count):
        row_start, row_shift, lane = window_place(starts, j, tile_rows, tile_cols, width, fast, slow)
        row_start = pl.multiple_of(row_start, 8)
        row_cos, row_sin = along_rows(cosines[2 * j : 2 * j + 1]), along_rows(sines[2 * j : 2 * j + 1])
        col_cos, col_sin = cosines[2 * j + 1 : 2 * j + 2], sines[2 * j + 1 : 2 * j + 2]
        ramp_real = row_cos * col_cos - row_sin * col_sin
        ramp_imag = row_cos * col_sin + row_sin * col_cos
        patch = []
        for part in range(2):
            rows = object_ref[part, pl.ds(row_start, high), :]
            rows = pltpu.roll(rows, lax.rem(ext_cols - lane, ext_cols), 1)[:, :width]
            patch.append(pltpu.roll(rows, lax.rem(high - row_shift, high), 0)[:width])
        lit_real = patch[0] * ramp_real - patch[1] * ramp_imag
        lit_imag = patch[0] * ramp_imag + patch[1] * ramp_real
        lits.append((lit_real, lit_imag))
        ramps.append((ramp_real, ramp_imag))
        for m in range(modes):
            p_real = probe_real[m * width : (m + 1) * width]
            p_imag = probe_imag[m * width : (m + 1) * width]
            at = (j * modes + m) * width
            wave_ref[at : at + width, :width] = p_real * lit_real - p_imag * lit_imag
            wave_ref[at : at + width, width:] = p_real * lit_imag + p_imag * lit_real

    half = product(split(wave_ref[...]), forward)
    for w in range(count * modes):
        at = w * width
        far_ref[:width, at : at + width] = half[at : at + width, :width]
        far_ref[width:, at : at + width] = half[at : at + width, width:]
    far = product(backward, split(far_ref[...]))
    far_ref[...] = far
    for j in range(count):
        intensity = None
        for m in range(modes):
            at = (j * modes + m) * width
            real, imag = far_ref[:width, at : at + width], far_ref[width:, at : at + width]
            power = real * real + imag * imag
            intensity = power if intensity is None else intensity + power
        factor = 1.0 - measured_ref[j] / jnp.sqrt(jnp.maximum(intensity, FLOOR_LEVEL))
        for m in range(modes):
            at = (j * modes + m) * width
            far_ref[:width, at : at + width] *= factor
            far_ref[width:, at : at + width] *= factor
    half = product(forward, split(far_ref[...]))
    for w in range(count * modes):
        at = w * width
        wave_ref[at : at + width, :width] = half[:width, at : at + width]
        wave_ref[at : at + width, width:] = half[width:, at : at + width]
    wave_ref[...] = product(split(wave_ref[...]), backward)

    gradient_ref[...] = jnp.zeros(gradient_ref.shape, F32)
    probe_grad = [[None] * modes, [None] * modes]
    descan_grad = [None] * 6
    centred_rows = along_rows(centred)
    for j in range(count):
        lit_real, lit_imag = lits[j]
        ramp_real, ramp_imag = ramps[j]
        sum_real = sum_imag = None
        for m in range(modes):
            p_real = probe_real[m * width : (m + 1) * width]
            p_imag = probe_imag[m * width : (m + 1) * width]
            at = (j * modes + m) * width
            real, imag = wave_ref[at : at + width, :width], wave_ref[at : at + width, width:]
            q_real = lit_real * real + lit_imag * imag
            q_imag = lit_real * imag - lit_imag * real
            probe_grad[0][m] = q_real if j == 0 else probe_grad[0][m] + q_real
            probe_grad[1][m] = q_imag if j == 0 else probe_grad[1][m] + q_imag
            h_real = p_real * real + p_imag * imag
            h_imag = p_real * imag - p_imag * real
            sum_real = h_real if m == 0 else sum_real + h_real
            sum_imag = h_imag if m == 0 else sum_imag + h_imag
        twist = lit_imag * sum_real - lit_real * sum_imag
        totals = (
            jnp.sum(jnp.sum(twist * centred_rows, axis=0, keepdims=True), axis=1, keepdims=True),
            jnp.sum(jnp.sum(twist, axis=0, keepdims=True) * centred, axis=1, keepdims=True),
        )
        frac_row, frac_col = fractions[j]
        for k in range(2):
            base = jnp.broadcast_to(-4 * math.pi * totals[k], (1, width))
            for n, term in enumerate((base, base * frac_row, base * frac_col)):
                descan_grad[3 * k + n] = term if j == 0 else descan_grad[3 * k + n] + term
        row_start, row_shift, lane = window_place(starts, j, tile_rows, tile_cols, width, fast, slow)
        row_start = pl.multiple_of(row_start, 8)
        parts = (
            ramp_real * sum_real + ramp_imag * sum_imag,
            ramp_real * sum_imag - ramp_imag * sum_real,
        )
        for part in range(2):
            value = jnp.concatenate([parts[part], jnp.zeros((8, width), F32)], axis=0)
            value = pltpu.roll(value, row_shift, 0)
            value = jnp.concatenate([value, jnp.zeros((high, ext_cols - width), F32)], axis=1)
            gradient_ref[part, pl.ds(row_start, high), :] += pltpu.roll(value, lane, 1)
    return probe_grad, descan_grad


def pick(parity, when_even, when_odd):
    return jnp.where(parity == 0, when_even, when_odd)


def both_sides(parity, even_ref, odd_ref, index=Ellipsis):
    even = even_ref[index]
    odd = jnp.zeros_like(even) if odd_ref is None else odd_ref[index]
    return pick(parity, even, odd), pick(parity, odd, even)


def put_sums(probe_grad, descan_grad, keep_ref, send_ref, core, width, modes):
    for m in range(modes):
        real, imag = probe_grad[0][m], probe_grad[1][m]
        keep_ref[m * width : (m + 1) * width] = jnp.where(core == 0, real, imag)
        send_ref[m * width : (m + 1) * width] = jnp.where(core == 0, imag, real)
    block = jnp.concatenate(descan_grad + [jnp.zeros((EXTRA - 6, width), F32)], axis=0)
    keep_ref[modes * width :] = block
    send_ref[modes * width :] = block


def put_quarters(probe_grad, descan_grad, mine_ref, beside_ref, send_ref, core, slow, width, modes):
    rows = modes * width
    real, imag = jnp.concatenate(probe_grad[0], axis=0), jnp.concatenate(probe_grad[1], axis=0)
    keep, send = pick(core, real, imag), pick(core, imag, real)
    half = rows // 2
    block = jnp.concatenate(descan_grad + [jnp.zeros((EXTRA - 6, width), F32)], axis=0)
    low, high = keep[:half], keep[half:]
    mine_ref[:half] = pick(slow, low, high)
    mine_ref[half:] = block
    beside_ref[:half] = pick(slow, high, low)
    beside_ref[half:] = block
    low, high = send[:half], send[half:]
    send_ref[0, :half] = pick(slow, low, high)
    send_ref[0, half:] = block
    send_ref[1, :half] = pick(slow, high, low)
    send_ref[1, half:] = block


def of_halves(halves, core, slow, rows):
    mine, other = halves[0][:rows], halves[1][...]
    return pick(core, mine, other), pick(core, other, mine)


def of_quarters(quarters, core, slow, rows):
    part = rows // 2
    values = [quarters[0][:part], quarters[1][...], quarters[2][:part], quarters[2][part:]]
    sums = []
    for own, beside in (
        (pick(core, values[0], values[2]), pick(core, values[1], values[3])),
        (pick(core, values[2], values[0]), pick(core, values[3], values[1])),
    ):
        sums.append(jnp.concatenate([pick(slow, own, beside), pick(slow, beside, own)], axis=0))
    return sums


def updated_probe(probe_ref, sums, total, width, modes):
    rows = modes * width
    real = probe_ref[0].reshape(rows, width) - PROBE_STEP / total * sums[0]
    imag = probe_ref[1].reshape(rows, width) - PROBE_STEP / total * sums[1]
    power = jnp.sum(jnp.sum(real * real + imag * imag, axis=0, keepdims=True), axis=1, keepdims=True)
    scale = jnp.sqrt(PROBE_POWER * rows * width / power)
    return real * scale, imag * scale


def halo_blocks(right, left, width):
    rim = width // 2
    low = lane_of(right.shape) < rim
    return jnp.where(low, right, pltpu.roll(left, rim, 1)), jnp.where(low, pltpu.roll(right, rim, 1), left)


def pack_kernel(sizes, object_ref, extended_ref, rows_even_ref, rows_odd_ref, *rest):
    tile_rows, tile_cols, width, modes, count, n_fast, n_slow = sizes
    rim = width // 2
    extended_ref[:, rim : rim + tile_rows, :tile_cols] = object_ref[...]
    fast = lax.rem(lax.axis_index("fast"), 2)
    initial, final = object_ref[:, :rim], object_ref[:, tile_rows - rim :]
    rows_even_ref[...] = pick(fast, final, initial)
    rows_odd_ref[...] = pick(fast, initial, final)
    swaps = len(rest) // 3
    put_edges(sizes, object_ref[...], rest[::3])
    for k in range(swaps):
        first, last = rest[3 * k][:rim], rest[3 * k][tile_rows - rim :]
        rest[3 * k + 1][...] = pick(fast, last, first)
        rest[3 * k + 2][...] = pick(fast, first, last)


def put_edges(sizes, rows, refs):
    tile_rows, tile_cols, width, modes, count, n_fast, n_slow = sizes
    rim = width // 2
    end, start = rows[:, :, tile_cols - width :], rows[:, :, :width]
    low = lane_of(end.shape[1:]) < rim
    to_right = jnp.where(low, pltpu.roll(end[0], rim, 1), end[1])
    to_left = jnp.where(low, start[0], pltpu.roll(start[1], rim, 1))
    put_strips(lax.axis_index("slow"), to_right, to_left, refs)


def first_kernel(
    sizes, starts, descan_ref, extended_in_ref, probe_ref, measured_ref, tables_ref,
    rows_even_ref, rows_odd_ref, halos,
    extended_ref, gradient_ref, strips, keep_ref, send_ref, wave_ref, far_ref,
):
    tile_rows, tile_cols, width, modes, count, n_fast, n_slow = sizes
    fast, slow = lax.axis_index("fast"), lax.axis_index("slow")
    core = lax.rem(fast, 2)
    rim = width // 2
    below, above = both_sides(core, rows_even_ref, rows_odd_ref)
    extended_ref[:, :rim, :tile_cols] = above
    extended_ref[:, rim + tile_rows :, :tile_cols] = below
    columns = []
    for middle_ref, even_ref, odd_ref in halos:
        after, before = both_sides(core, even_ref, odd_ref)
        columns.append(((0, before), (rim, middle_ref[...]), (rim + tile_rows, after)))
    for piece in range(3):
        at, even = columns[0][piece]
        odd = columns[-1][piece][1]
        real, imag = halo_blocks(pick(lax.rem(slow, 2), even, odd), pick(lax.rem(slow, 2), odd, even), width)
        extended_ref[0, at : at + even.shape[0], tile_cols:] = real
        extended_ref[1, at : at + even.shape[0], tile_cols:] = imag
    descan_rows = [jnp.broadcast_to(descan_ref[k // 3 : k // 3 + 1, k % 3 : k % 3 + 1], (1, width)) for k in range(6)]
    probe = tuple(probe_ref[part].reshape(modes * width, width) for part in range(2))
    probe_grad, descan_grad = gradients(
        extended_ref, probe, descan_rows, starts, measured_ref, tables_ref, gradient_ref, wave_ref, far_ref,
        sizes + (fast, slow), FIRST,
    )
    put_sums(probe_grad, descan_grad, keep_ref, send_ref, core, width, modes)
    halo = gradient_ref[:, :, tile_cols:]
    low = lane_of(halo.shape) < rim
    to_right = jnp.where(low, halo, gradient_ref[:, :, tile_cols - width : tile_cols])
    to_left = jnp.where(low, gradient_ref[:, :, :width], halo)
    put_strips(slow, to_right, to_left, strips)


def put_strips(place, to_next, to_previous, refs):
    parity = lax.rem(place, 2)
    refs[0][...] = pick(parity, to_next, to_previous)
    if len(refs) > 1:
        refs[1][...] = pick(parity, to_previous, to_next)


def add_columns(gradient, right, left, tile_cols, width):
    rim = width // 2
    low = lane_of(right.shape) < rim
    zero = jnp.zeros(right.shape, F32)
    blocks = [gradient[:, :, k : k + width] for k in range(0, tile_cols + width, width)]
    blocks[0] = blocks[0] + jnp.where(low, left, zero)
    blocks[-2] = blocks[-2] + jnp.where(low, zero, right)
    blocks[-1] = blocks[-1] + jnp.where(low, right, left)
    return jnp.concatenate(blocks, axis=2)


def toward_next(odd):
    return lax.rem(lax.axis_index("fast"), 2) == (1 if odd else 0)


def packed_halo(halo):
    rim = halo.shape[-1] // 2
    low = lane_of(halo.shape[1:]) < rim
    return jnp.where(low, halo[0], pltpu.roll(halo[1], rim, 1)), jnp.where(low, pltpu.roll(halo[0], rim, 1), halo[1])


def rows_shape(sizes):
    tile_rows, tile_cols, width, modes, count, n_fast, n_slow = sizes
    return (width, 2 * tile_cols + width) if n_slow == 2 else (2, width, tile_cols + width)


def rows_of(sizes, value):
    tile_rows, tile_cols, width, modes, count, n_fast, n_slow = sizes
    if n_slow > 2:
        return value[0], value[1]
    real, imag = halo_blocks(value[:, 2 * tile_cols :], value[:, 2 * tile_cols :], width)
    return (
        jnp.concatenate([value[:, :tile_cols], real], axis=1),
        jnp.concatenate([value[:, tile_cols : 2 * tile_cols], imag], axis=1),
    )


def rows_kernel(sizes, odd, gradient_ref, columns, token_ref, out_ref):
    tile_rows, tile_cols, width, modes, count, n_fast, n_slow = sizes
    slow = lax.rem(lax.axis_index("slow"), 2)
    at = pl.multiple_of(jnp.where(toward_next(odd), tile_rows, 0), 8)
    index = (slice(None), pl.ds(at, width))
    right, left = both_sides(slow, *columns, index)
    value = add_columns(gradient_ref[index], right, left, tile_cols, width)
    if n_slow > 2:
        out_ref[...] = value
        return
    out_ref[:, :tile_cols] = value[0, :, :tile_cols]
    out_ref[:, tile_cols : 2 * tile_cols] = value[1, :, :tile_cols]
    out_ref[:, 2 * tile_cols :] = pick(slow, *packed_halo(value[:, :, tile_cols:]))


def update_kernel(sizes, extended_ref, gradient_ref, columns, rows_even_ref, rows_odd_ref, object_ref):
    tile_rows, tile_cols, width, modes, count, n_fast, n_slow = sizes
    right, left = both_sides(lax.rem(lax.axis_index("slow"), 2), *columns)
    object_ref[...] = extended_ref[...] - OBJECT_STEP * add_columns(gradient_ref[...], right, left, tile_cols, width)
    below, above = both_sides(lax.rem(lax.axis_index("fast"), 2), rows_even_ref, rows_odd_ref)
    above, below = rows_of(sizes, above), rows_of(sizes, below)
    for part in range(2):
        object_ref[part, :width] -= OBJECT_STEP * above[part]
        object_ref[part, tile_rows:] -= OBJECT_STEP * below[part]


def second_kernel(
    sizes, total, starts, descan_ref, object_ref, probe_ref, measured_ref, tables_ref, mine_ref, other_ref,
    gradient_ref, strips, own_ref, beside_ref, send_ref, probe_out_ref, descan_out_ref, wave_ref, far_ref,
):
    tile_rows, tile_cols, width, modes, count, n_fast, n_slow = sizes
    fast, slow = lax.axis_index("fast"), lax.axis_index("slow")
    core = lax.rem(fast, 2)
    rim = width // 2
    sums = of_halves((mine_ref, other_ref), core, slow, modes * width)
    probe = updated_probe(probe_ref, sums, total, width, modes)
    probe_out_ref[0] = probe[0].reshape(modes, width, width)
    probe_out_ref[1] = probe[1].reshape(modes, width, width)
    at = modes * width
    descan_rows = [
        descan_ref[k // 3 : k // 3 + 1, k % 3 : k % 3 + 1] - DESCAN_STEP / total * mine_ref[at + k : at + k + 1]
        for k in range(6)
    ]
    descan_out_ref[...] = jnp.concatenate(descan_rows + [jnp.zeros((EXTRA - 6, width), F32)], axis=0)
    probe_grad, descan_grad = gradients(
        object_ref, probe, descan_rows, starts, measured_ref, tables_ref, gradient_ref, wave_ref, far_ref,
        sizes + (fast, slow), SECOND,
    )
    put_quarters(probe_grad, descan_grad, own_ref, beside_ref, send_ref, core, lax.rem(slow, 2), width, modes)
    real, imag = gradient_ref[0, :, tile_cols:], gradient_ref[1, :, tile_cols:]
    low = lane_of(real.shape) < rim
    to_right = jnp.where(low, real, pltpu.roll(imag, rim, 1))
    to_left = jnp.where(low, pltpu.roll(real, rim, 1), imag)
    put_strips(slow, to_right, to_left, strips)


def edge_blocks(slow, columns, rows, width):
    rim = width // 2
    right, left = both_sides(lax.rem(slow, 2), *columns, rows)
    low = lane_of(right.shape) < rim
    zero = jnp.zeros(right.shape, F32)
    first = (jnp.where(low, left, zero), jnp.where(low, pltpu.roll(left, rim, 1), zero))
    last = (jnp.where(low, zero, pltpu.roll(right, rim, 1)), jnp.where(low, zero, right))
    return first, last


def last_rows_kernel(sizes, odd, gradient_ref, columns, mine_ref, *rest):
    tile_rows, tile_cols, width, modes, count, n_fast, n_slow = sizes
    rim = width // 2
    out_ref = rest[-1]
    if odd:
        arrived_ref, sum_ref, out_ref = rest
        sum_ref[...] = mine_ref[...] + arrived_ref[...]
    at = pl.multiple_of(jnp.where(toward_next(odd), rim + tile_rows, 0), 8)
    out_ref[...] = gradient_ref[:, pl.ds(at, rim), :tile_cols]
    first, last = edge_blocks(lax.axis_index("slow"), columns, pl.ds(at, rim), width)
    for part in range(2):
        out_ref[part, :, :width] += first[part]
        out_ref[part, :, tile_cols - width :] += last[part]


def join_kernel(own_ref, beside_ref, *rest):
    rows = own_ref.shape[0]
    rest[-1][:rows] = own_ref[...]
    rest[-1][rows:] = beside_ref[...]


def object_kernel(sizes, object_ref, gradient_ref, columns, rows_even_ref, rows_odd_ref, out_ref):
    tile_rows, tile_cols, width, modes, count, n_fast, n_slow = sizes
    rim = width // 2
    inner = (slice(None), slice(rim, rim + tile_rows), slice(0, tile_cols))
    out_ref[...] = object_ref[inner] - OBJECT_STEP * gradient_ref[inner]
    first, last = edge_blocks(lax.axis_index("slow"), columns, slice(rim, rim + tile_rows), width)
    for part in range(2):
        out_ref[part, :, :width] -= OBJECT_STEP * first[part]
        out_ref[part, :, tile_cols - width :] -= OBJECT_STEP * last[part]
    below, above = both_sides(lax.rem(lax.axis_index("fast"), 2), rows_even_ref, rows_odd_ref)
    out_ref[:, :rim] -= OBJECT_STEP * above
    out_ref[:, tile_rows - rim :] -= OBJECT_STEP * below


def probe_kernel(sizes, total, probe_ref, descan_ref, quarters, probe_out_ref, descan_out_ref):
    tile_rows, tile_cols, width, modes, count, n_fast, n_slow = sizes
    core, slow = lax.rem(lax.axis_index("fast"), 2), lax.rem(lax.axis_index("slow"), 2)
    sums = of_quarters(quarters, core, slow, modes * width)
    real, imag = updated_probe(probe_ref, sums, total, width, modes)
    probe_out_ref[0] = real.reshape(modes, width, width)
    probe_out_ref[1] = imag.reshape(modes, width, width)
    at = modes * width // 2
    rows = descan_ref[...] - DESCAN_STEP / total * quarters[0][at : at + EXTRA]
    lane = lane_of((1, width))
    for k in range(2):
        values = [rows[3 * k + n : 3 * k + n + 1] for n in range(3)]
        row = jnp.where(lane == 0, values[0], jnp.where(lane == 1, values[1], values[2]))
        descan_out_ref[k : k + 1, :] = row[:, :3]


def call(kernel, outs, scratch, *operands, smem=0, hbm=False, semaphores=(), aliases=None, work=0):
    return pl.pallas_call(
        kernel,
        out_shape=[out if isinstance(out, jax.ShapeDtypeStruct) else jax.ShapeDtypeStruct(out, F32) for out in outs],
        in_specs=[SMEM] * smem + [HBM if hbm else VMEM] * (len(operands) - smem),
        out_specs=[VMEM] * len(outs),
        scratch_shapes=[pltpu.VMEM(shape, F32) for shape in scratch]
        + [pltpu.SemaphoreType.DMA(shape) for shape in semaphores],
        input_output_aliases=aliases or {},
        compiler_params=pltpu.CompilerParams(vmem_limit_bytes=LIMIT),
        cost_estimate=pl.CostEstimate(flops=work, bytes_accessed=work // 100, transcendentals=0) if work else None,
    )(*operands)


def on_device(object_field, probe_modes, descan, scan_positions, amplitudes):
    width = amplitudes.shape[-1]
    rim = width // 2
    modes = probe_modes.shape[1]
    count = scan_positions.shape[1]
    tile_rows, tile_cols = object_field.shape[1:]
    n_fast, n_slow = lax.axis_size("fast"), lax.axis_size("slow")
    total = count * n_fast * n_slow
    sizes = (tile_rows, tile_cols, width, modes, count, n_fast, n_slow)
    fast, slow = lax.axis_index("fast"), lax.axis_index("slow")
    starts = scan_positions.transpose(0, 2, 1)
    tables = transform_tables(width)
    ext_rows, ext_cols = tile_rows + width, tile_cols + width
    half_rows = modes * width
    swaps = 1 if n_slow == 2 else 2

    def partner(place, odd, length):
        other = place ^ 1 if not odd else ((place + 1) ^ 1) - 1
        return other if 0 <= other < length else None

    def exchanged(value, fast_swap=None, slow_swap=None):
        pairs = []
        for f in range(n_fast):
            for s in range(n_slow):
                to_fast = f if fast_swap is None else partner(f, fast_swap, n_fast)
                to_slow = s if slow_swap is None else partner(s, slow_swap, n_slow)
                if to_fast is not None and to_slow is not None:
                    pairs.append((f * n_slow + s, to_fast * n_slow + to_slow))
        return lax.ppermute(value, AXES, pairs)

    def swapped(value, axis, bit):
        return lax.ppermute(value, axis, [(i, i ^ bit) for i in range(lax.axis_size(axis))])

    assert n_fast >= 4 and n_slow >= 2 and not n_fast % 2 and not n_slow % 2
    regular = not (n_fast & (n_fast - 1) or n_slow & (n_slow - 1))
    fast_bits = [1 << k for k in range(1, n_fast.bit_length() - 1)]
    slow_bits = [1 << k for k in range(n_slow.bit_length() - 1)]

    def sum_begun(keep, send):
        mine = keep + swapped(send, "fast", 1)
        if regular:
            for bit in fast_bits[:-1]:
                mine = mine + swapped(mine, "fast", bit)
        return mine

    def fast_ended(mine):
        return mine + swapped(mine, "fast", fast_bits[-1]) if regular else mine

    def sum_ended(mine):
        if regular:
            for bit in slow_bits:
                mine = mine + swapped(mine, "slow", bit)
        else:
            core = lax.rem(fast, 2)
            every = lax.psum(jnp.where(jnp.arange(2)[:, None, None] == core, mine, 0.0), AXES) * 0.5
            mine = lax.dynamic_index_in_dim(every, core, keepdims=False)
        return mine, swapped(mine[:half_rows], "fast", 1)

    def pairwise(refs):
        return refs if swaps == 2 else (refs[0], None)

    extended, rows_even, rows_odd, *packed = call(
        functools.partial(pack_kernel, sizes),
        [(2, ext_rows, ext_cols)] + [(2, rim, tile_cols)] * 2
        + [(tile_rows, width), (rim, width), (rim, width)] * swaps, [],
        object_field, work=WORK,
    )
    halos = []
    rows_odd = exchanged(rows_odd, 1)
    for k in range(swaps):
        corner_odd = exchanged(packed[3 * k + 2], 1, k)
        middle = exchanged(packed[3 * k], None, k)
        halos += [middle, exchanged(packed[3 * k + 1], 0, k), corner_odd]
    rows_even = exchanged(rows_even, 0)
    def first(starts_ref, descan_ref, extended_ref, probe_ref, measured_ref, tables_ref, *rest):
        halo_refs = [rest[2 + 3 * k : 5 + 3 * k] for k in range(swaps)]
        extended_out_ref, gradient_ref, *rest_out = rest[2 + 3 * swaps :]
        first_kernel(sizes, starts_ref, descan_ref, extended_ref, probe_ref, measured_ref, tables_ref,
                     *rest[:2], halo_refs, extended_out_ref, gradient_ref, rest_out[:swaps], *rest_out[swaps:])

    scratch = [(count * modes * width, 2 * width), (2 * width, count * modes * width)]
    sums = [(half_rows + EXTRA, width)] * 2
    extended, gradient, *strips, keep, send = call(
        first,
        [(2, ext_rows, ext_cols)] * 2 + [(2, ext_rows, width)] * swaps + sums,
        scratch,
        starts, descan, extended, probe_modes, amplitudes, tables, rows_even, rows_odd, *halos,
        smem=1, aliases={2: 0},
    )
    columns = [exchanged(strip, None, k) for k, strip in enumerate(strips)]
    mine = sum_begun(keep, send)

    def rows(odd, gradient_ref, *rest):
        rows_kernel(sizes, odd, gradient_ref, pairwise(rest[:swaps]), *rest[swaps:])

    def rows_for(odd, token):
        return call(functools.partial(rows, odd), [rows_shape(sizes)], [], gradient, *columns, token)[0]

    rows_odd = exchanged(rows_for(True, mine), 1)
    rows_even = exchanged(rows_for(False, mine), 0)
    mine = fast_ended(mine)
    mine, other = sum_ended(mine)

    def update(extended_ref, gradient_ref, *rest):
        update_kernel(sizes, extended_ref, gradient_ref, pairwise(rest[:swaps]), *rest[swaps:])

    (extended,) = call(
        update, [(2, ext_rows, ext_cols)], [], extended, gradient, *columns, rows_even, rows_odd, aliases={0: 0},
    )

    def second(starts_ref, descan_ref, object_ref, probe_ref, measured_ref, tables_ref, mine_ref, other_ref, *rest):
        gradient_ref, *rest_out = rest
        second_kernel(sizes, total, starts_ref, descan_ref, object_ref, probe_ref, measured_ref, tables_ref,
                      mine_ref, other_ref, gradient_ref, rest_out[:swaps], *rest_out[swaps:])

    part = (half_rows // 2 + EXTRA, width)
    gradient, *strips, mine, beside, send, probes, descan_rows = call(
        second,
        [(2, ext_rows, ext_cols)] + [(ext_rows, width)] * swaps + [part, part, (2, *part)]
        + [probe_modes.shape, (EXTRA, width)],
        scratch,
        starts, descan, extended, probe_modes, amplitudes, tables, mine, other,
        smem=1,
    )
    columns = [exchanged(strip, None, k) for k, strip in enumerate(strips)]
    core_part = swapped(send, "fast", 1)
    mine = mine + core_part[0] + swapped(beside + core_part[1], "slow", 1)
    steps = [("fast", bit) for bit in fast_bits] + [("slow", bit) for bit in slow_bits[1:]]

    def last_rows(odd, gradient_ref, *rest):
        last_rows_kernel(sizes, odd, gradient_ref, pairwise(rest[:swaps]), *rest[swaps:])

    arrived = swapped(mine, *steps[0]) if regular else jnp.zeros_like(mine)
    mine, rows_odd = call(
        functools.partial(last_rows, True), [part, (2, rim, tile_cols)], [], gradient, *columns, mine, arrived,
    )
    rows_odd = exchanged(rows_odd, 1)
    if regular:
        for step in steps[1:]:
            mine = mine + swapped(mine, *step)
    else:
        place = 2 * lax.rem(fast, 2) + lax.rem(slow, 2)
        every = lax.psum(jnp.where(jnp.arange(4)[:, None, None] == place, mine, 0.0), AXES)
        mine = lax.dynamic_index_in_dim(every, place, keepdims=False)
    (rows_even,) = call(
        functools.partial(last_rows, False), [(2, rim, tile_cols)], [], gradient, *columns, mine,
    )
    rows_even = exchanged(rows_even, 0)
    own = mine[: half_rows // 2]
    beside = swapped(own, "slow", 1)
    (both,) = call(join_kernel, [(half_rows, width)], [], own, beside, rows_even, rows_odd)
    other = swapped(both, "fast", 1)

    def objects_of(object_ref, gradient_ref, *rest):
        object_kernel(sizes, object_ref, gradient_ref, pairwise(rest[:swaps]), *rest[swaps:])

    (objects,) = call(
        objects_of, [(2, tile_rows, tile_cols)], [], extended, gradient, *columns, rows_even, rows_odd,
    )

    def probe_of(probe_ref, descan_ref, q0, q1, q2, *outs):
        probe_kernel(sizes, total, probe_ref, descan_ref, (q0, q1, q2), *outs)

    probes, descan_out = call(
        probe_of, [probe_modes.shape, descan.shape], [],
        probes, descan_rows, mine, beside, other,
    )
    return objects, probes, descan_out


def solution(mesh):
    placed = (P(None, "fast", "slow"), P(), P(), P(None, "fast", "slow"), P("fast", "slow", None))
    return jax.shard_map(
        on_device,
        mesh=mesh,
        in_specs=placed,
        out_specs=(P(None, "fast", "slow"), P(), P()),
        check_vma=False,
    )
```

```python
import functools
import math

import jax
import jax.numpy as jnp
import numpy as np
from jax import lax
from jax.experimental import pallas as pl
from jax.experimental.pallas import tpu as pltpu
from jax.sharding import PartitionSpec as P

OBJECT_STEP = 0.1
PROBE_STEP = 8.0
DESCAN_STEP = 0.02
FLOOR_LEVEL = 0.25
PROBE_POWER = 0.5
EXTRA = 8
FIRST, SECOND = 3, 2
AXES = ("fast", "slow")
F32 = jnp.float32
BF16 = jnp.bfloat16
VMEM = pl.BlockSpec(memory_space=pltpu.VMEM)
SMEM = pl.BlockSpec(memory_space=pltpu.SMEM)
HBM = pl.BlockSpec(memory_space=pltpu.HBM)
LIMIT = 40 * 1024 * 1024
WORK = 2_000_000_000


def transform_tables(width):
    counter = np.arange(width)
    angles = 2.0 * np.pi / width * (counter[:, None] * counter[None, :] % width)
    real = np.cos(angles) / math.sqrt(width)
    imag = -np.sin(angles) / math.sqrt(width)
    forward = np.block([[real, imag], [-imag, real]])
    backward = np.block([[real, -imag], [imag, real]])
    parts = []
    for table in (forward, backward):
        for _ in range(3):
            parts.append(table.astype(BF16))
            table = table - parts[-1].astype(np.float64)
    return jnp.asarray(np.stack(parts))


def split(value):
    high = value.astype(BF16)
    value = value - high.astype(F32)
    middle = value.astype(BF16)
    return high, middle, (value - middle.astype(F32)).astype(BF16)


def dot(a, b):
    return jnp.dot(a, b, preferred_element_type=F32)


def product(left, right):
    (a, b, *c), (d, e, *f) = left, right
    if not c or not f:
        return dot(a, d) + (dot(a, e) + dot(b, d))
    (c,), (f,) = c, f
    return dot(a, d) + (dot(a, e) + dot(b, d) + (dot(b, e) + dot(a, f) + dot(c, d)))


def lane_of(shape):
    return lax.broadcasted_iota(jnp.int32, shape, len(shape) - 1)


def window_place(starts, j, tile_rows, tile_cols, width, fast, slow):
    rim = width // 2
    row = starts[0, 0, j] - fast * tile_rows + rim
    col = starts[1, 0, j] - slow * tile_cols
    lane = jnp.where(col < 0, col + tile_cols + width, col)
    block = jnp.minimum(row // 8, (tile_rows + width - width - 8) // 8)
    return block * 8, row - block * 8, lane


def gradients(
    object_ref, probe, descan_rows, starts, measured_ref, tables_ref, gradient_ref, wave_ref, far_ref, sizes, parts
):
    tile_rows, tile_cols, width, modes, count, n_fast, n_slow, fast, slow = sizes
    ext_cols = tile_cols + width
    high = width + 8
    probe_real, probe_imag = probe
    lane_row = lane_of((1, width)).astype(F32)
    centred = (lane_row - width // 2) / width
    tables = [tables_ref[k] for k in range(6)]
    forward, backward = tables[:parts], tables[3 : 3 + parts]

    fractions = []
    phases = []
    for j in range(count):
        frac_row = jnp.full((1, width), starts[0, 0, j], jnp.int32).astype(F32) / (tile_rows * n_fast)
        frac_col = jnp.full((1, width), starts[1, 0, j], jnp.int32).astype(F32) / (tile_cols * n_slow)
        fractions.append((frac_row, frac_col))
        for k in range(2):
            d = descan_rows[3 * k : 3 * k + 3]
            phases.append((2 * math.pi) * ((d[0] + d[1] * frac_row + d[2] * frac_col) * centred))
    while len(phases) % 8:
        phases.append(jnp.zeros((1, width), F32))
    phases = jnp.concatenate(phases, axis=0)
    cosines, sines = jnp.cos(phases), jnp.sin(phases)

    turned = jnp.transpose(jnp.concatenate([cosines, sines, jnp.broadcast_to(centred, (8, width))], axis=0))
    sine_at, centre_at = cosines.shape[0], 2 * cosines.shape[0]

    def along_rows(k):
        return jnp.broadcast_to(turned[:, k : k + 1], (width, width))

    lits = []
    ramps = []
    for j in range(count):
        row_start, row_shift, lane = window_place(starts, j, tile_rows, tile_cols, width, fast, slow)
        row_start = pl.multiple_of(row_start, 8)
        row_cos, row_sin = along_rows(2 * j), along_rows(sine_at + 2 * j)
        col_cos, col_sin = cosines[2 * j + 1 : 2 * j + 2], sines[2 * j + 1 : 2 * j + 2]
        ramp_real = row_cos * col_cos - row_sin * col_sin
        ramp_imag = row_cos * col_sin + row_sin * col_cos
        patch = []
        for part in range(2):
            rows = object_ref[part, pl.ds(row_start, high), :]
            rows = pltpu.roll(rows, lax.rem(ext_cols - lane, ext_cols), 1)[:, :width]
            patch.append(pltpu.roll(rows, lax.rem(high - row_shift, high), 0)[:width])
        lit_real = patch[0] * ramp_real - patch[1] * ramp_imag
        lit_imag = patch[0] * ramp_imag + patch[1] * ramp_real
        lits.append((lit_real, lit_imag))
        ramps.append((ramp_real, ramp_imag))
        for m in range(modes):
            p_real = probe_real[m * width : (m + 1) * width]
            p_imag = probe_imag[m * width : (m + 1) * width]
            at = (j * modes + m) * width
            wave_ref[at : at + width, :width] = p_real * lit_real - p_imag * lit_imag
            wave_ref[at : at + width, width:] = p_real * lit_imag + p_imag * lit_real

    half = product(split(wave_ref[...]), forward)
    for w in range(count * modes):
        at = w * width
        far_ref[:width, at : at + width] = half[at : at + width, :width]
        far_ref[width:, at : at + width] = half[at : at + width, width:]
    far = product(backward, split(far_ref[...]))
    far_ref[...] = far
    for j in range(count):
        intensity = None
        for m in range(modes):
            at = (j * modes + m) * width
            real, imag = far_ref[:width, at : at + width], far_ref[width:, at : at + width]
            power = real * real + imag * imag
            intensity = power if intensity is None else intensity + power
        factor = 1.0 - measured_ref[j] / jnp.sqrt(jnp.maximum(intensity, FLOOR_LEVEL))
        for m in range(modes):
            at = (j * modes + m) * width
            far_ref[:width, at : at + width] *= factor
            far_ref[width:, at : at + width] *= factor
    half = product(forward, split(far_ref[...]))
    for w in range(count * modes):
        at = w * width
        wave_ref[at : at + width, :width] = half[:width, at : at + width]
        wave_ref[at : at + width, width:] = half[width:, at : at + width]
    wave_ref[...] = product(split(wave_ref[...]), backward)

    gradient_ref[...] = jnp.zeros(gradient_ref.shape, F32)
    probe_grad = [[None] * modes, [None] * modes]
    descan_grad = [None] * 6
    centred_rows = along_rows(centre_at)
    for j in range(count):
        lit_real, lit_imag = lits[j]
        ramp_real, ramp_imag = ramps[j]
        sum_real = sum_imag = None
        for m in range(modes):
            p_real = probe_real[m * width : (m + 1) * width]
            p_imag = probe_imag[m * width : (m + 1) * width]
            at = (j * modes + m) * width
            real, imag = wave_ref[at : at + width, :width], wave_ref[at : at + width, width:]
            q_real = lit_real * real + lit_imag * imag
            q_imag = lit_real * imag - lit_imag * real
            probe_grad[0][m] = q_real if j == 0 else probe_grad[0][m] + q_real
            probe_grad[1][m] = q_imag if j == 0 else probe_grad[1][m] + q_imag
            h_real = p_real * real + p_imag * imag
            h_imag = p_real * imag - p_imag * real
            sum_real = h_real if m == 0 else sum_real + h_real
            sum_imag = h_imag if m == 0 else sum_imag + h_imag
        twist = lit_imag * sum_real - lit_real * sum_imag
        totals = (
            jnp.sum(jnp.sum(twist * centred_rows, axis=0, keepdims=True), axis=1, keepdims=True),
            jnp.sum(jnp.sum(twist, axis=0, keepdims=True) * centred, axis=1, keepdims=True),
        )
        frac_row, frac_col = fractions[j]
        for k in range(2):
            base = jnp.broadcast_to(-4 * math.pi * totals[k], (1, width))
            for n, term in enumerate((base, base * frac_row, base * frac_col)):
                descan_grad[3 * k + n] = term if j == 0 else descan_grad[3 * k + n] + term
        row_start, row_shift, lane = window_place(starts, j, tile_rows, tile_cols, width, fast, slow)
        row_start = pl.multiple_of(row_start, 8)
        parts = (
            ramp_real * sum_real + ramp_imag * sum_imag,
            ramp_real * sum_imag - ramp_imag * sum_real,
        )
        for part in range(2):
            value = jnp.concatenate([parts[part], jnp.zeros((8, width), F32)], axis=0)
            value = pltpu.roll(value, row_shift, 0)
            value = jnp.concatenate([value, jnp.zeros((high, ext_cols - width), F32)], axis=1)
            gradient_ref[part, pl.ds(row_start, high), :] += pltpu.roll(value, lane, 1)
    return probe_grad, descan_grad


def pick(parity, when_even, when_odd):
    return jnp.where(parity == 0, when_even, when_odd)


def both_sides(parity, even_ref, odd_ref, index=Ellipsis):
    even = even_ref[index]
    odd = jnp.zeros_like(even) if odd_ref is None else odd_ref[index]
    return pick(parity, even, odd), pick(parity, odd, even)


def put_sums(probe_grad, descan_grad, keep_ref, send_ref, core, width, modes):
    for m in range(modes):
        real, imag = probe_grad[0][m], probe_grad[1][m]
        keep_ref[m * width : (m + 1) * width] = jnp.where(core == 0, real, imag)
        send_ref[m * width : (m + 1) * width] = jnp.where(core == 0, imag, real)
    block = jnp.concatenate(descan_grad + [jnp.zeros((EXTRA - 6, width), F32)], axis=0)
    keep_ref[modes * width :] = block
    send_ref[modes * width :] = block


def put_quarters(probe_grad, descan_grad, mine_ref, beside_ref, send_ref, core, slow, width, modes):
    rows = modes * width
    real, imag = jnp.concatenate(probe_grad[0], axis=0), jnp.concatenate(probe_grad[1], axis=0)
    keep, send = pick(core, real, imag), pick(core, imag, real)
    half = rows // 2
    block = jnp.concatenate(descan_grad + [jnp.zeros((EXTRA - 6, width), F32)], axis=0)
    low, high = keep[:half], keep[half:]
    mine_ref[:half] = pick(slow, low, high)
    mine_ref[half:] = block
    beside_ref[:half] = pick(slow, high, low)
    beside_ref[half:] = block
    low, high = send[:half], send[half:]
    send_ref[0, :half] = pick(slow, low, high)
    send_ref[0, half:] = block
    send_ref[1, :half] = pick(slow, high, low)
    send_ref[1, half:] = block


def of_halves(halves, core, slow, rows):
    mine, other = halves[0][:rows], halves[1][...]
    return pick(core, mine, other), pick(core, other, mine)


def of_quarters(quarters, core, slow, rows):
    part = rows // 2
    values = [quarters[0][:part], quarters[1][...], quarters[2][:part], quarters[2][part:]]
    sums = []
    for own, beside in (
        (pick(core, values[0], values[2]), pick(core, values[1], values[3])),
        (pick(core, values[2], values[0]), pick(core, values[3], values[1])),
    ):
        sums.append(jnp.concatenate([pick(slow, own, beside), pick(slow, beside, own)], axis=0))
    return sums


def updated_probe(probe_ref, sums, total, width, modes):
    rows = modes * width
    real = probe_ref[0].reshape(rows, width) - PROBE_STEP / total * sums[0]
    imag = probe_ref[1].reshape(rows, width) - PROBE_STEP / total * sums[1]
    power = jnp.sum(jnp.sum(real * real + imag * imag, axis=0, keepdims=True), axis=1, keepdims=True)
    scale = jnp.sqrt(PROBE_POWER * rows * width / power)
    return real * scale, imag * scale


def halo_blocks(right, left, width):
    rim = width // 2
    low = lane_of(right.shape) < rim
    return jnp.where(low, right, pltpu.roll(left, rim, 1)), jnp.where(low, pltpu.roll(right, rim, 1), left)


def pack_kernel(sizes, object_ref, extended_ref, rows_even_ref, rows_odd_ref, *rest):
    tile_rows, tile_cols, width, modes, count, n_fast, n_slow = sizes
    rim = width // 2
    extended_ref[:, rim : rim + tile_rows, :tile_cols] = object_ref[...]
    fast = lax.rem(lax.axis_index("fast"), 2)
    initial, final = object_ref[:, :rim], object_ref[:, tile_rows - rim :]
    rows_even_ref[...] = pick(fast, final, initial)
    rows_odd_ref[...] = pick(fast, initial, final)
    swaps = len(rest) // 3
    put_edges(sizes, object_ref[...], rest[::3])
    for k in range(swaps):
        first, last = rest[3 * k][:rim], rest[3 * k][tile_rows - rim :]
        rest[3 * k + 1][...] = pick(fast, last, first)
        rest[3 * k + 2][...] = pick(fast, first, last)


def put_edges(sizes, rows, refs):
    tile_rows, tile_cols, width, modes, count, n_fast, n_slow = sizes
    rim = width // 2
    end, start = rows[:, :, tile_cols - width :], rows[:, :, :width]
    low = lane_of(end.shape[1:]) < rim
    to_right = jnp.where(low, pltpu.roll(end[0], rim, 1), end[1])
    to_left = jnp.where(low, start[0], pltpu.roll(start[1], rim, 1))
    put_strips(lax.axis_index("slow"), to_right, to_left, refs)


def first_kernel(
    sizes, starts, descan_ref, extended_in_ref, probe_ref, measured_ref, tables_ref,
    rows_even_ref, rows_odd_ref, halos,
    extended_ref, gradient_ref, strips, keep_ref, send_ref, wave_ref, far_ref,
):
    tile_rows, tile_cols, width, modes, count, n_fast, n_slow = sizes
    fast, slow = lax.axis_index("fast"), lax.axis_index("slow")
    core = lax.rem(fast, 2)
    rim = width // 2
    below, above = both_sides(core, rows_even_ref, rows_odd_ref)
    extended_ref[:, :rim, :tile_cols] = above
    extended_ref[:, rim + tile_rows :, :tile_cols] = below
    columns = []
    for middle_ref, even_ref, odd_ref in halos:
        after, before = both_sides(core, even_ref, odd_ref)
        columns.append(((0, before), (rim, middle_ref[...]), (rim + tile_rows, after)))
    for piece in range(3):
        at, even = columns[0][piece]
        odd = columns[-1][piece][1]
        real, imag = halo_blocks(pick(lax.rem(slow, 2), even, odd), pick(lax.rem(slow, 2), odd, even), width)
        extended_ref[0, at : at + even.shape[0], tile_cols:] = real
        extended_ref[1, at : at + even.shape[0], tile_cols:] = imag
    descan_rows = [jnp.broadcast_to(descan_ref[k // 3 : k // 3 + 1, k % 3 : k % 3 + 1], (1, width)) for k in range(6)]
    probe = tuple(probe_ref[part].reshape(modes * width, width) for part in range(2))
    probe_grad, descan_grad = gradients(
        extended_ref, probe, descan_rows, starts, measured_ref, tables_ref, gradient_ref, wave_ref, far_ref,
        sizes + (fast, slow), FIRST,
    )
    put_sums(probe_grad, descan_grad, keep_ref, send_ref, core, width, modes)
    halo = gradient_ref[:, :, tile_cols:]
    low = lane_of(halo.shape) < rim
    to_right = jnp.where(low, halo, gradient_ref[:, :, tile_cols - width : tile_cols])
    to_left = jnp.where(low, gradient_ref[:, :, :width], halo)
    put_strips(slow, to_right, to_left, strips)


def put_strips(place, to_next, to_previous, refs):
    parity = lax.rem(place, 2)
    refs[0][...] = pick(parity, to_next, to_previous)
    if len(refs) > 1:
        refs[1][...] = pick(parity, to_previous, to_next)


def add_columns(gradient, right, left, tile_cols, width):
    rim = width // 2
    low = lane_of(right.shape) < rim
    zero = jnp.zeros(right.shape, F32)
    blocks = [gradient[:, :, k : k + width] for k in range(0, tile_cols + width, width)]
    blocks[0] = blocks[0] + jnp.where(low, left, zero)
    blocks[-2] = blocks[-2] + jnp.where(low, zero, right)
    blocks[-1] = blocks[-1] + jnp.where(low, right, left)
    return jnp.concatenate(blocks, axis=2)


def toward_next(odd):
    return lax.rem(lax.axis_index("fast"), 2) == (1 if odd else 0)


def packed_halo(halo):
    rim = halo.shape[-1] // 2
    low = lane_of(halo.shape[1:]) < rim
    return jnp.where(low, halo[0], pltpu.roll(halo[1], rim, 1)), jnp.where(low, pltpu.roll(halo[0], rim, 1), halo[1])


def rows_shape(sizes):
    tile_rows, tile_cols, width, modes, count, n_fast, n_slow = sizes
    return (width, 2 * tile_cols + width) if n_slow == 2 else (2, width, tile_cols + width)


def rows_of(sizes, value):
    tile_rows, tile_cols, width, modes, count, n_fast, n_slow = sizes
    if n_slow > 2:
        return value[0], value[1]
    real, imag = halo_blocks(value[:, 2 * tile_cols :], value[:, 2 * tile_cols :], width)
    return (
        jnp.concatenate([value[:, :tile_cols], real], axis=1),
        jnp.concatenate([value[:, tile_cols : 2 * tile_cols], imag], axis=1),
    )


def rows_kernel(sizes, odd, gradient_ref, columns, token_ref, out_ref):
    tile_rows, tile_cols, width, modes, count, n_fast, n_slow = sizes
    slow = lax.rem(lax.axis_index("slow"), 2)
    at = pl.multiple_of(jnp.where(toward_next(odd), tile_rows, 0), 8)
    index = (slice(None), pl.ds(at, width))
    right, left = both_sides(slow, *columns, index)
    value = add_columns(gradient_ref[index], right, left, tile_cols, width)
    if n_slow > 2:
        out_ref[...] = value
        return
    out_ref[:, :tile_cols] = value[0, :, :tile_cols]
    out_ref[:, tile_cols : 2 * tile_cols] = value[1, :, :tile_cols]
    out_ref[:, 2 * tile_cols :] = pick(slow, *packed_halo(value[:, :, tile_cols:]))


def update_kernel(sizes, extended_ref, gradient_ref, columns, rows_even_ref, rows_odd_ref, object_ref):
    tile_rows, tile_cols, width, modes, count, n_fast, n_slow = sizes
    right, left = both_sides(lax.rem(lax.axis_index("slow"), 2), *columns)
    object_ref[...] = extended_ref[...] - OBJECT_STEP * add_columns(gradient_ref[...], right, left, tile_cols, width)
    below, above = both_sides(lax.rem(lax.axis_index("fast"), 2), rows_even_ref, rows_odd_ref)
    above, below = rows_of(sizes, above), rows_of(sizes, below)
    for part in range(2):
        object_ref[part, :width] -= OBJECT_STEP * above[part]
        object_ref[part, tile_rows:] -= OBJECT_STEP * below[part]


def second_kernel(
    sizes, total, starts, descan_ref, object_ref, probe_ref, measured_ref, tables_ref, mine_ref, other_ref,
    gradient_ref, strips, own_ref, beside_ref, send_ref, probe_out_ref, descan_out_ref, wave_ref, far_ref,
):
    tile_rows, tile_cols, width, modes, count, n_fast, n_slow = sizes
    fast, slow = lax.axis_index("fast"), lax.axis_index("slow")
    core = lax.rem(fast, 2)
    rim = width // 2
    sums = of_halves((mine_ref, other_ref), core, slow, modes * width)
    probe = updated_probe(probe_ref, sums, total, width, modes)
    probe_out_ref[0] = probe[0].reshape(modes, width, width)
    probe_out_ref[1] = probe[1].reshape(modes, width, width)
    at = modes * width
    descan_rows = [
        descan_ref[k // 3 : k // 3 + 1, k % 3 : k % 3 + 1] - DESCAN_STEP / total * mine_ref[at + k : at + k + 1]
        for k in range(6)
    ]
    descan_out_ref[...] = jnp.concatenate(descan_rows + [jnp.zeros((EXTRA - 6, width), F32)], axis=0)
    probe_grad, descan_grad = gradients(
        object_ref, probe, descan_rows, starts, measured_ref, tables_ref, gradient_ref, wave_ref, far_ref,
        sizes + (fast, slow), SECOND,
    )
    put_quarters(probe_grad, descan_grad, own_ref, beside_ref, send_ref, core, lax.rem(slow, 2), width, modes)
    real, imag = gradient_ref[0, :, tile_cols:], gradient_ref[1, :, tile_cols:]
    low = lane_of(real.shape) < rim
    to_right = jnp.where(low, real, pltpu.roll(imag, rim, 1))
    to_left = jnp.where(low, pltpu.roll(real, rim, 1), imag)
    put_strips(slow, to_right, to_left, strips)


def edge_blocks(slow, columns, rows, width):
    rim = width // 2
    right, left = both_sides(lax.rem(slow, 2), *columns, rows)
    low = lane_of(right.shape) < rim
    zero = jnp.zeros(right.shape, F32)
    first = (jnp.where(low, left, zero), jnp.where(low, pltpu.roll(left, rim, 1), zero))
    last = (jnp.where(low, zero, pltpu.roll(right, rim, 1)), jnp.where(low, zero, right))
    return first, last


def last_rows_kernel(sizes, odd, gradient_ref, columns, mine_ref, *rest):
    tile_rows, tile_cols, width, modes, count, n_fast, n_slow = sizes
    rim = width // 2
    out_ref = rest[-1]
    if odd:
        arrived_ref, sum_ref, out_ref = rest
        sum_ref[...] = mine_ref[...] + arrived_ref[...]
    at = pl.multiple_of(jnp.where(toward_next(odd), rim + tile_rows, 0), 8)
    out_ref[...] = gradient_ref[:, pl.ds(at, rim), :tile_cols]
    first, last = edge_blocks(lax.axis_index("slow"), columns, pl.ds(at, rim), width)
    for part in range(2):
        out_ref[part, :, :width] += first[part]
        out_ref[part, :, tile_cols - width :] += last[part]


def join_kernel(own_ref, beside_ref, *rest):
    rows = own_ref.shape[0]
    rest[-1][:rows] = own_ref[...]
    rest[-1][rows:] = beside_ref[...]


def object_kernel(sizes, object_ref, gradient_ref, columns, rows_even_ref, rows_odd_ref, out_ref):
    tile_rows, tile_cols, width, modes, count, n_fast, n_slow = sizes
    rim = width // 2
    inner = (slice(None), slice(rim, rim + tile_rows), slice(0, tile_cols))
    out_ref[...] = object_ref[inner] - OBJECT_STEP * gradient_ref[inner]
    first, last = edge_blocks(lax.axis_index("slow"), columns, slice(rim, rim + tile_rows), width)
    for part in range(2):
        out_ref[part, :, :width] -= OBJECT_STEP * first[part]
        out_ref[part, :, tile_cols - width :] -= OBJECT_STEP * last[part]
    below, above = both_sides(lax.rem(lax.axis_index("fast"), 2), rows_even_ref, rows_odd_ref)
    out_ref[:, :rim] -= OBJECT_STEP * above
    out_ref[:, tile_rows - rim :] -= OBJECT_STEP * below


def probe_kernel(sizes, total, probe_ref, descan_ref, quarters, probe_out_ref, descan_out_ref):
    tile_rows, tile_cols, width, modes, count, n_fast, n_slow = sizes
    core, slow = lax.rem(lax.axis_index("fast"), 2), lax.rem(lax.axis_index("slow"), 2)
    sums = of_quarters(quarters, core, slow, modes * width)
    real, imag = updated_probe(probe_ref, sums, total, width, modes)
    probe_out_ref[0] = real.reshape(modes, width, width)
    probe_out_ref[1] = imag.reshape(modes, width, width)
    at = modes * width // 2
    rows = descan_ref[...] - DESCAN_STEP / total * quarters[0][at : at + EXTRA]
    lane = lane_of((1, width))
    for k in range(2):
        values = [rows[3 * k + n : 3 * k + n + 1] for n in range(3)]
        row = jnp.where(lane == 0, values[0], jnp.where(lane == 1, values[1], values[2]))
        descan_out_ref[k : k + 1, :] = row[:, :3]


def call(kernel, outs, scratch, *operands, smem=0, hbm=False, semaphores=(), aliases=None, work=0):
    return pl.pallas_call(
        kernel,
        out_shape=[out if isinstance(out, jax.ShapeDtypeStruct) else jax.ShapeDtypeStruct(out, F32) for out in outs],
        in_specs=[SMEM] * smem + [HBM if hbm else VMEM] * (len(operands) - smem),
        out_specs=[VMEM] * len(outs),
        scratch_shapes=[pltpu.VMEM(shape, F32) for shape in scratch]
        + [pltpu.SemaphoreType.DMA(shape) for shape in semaphores],
        input_output_aliases=aliases or {},
        compiler_params=pltpu.CompilerParams(vmem_limit_bytes=LIMIT),
        cost_estimate=pl.CostEstimate(flops=work, bytes_accessed=work // 100, transcendentals=0) if work else None,
    )(*operands)


def on_device(object_field, probe_modes, descan, scan_positions, amplitudes):
    width = amplitudes.shape[-1]
    rim = width // 2
    modes = probe_modes.shape[1]
    count = scan_positions.shape[1]
    tile_rows, tile_cols = object_field.shape[1:]
    n_fast, n_slow = lax.axis_size("fast"), lax.axis_size("slow")
    total = count * n_fast * n_slow
    sizes = (tile_rows, tile_cols, width, modes, count, n_fast, n_slow)
    fast, slow = lax.axis_index("fast"), lax.axis_index("slow")
    starts = scan_positions.transpose(0, 2, 1)
    tables = transform_tables(width)
    ext_rows, ext_cols = tile_rows + width, tile_cols + width
    half_rows = modes * width
    swaps = 1 if n_slow == 2 else 2

    def partner(place, odd, length):
        other = place ^ 1 if not odd else ((place + 1) ^ 1) - 1
        return other if 0 <= other < length else None

    def exchanged(value, fast_swap=None, slow_swap=None):
        pairs = []
        for f in range(n_fast):
            for s in range(n_slow):
                to_fast = f if fast_swap is None else partner(f, fast_swap, n_fast)
                to_slow = s if slow_swap is None else partner(s, slow_swap, n_slow)
                if to_fast is not None and to_slow is not None:
                    pairs.append((f * n_slow + s, to_fast * n_slow + to_slow))
        return lax.ppermute(value, AXES, pairs)

    def swapped(value, axis, bit):
        return lax.ppermute(value, axis, [(i, i ^ bit) for i in range(lax.axis_size(axis))])

    assert n_fast >= 4 and n_slow >= 2 and not n_fast % 2 and not n_slow % 2
    regular = not (n_fast & (n_fast - 1) or n_slow & (n_slow - 1))
    fast_bits = [1 << k for k in range(1, n_fast.bit_length() - 1)]
    slow_bits = [1 << k for k in range(n_slow.bit_length() - 1)]

    def sum_begun(keep, send):
        mine = keep + swapped(send, "fast", 1)
        if regular:
            for bit in fast_bits[:-1]:
                mine = mine + swapped(mine, "fast", bit)
        return mine

    def fast_ended(mine):
        return mine + swapped(mine, "fast", fast_bits[-1]) if regular else mine

    def sum_ended(mine):
        if regular:
            for bit in slow_bits:
                mine = mine + swapped(mine, "slow", bit)
        else:
            core = lax.rem(fast, 2)
            every = lax.psum(jnp.where(jnp.arange(2)[:, None, None] == core, mine, 0.0), AXES) * 0.5
            mine = lax.dynamic_index_in_dim(every, core, keepdims=False)
        return mine, swapped(mine[:half_rows], "fast", 1)

    def pairwise(refs):
        return refs if swaps == 2 else (refs[0], None)

    extended, rows_even, rows_odd, *packed = call(
        functools.partial(pack_kernel, sizes),
        [(2, ext_rows, ext_cols)] + [(2, rim, tile_cols)] * 2
        + [(tile_rows, width), (rim, width), (rim, width)] * swaps, [],
        object_field, work=WORK,
    )
    halos = []
    rows_odd = exchanged(rows_odd, 1)
    for k in range(swaps):
        corner_odd = exchanged(packed[3 * k + 2], 1, k)
        middle = exchanged(packed[3 * k], None, k)
        halos += [middle, exchanged(packed[3 * k + 1], 0, k), corner_odd]
    rows_even = exchanged(rows_even, 0)
    def first(starts_ref, descan_ref, extended_ref, probe_ref, measured_ref, tables_ref, *rest):
        halo_refs = [rest[2 + 3 * k : 5 + 3 * k] for k in range(swaps)]
        extended_out_ref, gradient_ref, *rest_out = rest[2 + 3 * swaps :]
        first_kernel(sizes, starts_ref, descan_ref, extended_ref, probe_ref, measured_ref, tables_ref,
                     *rest[:2], halo_refs, extended_out_ref, gradient_ref, rest_out[:swaps], *rest_out[swaps:])

    scratch = [(count * modes * width, 2 * width), (2 * width, count * modes * width)]
    sums = [(half_rows + EXTRA, width)] * 2
    extended, gradient, *strips, keep, send = call(
        first,
        [(2, ext_rows, ext_cols)] * 2 + [(2, ext_rows, width)] * swaps + sums,
        scratch,
        starts, descan, extended, probe_modes, amplitudes, tables, rows_even, rows_odd, *halos,
        smem=1, aliases={2: 0},
    )
    columns = [exchanged(strip, None, k) for k, strip in enumerate(strips)]
    mine = sum_begun(keep, send)

    def rows(odd, gradient_ref, *rest):
        rows_kernel(sizes, odd, gradient_ref, pairwise(rest[:swaps]), *rest[swaps:])

    def rows_for(odd, token):
        return call(functools.partial(rows, odd), [rows_shape(sizes)], [], gradient, *columns, token)[0]

    rows_odd = exchanged(rows_for(True, mine), 1)
    rows_even = exchanged(rows_for(False, mine), 0)
    mine = fast_ended(mine)
    mine, other = sum_ended(mine)

    def update(extended_ref, gradient_ref, *rest):
        update_kernel(sizes, extended_ref, gradient_ref, pairwise(rest[:swaps]), *rest[swaps:])

    (extended,) = call(
        update, [(2, ext_rows, ext_cols)], [], extended, gradient, *columns, rows_even, rows_odd, aliases={0: 0},
    )

    def second(starts_ref, descan_ref, object_ref, probe_ref, measured_ref, tables_ref, mine_ref, other_ref, *rest):
        gradient_ref, *rest_out = rest
        second_kernel(sizes, total, starts_ref, descan_ref, object_ref, probe_ref, measured_ref, tables_ref,
                      mine_ref, other_ref, gradient_ref, rest_out[:swaps], *rest_out[swaps:])

    part = (half_rows // 2 + EXTRA, width)
    gradient, *strips, mine, beside, send, probes, descan_rows = call(
        second,
        [(2, ext_rows, ext_cols)] + [(ext_rows, width)] * swaps + [part, part, (2, *part)]
        + [probe_modes.shape, (EXTRA, width)],
        scratch,
        starts, descan, extended, probe_modes, amplitudes, tables, mine, other,
        smem=1,
    )
    columns = [exchanged(strip, None, k) for k, strip in enumerate(strips)]
    core_part = swapped(send, "fast", 1)
    mine = mine + core_part[0] + swapped(beside + core_part[1], "slow", 1)
    steps = [("fast", bit) for bit in fast_bits] + [("slow", bit) for bit in slow_bits[1:]]

    def last_rows(odd, gradient_ref, *rest):
        last_rows_kernel(sizes, odd, gradient_ref, pairwise(rest[:swaps]), *rest[swaps:])

    arrived = swapped(mine, *steps[0]) if regular else jnp.zeros_like(mine)
    mine, rows_odd = call(
        functools.partial(last_rows, True), [part, (2, rim, tile_cols)], [], gradient, *columns, mine, arrived,
    )
    rows_odd = exchanged(rows_odd, 1)
    if regular:
        for step in steps[1:]:
            mine = mine + swapped(mine, *step)
    else:
        place = 2 * lax.rem(fast, 2) + lax.rem(slow, 2)
        every = lax.psum(jnp.where(jnp.arange(4)[:, None, None] == place, mine, 0.0), AXES)
        mine = lax.dynamic_index_in_dim(every, place, keepdims=False)
    (rows_even,) = call(
        functools.partial(last_rows, False), [(2, rim, tile_cols)], [], gradient, *columns, mine,
    )
    rows_even = exchanged(rows_even, 0)
    own = mine[: half_rows // 2]
    beside = swapped(own, "slow", 1)
    (both,) = call(join_kernel, [(half_rows, width)], [], own, beside, rows_even, rows_odd)
    other = swapped(both, "fast", 1)

    def objects_of(object_ref, gradient_ref, *rest):
        object_kernel(sizes, object_ref, gradient_ref, pairwise(rest[:swaps]), *rest[swaps:])

    (objects,) = call(
        objects_of, [(2, tile_rows, tile_cols)], [], extended, gradient, *columns, rows_even, rows_odd,
    )

    def probe_of(probe_ref, descan_ref, q0, q1, q2, *outs):
        probe_kernel(sizes, total, probe_ref, descan_ref, (q0, q1, q2), *outs)

    probes, descan_out = call(
        probe_of, [probe_modes.shape, descan.shape], [],
        probes, descan_rows, mine, beside, other,
    )
    return objects, probes, descan_out


def solution(mesh):
    placed = (P(None, "fast", "slow"), P(), P(), P(None, "fast", "slow"), P("fast", "slow", None))
    return jax.shard_map(
        on_device,
        mesh=mesh,
        in_specs=placed,
        out_specs=(P(None, "fast", "slow"), P(), P()),
        check_vma=False,
    )
```
